128 devices in a mesh: blk: 32 (over z_lo, x, y), tp: 4 (over z_hi, core).
Axes of the slice: x: 4, y: 4, z: 4 (z_hi: 2, z_lo: 2; z = z_hi * 2 + z_lo), core: 2. Of those that a mesh axis runs over, the one named last changes fastest.
Arguments:
- tokens: bfloat16 [8192, 1536], P('blk'), may hold values from -6 to 6
- norm_gain: float32 [1536], replicated, may hold values from 0.5 to 1.5
- query_weight: bfloat16 [1536, 1536], P(None, 'tp'), may hold values from -0.21875 to 0.21875
- key_matrix: bfloat16 [1536, 768], P(None, 'tp'), may hold values from -0.15625 to 0.15625
- value_matrix: bfloat16 [1536, 768], P(None, 'tp'), may hold values from -0.15625 to 0.15625
- out_weight: bfloat16 [1536, 1536], P('tp'), may hold values from -1.5 to 1.5
- ffn_gain: float32 [1536], replicated, may hold values from 0.5 to 1.5
- gate_weight: bfloat16 [1536, 4096], P(None, 'tp'), may hold values from -0.15625 to 0.15625
- up_weight: bfloat16 [1536, 4096], P(None, 'tp'), may hold values from -0.15625 to 0.15625
- down_weight: bfloat16 [4096, 1536], P('tp'), may hold values from -0.09375 to 0.09375
- cotangent: bfloat16 [8192, 1536], P('blk'), may hold values from -6 to 6
- lengths: int32 [5], replicated, may hold values from 1 to 7936, as said below
Outputs:
- result: bfloat16 [8192, 1536], P('blk')
- tokens_grad: bfloat16 [8192, 1536], P('blk')
- norm_gain_grad: float32 [1536], P('blk')
- query_weight_grad: float32 [1536, 1536], P('blk', 'tp')
- key_weight_grad: float32 [1536, 768], P('blk', 'tp')
- value_weight_grad: float32 [1536, 768], P('blk', 'tp')
- out_weight_grad: float32 [1536, 1536], P('tp', 'blk')
- ffn_gain_grad: float32 [1536], P('blk')
- gate_weight_grad: float32 [1536, 4096], P('blk', 'tp')
- up_weight_grad: float32 [1536, 4096], P('blk', 'tp')
- down_weight_grad: float32 [4096, 1536], P('tp', 'blk')
The draws below stay inside these ranges and needn't reach their ends.
Inputs may be any that keep to these rules, and one draw needn't show every extreme that they name: The lengths sum to 8192; one of the second, third or fourth documents, which one drawn from the seed, has 7936 tokens, and the other four share the remaining 256 tokens.
All inputs are finite; a program needn't handle non-finite values.
Results may differ from the reference program's by a relative error of at most 0.033.
Values may be sent and summed in bfloat16 or wider, within the bound.
A program may use at most 128 MiB of HBM per device.

```python
from functools import partial
import jax
import jax.numpy as jnp
from jax import lax

MODEL_WIDTH = 1536
QUERY_HEADS = 16
KEY_VALUE_HEADS = 8
HEAD_SIZE = 96
FF = 4096
TOK_BLK = 256
PACKED_TOKENS = 8192


def draw_lengths(key, part):
    key = jax.random.fold_in(key, 11)
    first_key, second_key = jax.random.split(key, 2)
    shuffled = jax.random.permutation(first_key, TOK_BLK - 1).astype(jnp.int32) + 1
    cuts = jnp.sort(shuffled[:3])
    bounds = jnp.concatenate([jnp.zeros((1,), jnp.int32), cuts, jnp.full((1,), TOK_BLK, jnp.int32)])
    short = (bounds[1:] - bounds[:-1]).astype(jnp.int32)
    where_long = jax.random.randint(second_key, (), 1, 4).astype(jnp.int32)
    places = jnp.arange(5, dtype=jnp.int32)
    source_index = jnp.clip(jnp.where(places < where_long, places, places - 1), 0, 3)
    picked = jnp.take(short, source_index)
    longest = jnp.full((5,), PACKED_TOKENS - TOK_BLK, jnp.int32)
    return jnp.where(places == where_long, longest, picked).astype(jnp.int32)


def raised(values, rng, source, target, shards_of, factor):
    owner, partner = [(jnp.arange(values.shape[dim]) // (values.shape[dim] // shards_of)).reshape([-1 if axis == dim else 1 for axis in range(values.ndim)]) for dim in (source, target)]
    chosen = jax.random.permutation(rng, shards_of)[partner]
    strong = (owner == chosen) | (owner == (partner + shards_of // 2) % shards_of)
    return jnp.where(strong, factor * values, values)


def block_levels(own_key, extent, cuts, least, high):
    level = 1.0
    for axis_at, blocks in cuts:
        heights = jax.random.uniform(jax.random.fold_in(jax.random.fold_in(own_key, 6), axis_at), (blocks,), jnp.float32, least / len(cuts), high / len(cuts))
        level = level * jnp.repeat(jnp.exp(heights), extent[axis_at] // blocks).reshape((-1,) + (1,) * (len(extent) - 1 - axis_at))
    return level


def gaussian(stream_key, dims, scale, most, shards=(), kind=jnp.bfloat16):
    level = block_levels(stream_key, dims, shards, -0.22, 0.18) if shards else 1.0
    result = jax.random.normal(stream_key, dims, jnp.float32) * scale * level
    return jnp.minimum(jnp.maximum(result, -most), most).astype(kind)


def gaussian_with(key, shape, width, bound, cuts, heavy, kind=jnp.bfloat16):
    array = width * jax.random.normal(key, shape, jnp.float32)
    if cuts:
        array = array * block_levels(key, shape, cuts, -0.22, 0.18)
    return jnp.clip(raised(array, jax.random.fold_in(key, 3), *heavy), -bound, bound).astype(kind)


def setup_inputs(seed: int = 0) -> dict:
    seeds = jax.random.split(jax.random.key(seed), 13)
    tokens = gaussian(seeds[0], (PACKED_TOKENS, MODEL_WIDTH), 1.0, 6.0, ((0, 32),))
    norm_gain = jnp.clip(1.0 + 0.1 * jax.random.normal(seeds[1], (MODEL_WIDTH,), jnp.float32), 0.5, 1.5)
    query_weight = gaussian(seeds[2], (MODEL_WIDTH, QUERY_HEADS * HEAD_SIZE), (MODEL_WIDTH // 2) ** -0.5, 0.21875, ((1, 4),))
    key_matrix = gaussian(seeds[3], (MODEL_WIDTH, KEY_VALUE_HEADS * HEAD_SIZE), MODEL_WIDTH ** -0.5, 0.15625, ((1, 4),))
    value_matrix = gaussian(seeds[4], (MODEL_WIDTH, KEY_VALUE_HEADS * HEAD_SIZE), MODEL_WIDTH ** -0.5, 0.15625, ((1, 4),))
    out_weight = gaussian(seeds[5], (QUERY_HEADS * HEAD_SIZE, MODEL_WIDTH), 16 ** -0.5, 1.5, ((0, 4),))
    ffn_gain = jnp.clip(1.0 + 0.1 * jax.random.normal(seeds[6], (MODEL_WIDTH,), jnp.float32), 0.5, 1.5)
    gate_weight = gaussian(seeds[7], (MODEL_WIDTH, FF), MODEL_WIDTH ** -0.5, 0.15625, ((1, 4),))
    up_weight = gaussian(seeds[8], (MODEL_WIDTH, FF), MODEL_WIDTH ** -0.5, 0.15625, ((1, 4),))
    down_weight = gaussian(seeds[9], (FF, MODEL_WIDTH), FF ** -0.5, 0.09375, ((0, 4),))
    cotangent = gaussian_with(seeds[10], (PACKED_TOKENS, MODEL_WIDTH), 1.0, 6.0, ((0, 32),), (0, 1, 32, 2.75))
    lengths = draw_lengths(jax.random.fold_in(seeds[12], 71), 0)
    return dict(tokens=tokens, norm_gain=norm_gain, query_weight=query_weight, key_matrix=key_matrix, value_matrix=value_matrix, out_weight=out_weight, ffn_gain=ffn_gain, gate_weight=gate_weight, up_weight=up_weight, down_weight=down_weight, cotangent=cotangent, lengths=lengths)


eps = 1e-05
theta = 100000.0

@jax.custom_vjp
def low(v):
    return lax.optimization_barrier(v.astype(jnp.bfloat16)).astype(jnp.float32)

@jax.custom_vjp
def low_back(v):
    return v

def low_keep(v):
    return (low(v), None)

def low_pass(kept, grad):
    return (grad,)

def back_keep(v):
    return (v, None)

def back_low(kept, grad):
    return (low(grad),)
low.defvjp(low_keep, low_pass)
low_back.defvjp(back_keep, back_low)

def dense_matmul(left, right):
    return jnp.dot(left, right, precision=lax.Precision.HIGHEST, preferred_element_type=jnp.float32)

def rms(field, gain):
    inverse = lax.rsqrt(lax.optimization_barrier(jnp.mean(field * field, -1, keepdims=True)) + eps)
    return field * inverse * gain

def apply_rotary(field, token_position):
    half = field.shape[-1] // 2
    freq = theta ** (-2.0 * jnp.arange(half).astype(field.dtype) / field.shape[-1])
    angle = token_position.astype(field.dtype)[:, None] * freq[None, :]
    cosine = jnp.cos(angle)[:, None, :]
    sine = jnp.sin(angle)[:, None, :]
    first = field[..., :half]
    second = field[..., half:]
    return jnp.concatenate([first * cosine - second * sine, second * cosine + first * sine], -1)

def attend(query_rows, key_rows, value_rows, query_segment, key_segment, offset):
    token_rows = query_rows.shape[0]
    query_groups = QUERY_HEADS // KEY_VALUE_HEADS
    query_rows = query_rows.reshape(token_rows, KEY_VALUE_HEADS, query_groups, HEAD_SIZE)
    scores = jnp.einsum('qkgd,skd->kgqs', query_rows, key_rows, precision=lax.Precision.HIGHEST) * HEAD_SIZE ** (-0.5)
    scores = low_back(scores)
    key_index = jnp.arange(key_rows.shape[0], dtype=jnp.int32)
    query_index = offset + jnp.arange(token_rows, dtype=jnp.int32)
    allowed = (query_segment[:, None] == key_segment[None, :]) & (key_index[None, :] <= query_index[:, None])
    scores = jnp.where(allowed[None, None], scores, -1e+30)
    peak = lax.optimization_barrier(jnp.max(scores, -1, keepdims=True))
    weight = jnp.exp(scores - peak)
    prob = weight / lax.optimization_barrier(jnp.sum(weight, -1, keepdims=True))
    mixed = jnp.einsum('kgqs,skd->qkgd', low(prob), value_rows, precision=lax.Precision.HIGHEST)
    return mixed.reshape(token_rows, QUERY_HEADS * HEAD_SIZE)

def layer(tokens, norm_gain, query_weight, key_matrix, value_matrix, out_weight, ffn_gain, gate_weight, up_weight, down_weight, segment, token_position):
    normalized_input = low(rms(tokens, norm_gain))
    query_rows = low(apply_rotary(low_back(dense_matmul(normalized_input, query_weight)).reshape(PACKED_TOKENS, QUERY_HEADS, HEAD_SIZE), token_position))
    key_rows = low(apply_rotary(low_back(dense_matmul(normalized_input, key_matrix)).reshape(PACKED_TOKENS, KEY_VALUE_HEADS, HEAD_SIZE), token_position))
    value_rows = low(low_back(dense_matmul(normalized_input, value_matrix))).reshape(PACKED_TOKENS, KEY_VALUE_HEADS, HEAD_SIZE)
    block = min(512, PACKED_TOKENS)
    pieces = []
    for number in range(PACKED_TOKENS // block):
        start = number * block
        stop = start + block
        pieces.append(jax.checkpoint(partial(attend, offset=start))(query_rows[start:stop], key_rows[:stop], value_rows[:stop], segment[start:stop], segment[:stop]))
    attended = low(low_back(jnp.concatenate(pieces, 0)))
    mixed = tokens + low_back(dense_matmul(attended, out_weight))
    normed_two = low(rms(mixed, ffn_gain))
    gate = low_back(dense_matmul(normed_two, gate_weight))
    upper = low_back(dense_matmul(normed_two, up_weight))
    hidden = low(jax.nn.silu(gate) * upper)
    return mixed + dense_matmul(hidden, down_weight)

def reference(tokens, norm_gain, query_weight, key_matrix, value_matrix, out_weight, ffn_gain, gate_weight, up_weight, down_weight, cotangent, lengths):
    ends = jnp.cumsum(lengths).astype(jnp.int32)
    index = jnp.arange(PACKED_TOKENS, dtype=jnp.int32)
    after = index[:, None] >= ends[None, :]
    segment = lax.optimization_barrier(jnp.sum(after.astype(jnp.int32), 1)).astype(jnp.int32)
    token_position = (index - lax.optimization_barrier(jnp.sum(jnp.where(after, lengths[None, :], 0), 1))).astype(jnp.int32)
    floats = tuple((item.astype(jnp.float32) for item in (tokens, norm_gain, query_weight, key_matrix, value_matrix, out_weight, ffn_gain, gate_weight, up_weight, down_weight)))
    output, pullback = jax.vjp(partial(layer, segment=segment, token_position=token_position), *floats)
    grads = pullback(cotangent.astype(jnp.float32))
    return (output.astype(jnp.bfloat16), grads[0].astype(jnp.bfloat16), grads[1], grads[2], grads[3], grads[4], grads[5], grads[6], grads[7], grads[8], grads[9])
```

```python
import jax
import jax.numpy as jnp
import numpy as np
from jax import lax
from jax.experimental import pallas as pl
from jax.experimental.pallas import tpu as pltpu
from jax.sharding import Mesh
from jax.sharding import PartitionSpec as P

AXES = ("zl", "x", "y", "zh", "c")
BLK = ("zl", "x", "y")
TP = ("zh", "c")
HEAD = 96
HALF = HEAD // 2
ROWS = 256
WIDTH = 1536
HEADS_LOCAL = 384
PAIRS_LOCAL = 192
FFL = 1024
EPS = 1e-05
THETA = 100000.0
SCALE = HEAD**-0.5
LOG2E = float(np.log2(np.e))
LN2 = float(np.log(2.0))
BIG = 1e30
SEG = 16
MESH = pl.DeviceIdType.MESH
F32 = jnp.float32
BF16 = jnp.bfloat16
VMEM_LIMIT = 60 * 2**20


def dot(a, b, ca=1, cb=0):
    return lax.dot_general(a, b, (((ca,), (cb,)), ((), ())), preferred_element_type=F32)


class Place:
    def __init__(self):
        self.zl, self.x, self.y, self.zh, self.c = (lax.axis_index(a) for a in AXES)

    def at(self, **changes):
        own = dict(zl=self.zl, x=self.x, y=self.y, zh=self.zh, c=self.c)
        own.update(changes)
        return tuple(own[a] for a in AXES)

    def along(self, axis, step):
        return self.at(**{axis: lax.rem(getattr(self, axis) + (step + 4), 4)})

    @property
    def pair(self):
        return dict(zl=1 - self.zl, x=3 - self.x, y=3 - self.y)

    def low_block(self, x, y):
        p = x * 4 + y
        return jnp.where(self.zl == 0, p, 15 - p)


def greet(peers):
    barrier = pltpu.get_barrier_semaphore()
    for peer in peers:
        pl.semaphore_signal(barrier, inc=1, device_id=peer, device_id_type=MESH)
    pl.semaphore_wait(barrier, len(peers))


def remote(src, dst, send, recv, device):
    return pltpu.make_async_remote_copy(
        src_ref=src, dst_ref=dst, send_sem=send, recv_sem=recv, device_id=device, device_id_type=MESH
    )


def seg_rows(ends, base):
    token = base + lax.broadcasted_iota(jnp.int32, (SEG, ROWS), 1)
    row = lax.broadcasted_iota(jnp.int32, (SEG, ROWS), 0)
    inside = jnp.zeros((SEG, ROWS), F32)
    start = 0
    for d in range(5):
        hit = (row == d) & (token >= start) & (token < ends[d])
        inside = jnp.where(hit, 1.0, inside)
        start = ends[d]
    return inside, row


def key_segments(ends, base):
    return seg_rows(ends, base)[0].astype(BF16)


def query_segments(ends, base):
    inside, row = seg_rows(ends, base)
    return jnp.where(row < 5, (inside - 1.0) * BIG, 0.0).astype(BF16)


def ends_of(lengths_ref):
    ends, total = [], 0
    for d in range(5):
        total = total + lengths_ref[d]
        ends.append(total)
    return ends


def rotation(ends, lengths_ref, base, freq):
    token = base + lax.broadcasted_iota(jnp.int32, (1, ROWS), 1)
    begin = jnp.zeros((1, ROWS), jnp.int32)
    for d in range(5):
        begin = begin + jnp.where(token >= ends[d], lengths_ref[d], 0)
    angle = (token - begin).astype(F32) * freq
    return jnp.cos(angle), jnp.sin(angle)


class RingSum:
    def __init__(self, place, axis, half, bufs, out, send, recv, add2, add3):
        self.half, self.bufs, self.out, self.add2, self.add3 = half, bufs, out, add2, add3
        me = getattr(place, axis)
        self.me = me
        self.r, self.l, self.o = (lax.rem(me + k, 4) for k in (1, 3, 2))
        self.right, self.left = place.along(axis, 1), place.along(axis, -1)
        self.send, self.recv = send, recv

    def cp(self, k):
        src = (
            lambda: self.half(self.o, 0),
            lambda: self.half(self.o, 1),
            lambda: self.half(self.r, 1),
            lambda: self.half(self.l, 0),
            lambda: self.bufs(0),
            lambda: self.bufs(1),
        )[k]()
        return remote(
            src, self.bufs(k), self.send(k), self.recv(k), (self.right, self.left)[k % 2]
        )

    def start(self):
        for k in range(4):
            self.cp(k).start()

    def mid(self):
        self.cp(0).wait_recv()
        self.cp(0).wait_send()
        self.add2(self.bufs(0), self.half(self.r, 0))
        self.cp(4).start()
        self.cp(1).wait_recv()
        self.cp(1).wait_send()
        self.add2(self.bufs(1), self.half(self.l, 1))
        self.cp(5).start()

    def fin(self):
        self.cp(4).wait_recv()
        self.cp(3).wait_recv()
        self.add3(self.out(0), self.half(self.me, 0), self.bufs(4), self.bufs(3))
        self.cp(5).wait_recv()
        self.cp(2).wait_recv()
        self.add3(self.out(1), self.half(self.me, 1), self.bufs(5), self.bufs(2))

    def end(self):
        for k in range(2, 6):
            self.cp(k).wait_send()


def add2_lead(dst, src):
    for i in range(dst.shape[0]):
        dst[i] = dst[i] + src[i]


def add3_lead(out, a, b, d):
    for i in range(out.shape[0]):
        out[i] = (a[i].astype(F32) + b[i].astype(F32) + d[i].astype(F32)).astype(BF16)


def add2_flat(dst, src):
    dst[...] = dst[...] + src[...]


def add3_flat(out, a, b, d):
    out[...] = (a[...].astype(F32) + b[...].astype(F32) + d[...].astype(F32)).astype(BF16)


class GradSum:
    def __init__(self, place, first, lo, w, g, bufs, sems, n):
        b1, r1, b2, r2, zb = bufs
        send, recv = sems
        self.place, self.cols, self.r2, self.zb, self.n = place, pl.ds(lo, w), r2, zb, n
        self.send, self.recv = send, recv
        cols = self.cols
        second = "y" if first == "x" else "x"
        if first == "x":
            half1 = lambda d, h: g.at[h, d, :, :, cols]
        else:
            half1 = lambda d, h: g.at[h, :, d, :, cols]
        self.one = RingSum(
            place, first, half1, lambda k: b1.at[k, :, :, cols], lambda h: r1.at[h, :, :, cols],
            lambda k: send.at[n, k], lambda k: recv.at[n, k], add2_lead, add3_lead,
        )
        self.two = RingSum(
            place, second, lambda d, h: r1.at[h, d, :, cols], lambda k: b2.at[k, :, cols],
            lambda h: r2.at[h, :, cols], lambda k: send.at[n, 6 + k], lambda k: recv.at[n, 6 + k],
            add2_flat, add3_flat,
        )

    def zcp(self):
        other = 1 - self.place.zl
        return remote(
            self.r2.at[other, :, self.cols], self.zb.at[:, self.cols], self.send.at[self.n, 12],
            self.recv.at[self.n, 12], self.place.at(zl=other),
        )

    def total(self):
        self.zcp().wait_recv()
        own = self.r2[self.place.zl, :, self.cols].astype(F32)
        return own + self.zb[:, self.cols].astype(F32)

    def end(self):
        self.one.end()
        self.two.end()
        self.zcp().wait_send()


def grad_scratch(width, pieces):
    return [
        pltpu.VMEM((6, 4, 48, width), BF16),
        pltpu.VMEM((2, 4, 48, width), BF16),
        pltpu.VMEM((6, 48, width), BF16),
        pltpu.VMEM((2, 48, width), BF16),
        pltpu.VMEM((48, width), BF16),
        pltpu.SemaphoreType.DMA((pieces, 13)),
        pltpu.SemaphoreType.DMA((pieces, 13)),
    ]


AR_PIECES = 4
AR_ROWS = ROWS // 2 // AR_PIECES


class TpSum:
    def __init__(self, place, part, total, buf, sems):
        self.place, self.part, self.total, self.buf = place, part, total, buf
        self.send, self.recv = sems
        self.core = place.at(c=1 - place.c)
        self.far = place.at(zh=1 - place.zh)

    def a(self, k):
        return remote(
            self.part.at[1 - self.place.c, k], self.buf.at[0, k], self.send.at[0, k], self.recv.at[0, k], self.core
        )

    def b(self, k):
        return remote(self.buf.at[0, k], self.buf.at[1, k], self.send.at[1, k], self.recv.at[1, k], self.far)

    def d(self, k):
        rows = self.total.at[self.place.c, k]
        return remote(rows, rows, self.send.at[2, k], self.recv.at[2, k], self.core)

    def start(self):
        for k in range(AR_PIECES):
            self.a(k).start()

    def mid(self):
        for k in range(AR_PIECES):
            self.a(k).wait_recv()
            self.buf[0, k] = self.buf[0, k] + self.part[self.place.c, k]
            self.b(k).start()

    def fin(self):
        for k in range(AR_PIECES):
            self.b(k).wait_recv()
            self.total[self.place.c, k] = self.buf[0, k] + self.buf[1, k]
            self.d(k).start()

    def landed(self):
        for k in range(AR_PIECES):
            rows = self.total.at[1 - self.place.c, k]
            remote(rows, rows, self.send.at[2, k], self.recv.at[2, k], self.core).wait_recv()

    def end(self):
        for k in range(AR_PIECES):
            self.a(k).wait_send()
            self.b(k).wait_send()
            self.d(k).wait_send()


def tp_scratch():
    return [
        pltpu.VMEM((2, AR_PIECES, AR_ROWS, WIDTH), BF16),
        pltpu.SemaphoreType.DMA((3, AR_PIECES)),
        pltpu.SemaphoreType.DMA((3, AR_PIECES)),
    ]


def ar_view(value):
    return value.reshape(2, AR_PIECES, AR_ROWS, WIDTH)


def ar_load(ref):
    return ref[...].reshape(ROWS, WIDTH)


def front_kernel(
    lengths, freq, tokens, gain, wq, wk, wv, wo,
    normed_out, qkv, kvall, att, o_out, lse_out, wo_full,
    grp, qaug, acc, peak, total, mine,
    pair_sem, ag_send, ag_recv, o_send, o_recv, w_send, w_recv, loc_sem,
):
    place = Place()
    zl, x, y, zh, c = place.zl, place.x, place.y, place.zh, place.c
    partner = place.at(**place.pair)
    far_partner = place.at(**place.pair, zh=1 - zh)
    far = place.at(zh=1 - zh)
    core = place.at(c=1 - c)
    xr, xl, yr, yl = place.along("x", 1), place.along("x", -1), place.along("y", 1), place.along("y", -1)
    greet([partner, far_partner, far, core, xr, xl, yr, yl])
    ends = ends_of(lengths)
    block = zl * 16 + x * 4 + y
    cosine, sine = rotation(ends, lengths, block * ROWS, freq[...])
    source = tokens[...].astype(F32)
    inverse = lax.rsqrt(jnp.mean(source * source, -1, keepdims=True) + EPS)
    normed = (source * inverse * gain[...]).astype(BF16)
    normed_out[...] = normed

    def turned(u, factor):
        a, b = u[:HALF], u[HALF:]
        if factor is None:
            return a * cosine - b * sine, b * cosine + a * sine
        return (a * cosine - b * sine) * factor, (b * cosine + a * sine) * factor

    qt = dot(normed, wq[...]).T
    kt = dot(normed, wk[...]).T
    vt = dot(normed, wv[...]).T
    for g in range(2):
        for h in range(2):
            a, b = turned(qt[(2 * g + h) * HEAD : (2 * g + h + 1) * HEAD], SCALE * LOG2E)
            grp[g, h * HEAD : h * HEAD + HALF] = a.astype(BF16)
            grp[g, h * HEAD + HALF : (h + 1) * HEAD] = b.astype(BF16)
        a, b = turned(kt[g * HEAD : (g + 1) * HEAD], None)
        grp[g, 2 * HEAD : 2 * HEAD + HALF] = a.astype(BF16)
        grp[g, 2 * HEAD + HALF : 3 * HEAD] = b.astype(BF16)
        grp[g, 3 * HEAD :] = vt[g * HEAD : (g + 1) * HEAD].astype(BF16)

    pair_cp = remote(grp.at[1 - zl], qkv.at[zl], pair_sem.at[0], pair_sem.at[1], partner)
    pair_cp.start()
    qkv[zl] = grp[zl]
    kvall[x, y, zl] = grp[zl, 2 * HEAD :]
    me_t = zh * 2 + c
    wo_local = pltpu.make_async_copy(wo, wo_full.at[me_t], loc_sem.at[0])
    wo_local.start()
    pair_cp.wait_recv()
    kvall[x, y, 1 - zl] = qkv[1 - zl, 2 * HEAD :]

    def gather(slot, first):
        swap = first == "y"
        me1, me2 = (y, x) if swap else (x, y)
        r1, l1, r2, l2 = (yr, yl, xr, xl) if swap else (xr, xl, yr, yl)

        def ref(i, j, part=None):
            i, j = lax.rem(i + 4, 4), lax.rem(j + 4, 4)
            v = kvall.at[j, i, slot] if swap else kvall.at[i, j, slot]
            return v if part is None else v.at[pl.ds(part * HEAD, HEAD)]

        def cp(n, view, dev):
            return remote(view, view, ag_send.at[slot, n], ag_recv.at[slot, n], dev)

        def stage(base, i, j, di, dj, r, l):
            own = (i, j)
            return dict(
                right=cp(base, ref(i, j), r),
                left=cp(base + 1, ref(i, j), l),
                from_left=cp(base, ref(i - di, j - dj), r),
                from_right=cp(base + 1, ref(i + di, j + dj), l),
                on_right=cp(base + 2, ref(i - di, j - dj, 0), r),
                on_left=cp(base + 3, ref(i + di, j + dj, 1), l),
                from_left2=cp(base + 2, ref(i + 2 * di, j + 2 * dj, 0), r),
                from_right2=cp(base + 3, ref(i + 2 * di, j + 2 * dj, 1), l),
            )

        s1 = stage(0, me1, me2, 1, 0, r1, l1)
        s2 = [stage(4 + 4 * k, me1 + k, me2, 0, 1, r2, l2) for k in range(4)]
        return s1, s2

    ga, gb = gather(0, "x"), gather(1, "y")
    both = (ga, gb)
    for s1, s2 in both:
        s1["right"].start()
        s1["left"].start()
    for s1, s2 in both:
        s2[0]["right"].start()
        s2[0]["left"].start()
    wo_cps = [
        remote(wo, wo_full.at[me_t], w_send.at[0], w_recv.at[0], far),
        remote(wo, wo_full.at[me_t], w_send.at[1], w_recv.at[1], core),
    ]
    for cp in wo_cps:
        cp.start()
    for s1, s2 in both:
        s1["from_left"].wait_recv()
        s1["on_right"].start()
        s1["from_right"].wait_recv()
        s1["on_left"].start()
    for k in (3, 1):
        for s1, s2 in both:
            s2[k]["right"].start()
            s2[k]["left"].start()
    for s1, s2 in both:
        s2[0]["from_left"].wait_recv()
        s2[0]["on_right"].start()
        s2[0]["from_right"].wait_recv()
        s2[0]["on_left"].start()
    for s1, s2 in both:
        s1["from_left2"].wait_recv()
        s1["from_right2"].wait_recv()
        s2[2]["right"].start()
        s2[2]["left"].start()
    for k in (3, 1, 2):
        for s1, s2 in both:
            s2[k]["from_left"].wait_recv()
            s2[k]["on_right"].start()
            s2[k]["from_right"].wait_recv()
            s2[k]["on_left"].start()
    for k in (0, 3, 1, 2):
        for s1, s2 in both:
            s2[k]["from_left2"].wait_recv()
            s2[k]["from_right2"].wait_recv()

    low = place.low_block(x, y)
    for s in range(2):
        base = jnp.where(s == 0, low, 31 - low) * ROWS
        segs = query_segments(ends, base)
        for h in range(2):
            qaug[s, :HEAD, h * ROWS : (h + 1) * ROWS] = qkv[s, h * HEAD : (h + 1) * HEAD]
            qaug[s, HEAD:, h * ROWS : (h + 1) * ROWS] = segs
    peak[...] = jnp.full(peak.shape, -BIG, F32)
    total[...] = jnp.zeros(total.shape, F32)
    acc[...] = jnp.zeros(acc.shape, F32)

    def unit(qs, kx, ky, ks, kbase, causal):
        kv = kvall[kx, ky, ks]
        ka = jnp.concatenate([kv[:HEAD], key_segments(ends, kbase)], 0)
        s = dot(ka, qaug[qs], 0, 0)
        if causal:
            key = lax.broadcasted_iota(jnp.int32, (ROWS, 2 * ROWS), 0)
            query = lax.broadcasted_iota(jnp.int32, (ROWS, 2 * ROWS), 1)
            s = jnp.where(key <= jnp.where(query >= ROWS, query - ROWS, query), s, -BIG)
        old = peak[qs]
        new = jnp.maximum(old, jnp.max(s, 0, keepdims=True))
        p = jnp.exp2(s - new)
        fade = jnp.exp2(old - new)
        peak[qs] = new
        total[qs] = total[qs] * fade + jnp.sum(p, 0, keepdims=True)
        acc[qs] = acc[qs] * fade + dot(kv[HEAD:], p.astype(BF16))

    unit(0, x, y, 0, low * ROWS, True)
    unit(1, x, y, 1, (31 - low) * ROWS, True)
    unit(1, x, y, 0, low * ROWS, False)

    def step(i, carry):
        kx, ky = lax.rem(x + i // 4, 4), lax.rem(y + i % 4, 4)
        there = place.low_block(kx, ky)
        unit(1, kx, ky, 0, there * ROWS, False)
        sel = jnp.where(there < low, 0, 1)
        unit(sel, kx, ky, sel, jnp.where(there < low, there, 31 - there) * ROWS, False)
        return carry

    lax.fori_loop(1, 16, step, 0)
    for s in range(2):
        out = acc[s] / total[s]
        lse_out[s] = peak[s] + jnp.log2(total[s])
        for h in range(2):
            part = out[:, h * ROWS : (h + 1) * ROWS]
            o_out[s, h * HEAD : (h + 1) * HEAD] = part
            mine[s, h * HEAD : (h + 1) * HEAD] = part.astype(BF16)

    group = me_t * 2 + zl
    att[group] = mine[zl]
    sends = [
        remote(mine.at[1 - zl], att.at[group], o_send.at[0], o_recv.at[0], partner),
        remote(mine.at[1 - zl], att.at[group], o_send.at[1], o_recv.at[1], far_partner),
        remote(mine.at[zl], att.at[group], o_send.at[2], o_recv.at[2], far),
    ]
    for cp in sends:
        cp.start()
    there_t = (1 - zh) * 2 + c
    order = [
        (None, group), (0, me_t * 2 + 1 - zl), (1, there_t * 2 + 1 - zl), (2, there_t * 2 + zl),
    ]
    relays = []
    for n, (sem, which) in enumerate(order):
        if sem is not None:
            remote(att.at[which], att.at[which], o_send.at[sem], o_recv.at[sem], far).wait_recv()
        cp = remote(att.at[which], att.at[which], o_send.at[3 + n], o_recv.at[3 + n], core)
        cp.start()
        relays.append(cp)
    wo_far = wo_full.at[there_t]
    remote(wo_far, wo_far, w_send.at[0], w_recv.at[0], far).wait_recv()
    wo_relay = remote(wo_far, wo_far, w_send.at[2], w_recv.at[2], core)
    wo_relay.start()
    mine_t, other_t = zh * 2 + (1 - c), (1 - zh) * 2 + (1 - c)
    for n, which in enumerate([mine_t * 2 + zl, mine_t * 2 + 1 - zl, other_t * 2 + 1 - zl, other_t * 2 + zl]):
        remote(att.at[which], att.at[which], o_send.at[3 + n], o_recv.at[3 + n], core).wait_recv()
    w1, w2 = wo_full.at[mine_t], wo_full.at[other_t]
    remote(w1, w1, w_send.at[1], w_recv.at[1], core).wait_recv()
    remote(w2, w2, w_send.at[2], w_recv.at[2], core).wait_recv()
    wo_local.wait()
    pair_cp.wait_send()
    for s1, s2 in both:
        for st in [s1, *s2]:
            for name in ("right", "left", "on_right", "on_left"):
                st[name].wait_send()
    for cp in [*wo_cps, wo_relay, *sends, *relays]:
        cp.wait_send()


def front(lengths, freq, tokens, gain, wq, wk, wv, wo):
    vm = pl.BlockSpec(memory_space=pltpu.VMEM)
    anywhere = pl.BlockSpec(memory_space=pl.ANY)
    dma = pltpu.SemaphoreType.DMA
    return pl.pallas_call(
        front_kernel,
        out_shape=(
            jax.ShapeDtypeStruct((ROWS, WIDTH), BF16),
            jax.ShapeDtypeStruct((2, 4 * HEAD, ROWS), BF16),
            jax.ShapeDtypeStruct((4, 4, 2, 2 * HEAD, ROWS), BF16),
            jax.ShapeDtypeStruct((8, 2 * HEAD, ROWS), BF16),
            jax.ShapeDtypeStruct((2, 2 * HEAD, ROWS), F32),
            jax.ShapeDtypeStruct((2, 1, 2 * ROWS), F32),
            jax.ShapeDtypeStruct((4, HEADS_LOCAL, WIDTH), BF16),
        ),
        in_specs=[pl.BlockSpec(memory_space=pltpu.SMEM), vm, vm, vm, vm, vm, vm, anywhere],
        out_specs=(vm, vm, vm, vm, vm, vm, anywhere),
        scratch_shapes=[
            pltpu.VMEM((2, 4 * HEAD, ROWS), BF16),
            pltpu.VMEM((2, HEAD + SEG, 2 * ROWS), BF16),
            pltpu.VMEM((2, HEAD, 2 * ROWS), F32),
            pltpu.VMEM((2, 1, 2 * ROWS), F32),
            pltpu.VMEM((2, 1, 2 * ROWS), F32),
            pltpu.VMEM((2, 2 * HEAD, ROWS), BF16),
            dma((2,)),
            dma((2, 20)),
            dma((2, 20)),
            dma((7,)),
            dma((7,)),
            dma((3,)),
            dma((3,)),
            dma((1,)),
        ],
        compiler_params=pltpu.CompilerParams(
            collective_id=0, has_side_effects=True, vmem_limit_bytes=VMEM_LIMIT
        ),
        name="front",
    )(lengths, freq, tokens, gain, wq, wk, wv, wo)


W_FFN = 3 * FFL
W_MID = W_FFN + HEADS_LOCAL


def norm_back(source, inverse, gain, grad):
    scaled = grad * gain
    gain_grad = jnp.sum(grad * source * inverse, 0, keepdims=True)
    mean = jnp.mean(scaled * source, -1, keepdims=True)
    return inverse * scaled - source * (inverse * inverse * inverse) * mean, gain_grad


def middle_kernel(
    tokens, cot, att, wo, gain, wg, wu, wd,
    result, grads, mixed_grad_out, dout, gain_grad_out,
    gate_s, upper_s, left, part3, part2, tot3, tot2, buf3, s3, r3, buf2, s2, r2, dgrp, pair_sem,
):
    place = Place()
    partner = place.at(**place.pair)
    greet([partner, place.at(zh=1 - place.zh), place.at(c=1 - place.c)])
    zl = place.zl
    mixed = tokens[...].astype(F32)
    mixed = mixed + dot(att[...].reshape(WIDTH, ROWS), wo[...].reshape(WIDTH, WIDTH), 0, 0)
    inverse = lax.rsqrt(jnp.mean(mixed * mixed, -1, keepdims=True) + EPS)
    normed = (mixed * inverse * gain[...]).astype(BF16)
    gate_s[...] = dot(normed, wg[...])
    upper_s[...] = dot(normed, wu[...])
    hidden_grad = dot(cot[...], wd[...], 1, 1)
    gate, upper = gate_s[...], upper_s[...]
    sig = jax.nn.sigmoid(gate)
    silu = gate * sig
    hidden = (silu * upper).astype(BF16)
    gate_grad = (hidden_grad * upper * sig * (1.0 + gate * (1.0 - sig))).astype(BF16)
    upper_grad = (hidden_grad * silu).astype(BF16)
    back = dot(gate_grad, wg[...], 1, 1) + dot(upper_grad, wu[...], 1, 1)
    part3[...] = ar_view(back.astype(BF16))
    sum3 = TpSum(place, part3, tot3, buf3, (s3, r3))
    sum3.start()
    part2[...] = ar_view(dot(hidden, wd[...]).astype(BF16))
    sum3.mid()
    sum2 = TpSum(place, part2, tot2, buf2, (s2, r2))
    sum2.start()

    def weight_grad(lhs, rhs, lo, cb=0):
        left[...] = lhs.T
        w = rhs.shape[1 - cb]

        def rows(i, carry):
            piece = dot(left[pl.ds(pl.multiple_of(i * 192, 192), 192)], rhs, 1, cb)
            grads[i // 4, i % 4, :, :, lo : lo + w] = piece.astype(BF16).reshape(4, 48, w)
            return carry

        lax.fori_loop(0, 8, rows, 0)

    weight_grad(normed, gate_grad, 0)
    weight_grad(normed, upper_grad, FFL)
    sum2.mid()
    weight_grad(cot[...], hidden, 2 * FFL)
    sum3.fin()
    sum3.landed()
    grad = ar_load(tot3).astype(F32)
    mixed_part, gain_grad = norm_back(mixed, inverse, gain[...], grad)
    gain_grad_out[...] = gain_grad
    mixed_grad = cot[...].astype(F32) + mixed_part
    mixed_grad_out[...] = mixed_grad
    branch = mixed_grad.astype(BF16)
    me_t = place.zh * 2 + place.c
    own = dot(wo[me_t], branch, 1, 1).astype(BF16)
    dgrp[0] = own[: 2 * HEAD]
    dgrp[1] = own[2 * HEAD :]
    pair_cp = remote(dgrp.at[1 - zl], dout.at[zl], pair_sem.at[0], pair_sem.at[1], partner)
    pair_cp.start()
    dout[zl] = dgrp[zl]
    heads = att[pl.ds(me_t * 2, 2)].reshape(HEADS_LOCAL, ROWS)
    weight_grad(branch, heads, W_FFN, 1)
    sum2.fin()
    sum2.landed()
    result[...] = (mixed + ar_load(tot2).astype(F32)).astype(BF16)
    pair_cp.wait_recv()
    pair_cp.wait_send()
    sum3.end()
    sum2.end()


def middle(tokens, cot, att, wo, gain, wg, wu, wd):
    vm = pl.BlockSpec(memory_space=pltpu.VMEM)
    shape = (2, AR_PIECES, AR_ROWS, WIDTH)
    return pl.pallas_call(
        middle_kernel,
        out_shape=(
            jax.ShapeDtypeStruct((ROWS, WIDTH), BF16),
            jax.ShapeDtypeStruct((2, 4, 4, 48, W_MID), BF16),
            jax.ShapeDtypeStruct((ROWS, WIDTH), F32),
            jax.ShapeDtypeStruct((2, 2 * HEAD, ROWS), BF16),
            jax.ShapeDtypeStruct((1, WIDTH), F32),
        ),
        in_specs=[vm] * 8,
        out_specs=(vm,) * 5,
        scratch_shapes=[
            pltpu.VMEM((ROWS, FFL), F32),
            pltpu.VMEM((ROWS, FFL), F32),
            pltpu.VMEM((WIDTH, ROWS), BF16),
            pltpu.VMEM(shape, BF16),
            pltpu.VMEM(shape, BF16),
            pltpu.VMEM(shape, BF16),
            pltpu.VMEM(shape, BF16),
            *tp_scratch(),
            *tp_scratch(),
            pltpu.VMEM((2, 2 * HEAD, ROWS), BF16),
            pltpu.SemaphoreType.DMA((2,)),
        ],
        compiler_params=pltpu.CompilerParams(
            collective_id=1, has_side_effects=True, vmem_limit_bytes=VMEM_LIMIT
        ),
        name="middle",
    )(tokens, cot, att, wo, gain, wg, wu, wd)


def cut(width, first="x", sizes=(3, 4)):
    pieces, lo, n = [], 0, 0
    order = ("x", "y") if first == "x" else ("y", "x")
    while lo < width:
        w = min(sizes[n % len(sizes)] * 128, width - lo)
        pieces.append((order[n % 2], lo, w))
        lo += w
        n += 1
    return pieces


MID_PIECES = cut(W_MID, "x", (3, 4))


def back_kernel(
    lengths, qkv, kvall, o_in, lse, dout, grads,
    dqkv, sums,
    qaug, dot_t, delta, dq, dkv, mine,
    kb1, kr1, kb2, kr2, ksend, krecv,
    b1, r1, b2, r2, zb, gsend, grecv, pair_sem,
):
    place = Place()
    zl, x, y = place.zl, place.x, place.y
    partner = place.at(**place.pair)
    greet(
        [partner, place.at(zl=1 - zl)]
        + [place.along(a, s) for a in ("x", "y") for s in (1, -1)]
    )
    pieces = [
        GradSum(place, first, lo, w, grads, (b1, r1, b2, r2, zb), (gsend, grecv), n)
        for n, (first, lo, w) in enumerate(MID_PIECES)
    ]
    for piece in pieces:
        piece.one.start()
    ends = ends_of(lengths)
    low = place.low_block(x, y)
    for s in range(2):
        segs = query_segments(ends, jnp.where(s == 0, low, 31 - low) * ROWS)
        for h in range(2):
            lanes, feats = slice(h * ROWS, (h + 1) * ROWS), slice(h * HEAD, (h + 1) * HEAD)
            qaug[s, :HEAD, lanes] = qkv[s, feats]
            qaug[s, HEAD:, lanes] = segs
            d = dout[s, feats]
            dot_t[s, :, lanes] = d
            delta[s, :, lanes] = jnp.sum(d.astype(F32) * o_in[s, feats], 0, keepdims=True)
    dq[...] = jnp.zeros(dq.shape, F32)

    def unit(qs, kx, ky, ks, kbase, causal):
        kv = kvall[kx, ky, ks]
        q = qaug[qs]
        do = dot_t[qs]
        ka = jnp.concatenate([kv[:HEAD], key_segments(ends, kbase)], 0)
        s = dot(ka, q, 0, 0)
        p = jnp.exp2(s - lse[qs])
        if causal:
            key = lax.broadcasted_iota(jnp.int32, (ROWS, 2 * ROWS), 0)
            query = lax.broadcasted_iota(jnp.int32, (ROWS, 2 * ROWS), 1)
            p = jnp.where(key <= jnp.where(query >= ROWS, query - ROWS, query), p, 0.0)
        dp = dot(kv[HEAD:], do, 0, 0)
        ds = (p * (dp - delta[qs])).astype(BF16)
        dq[qs] = dq[qs] + dot(kv[:HEAD], ds)
        dk = dot(q[:HEAD], ds, 1, 1)
        dv = dot(do, p.astype(BF16), 1, 1)
        return jnp.concatenate([dk, dv], 0)

    first = unit(0, x, y, 0, low * ROWS, True) + unit(1, x, y, 0, low * ROWS, False)
    dkv[x, y, 0] = first.astype(BF16)
    dkv[x, y, 1] = unit(1, x, y, 1, (31 - low) * ROWS, True).astype(BF16)

    def step(i, carry):
        kx, ky = lax.rem(x + i // 4, 4), lax.rem(y + i % 4, 4)
        there = place.low_block(kx, ky)
        one = unit(1, kx, ky, 0, there * ROWS, False)
        before = there < low
        sel = jnp.where(before, 0, 1)
        two = unit(sel, kx, ky, sel, jnp.where(before, there, 31 - there) * ROWS, False)
        share = jnp.where(before, 1.0, 0.0)
        dkv[kx, ky, 0] = (one + two * share).astype(BF16)
        dkv[kx, ky, 1] = (two * (1.0 - share)).astype(BF16)
        return carry

    lax.fori_loop(1, 6, step, 0)
    for piece in pieces:
        piece.one.mid()
    lax.fori_loop(6, 16, step, 0)

    def key_sum(slot, axis):
        other = "y" if axis == "x" else "x"
        if axis == "x":
            half = lambda d, h: dkv.at[d, :, slot, pl.ds(h * HEAD, HEAD)]
        else:
            half = lambda d, h: dkv.at[:, d, slot, pl.ds(h * HEAD, HEAD)]
        one = RingSum(
            place, axis, half, lambda k: kb1.at[slot, k], lambda h: kr1.at[slot, h],
            lambda k: ksend.at[slot, k], lambda k: krecv.at[slot, k], add2_lead, add3_lead,
        )
        two = RingSum(
            place, other, lambda d, h: kr1.at[slot, h, d], lambda k: kb2.at[slot, k],
            lambda h: kr2.at[slot, h], lambda k: ksend.at[slot, 6 + k], lambda k: krecv.at[slot, 6 + k],
            add2_flat, add3_flat,
        )
        return one, two

    ka, kb = key_sum(0, "x"), key_sum(1, "y")
    ka[0].start()
    kb[0].start()
    for piece in pieces:
        piece.one.fin()
        piece.two.start()
    ka[0].mid()
    kb[0].mid()
    for piece in pieces:
        piece.two.mid()
    ka[0].fin()
    kb[0].fin()
    ka[1].start()
    kb[1].start()
    for piece in pieces:
        piece.two.fin()
        piece.zcp().start()
    ka[1].mid()
    kb[1].mid()
    ka[1].fin()
    kb[1].fin()
    for s in range(2):
        for h in range(2):
            mine[s, h * HEAD : (h + 1) * HEAD] = (dq[s, :, h * ROWS : (h + 1) * ROWS] * SCALE).astype(BF16)
            mine[s, (2 + h) * HEAD : (3 + h) * HEAD] = kr2[s, h]
    pair_cp = remote(mine.at[1 - zl], dqkv.at[zl], pair_sem.at[0], pair_sem.at[1], partner)
    pair_cp.start()
    dqkv[zl] = mine[zl]
    for piece, (_, lo, w) in zip(pieces, MID_PIECES):
        sums[:, lo : lo + w] = piece.total()
    landing = dqkv.at[1 - zl]
    pair_cp.wait_send()
    remote(landing, landing, pair_sem.at[0], pair_sem.at[1], partner).wait_recv()
    for piece in pieces:
        piece.end()
    for one, two in (ka, kb):
        one.end()
        two.end()


def back(lengths, qkv, kvall, o_in, lse, dout, grads):
    vm = pl.BlockSpec(memory_space=pltpu.VMEM)
    dma = pltpu.SemaphoreType.DMA
    return pl.pallas_call(
        back_kernel,
        out_shape=(
            jax.ShapeDtypeStruct((2, 4 * HEAD, ROWS), BF16),
            jax.ShapeDtypeStruct((48, W_MID), F32),
        ),
        in_specs=[pl.BlockSpec(memory_space=pltpu.SMEM)] + [vm] * 6,
        out_specs=(vm,) * 2,
        scratch_shapes=[
            pltpu.VMEM((2, HEAD + SEG, 2 * ROWS), BF16),
            pltpu.VMEM((2, HEAD, 2 * ROWS), BF16),
            pltpu.VMEM((2, 1, 2 * ROWS), F32),
            pltpu.VMEM((2, HEAD, 2 * ROWS), F32),
            pltpu.VMEM((4, 4, 2, 2 * HEAD, ROWS), BF16),
            pltpu.VMEM((2, 4 * HEAD, ROWS), BF16),
            pltpu.VMEM((2, 6, 4, HEAD, ROWS), BF16),
            pltpu.VMEM((2, 2, 4, HEAD, ROWS), BF16),
            pltpu.VMEM((2, 6, HEAD, ROWS), BF16),
            pltpu.VMEM((2, 2, HEAD, ROWS), BF16),
            dma((2, 12)),
            dma((2, 12)),
            *grad_scratch(W_MID, len(MID_PIECES)),
            dma((2,)),
        ],
        compiler_params=pltpu.CompilerParams(
            collective_id=2, has_side_effects=True, vmem_limit_bytes=VMEM_LIMIT
        ),
        name="back",
    )(lengths, qkv, kvall, o_in, lse, dout, grads)


W_TAIL = HEADS_LOCAL + 2 * PAIRS_LOCAL
TAIL_PIECES = cut(W_TAIL, "x", (1, 1, 2, 2))
GAIN_ROWS = 2 * WIDTH // 128


def tail_kernel(
    lengths, freq, tokens, gain, normed, dqkv, wq, wk, wv, mixed_grad, ffn_gain_grad,
    tokens_grad, sums, gains,
    rows, left, grads, part, total, buf, s4, r4,
    b1, r1, b2, r2, zb, gsend, grecv, gain_buf, gain_sum, gn_send, gn_recv,
):
    place = Place()
    zl, x, y = place.zl, place.x, place.y
    others = [place.along(a, s) for a in ("x", "y") for s in (1, 2, 3)]
    greet(others + [place.at(zl=1 - zl), place.at(zh=1 - place.zh), place.at(c=1 - place.c)])
    ends = ends_of(lengths)
    block = zl * 16 + x * 4 + y
    cosine, sine = rotation(ends, lengths, block * ROWS, freq[...])
    for g in range(2):
        for h in range(3):
            a = dqkv[g, h * HEAD : h * HEAD + HALF].astype(F32)
            b = dqkv[g, h * HEAD + HALF : (h + 1) * HEAD].astype(F32)
            if h == 2:
                a, b = a * LN2, b * LN2
            at = (2 * g + h) * HEAD if h < 2 else HEADS_LOCAL + g * HEAD
            rows[at : at + HALF] = (a * cosine + b * sine).astype(BF16)
            rows[at + HALF : at + HEAD] = (b * cosine - a * sine).astype(BF16)
        at = HEADS_LOCAL + PAIRS_LOCAL + g * HEAD
        rows[at : at + HEAD] = dqkv[g, 3 * HEAD :]
    back = dot(rows[:HEADS_LOCAL], wq[...], 0, 1)
    back = back + dot(rows[HEADS_LOCAL : HEADS_LOCAL + PAIRS_LOCAL], wk[...], 0, 1)
    back = back + dot(rows[HEADS_LOCAL + PAIRS_LOCAL :], wv[...], 0, 1)
    part[...] = ar_view(back.astype(BF16))
    sum4 = TpSum(place, part, total, buf, (s4, r4))
    sum4.start()
    left[...] = normed[...].T

    def weight_rows(i, carry):
        piece = dot(left[pl.ds(pl.multiple_of(i * 192, 192), 192)], rows[...], 1, 1)
        grads[i // 4, i % 4] = piece.astype(BF16).reshape(4, 48, W_TAIL)
        return carry

    lax.fori_loop(0, 8, weight_rows, 0)
    pieces = [
        GradSum(place, first, lo, w, grads, (b1, r1, b2, r2, zb), (gsend, grecv), n)
        for n, (first, lo, w) in enumerate(TAIL_PIECES)
    ]
    for piece in pieces:
        piece.one.start()
    sum4.mid()
    for piece in pieces:
        piece.one.mid()
    sum4.fin()
    sum4.landed()
    source = tokens[...].astype(F32)
    inverse = lax.rsqrt(jnp.mean(source * source, -1, keepdims=True) + EPS)
    grad = ar_load(total).astype(F32)
    source_part, gain_grad = norm_back(source, inverse, gain[...], grad)
    tokens_grad[...] = (mixed_grad[...] + source_part).astype(BF16)
    gain_sum[0, 0:1] = gain_grad
    gain_sum[0, 1:2] = ffn_gain_grad[...]

    def gain_copies(stage, axis):
        if axis == "zl":
            peers = [place.at(zl=1 - zl)]
        else:
            peers = [place.along(axis, s) for s in (1, 2, 3)]
        return [
            remote(gain_sum.at[stage], gain_buf.at[stage, k], gn_send.at[stage, k], gn_recv.at[stage, k], peer)
            for k, peer in enumerate(peers)
        ]

    sent = gain_copies(0, "x")
    for cp in sent:
        cp.start()
    for piece in pieces:
        piece.one.fin()
        piece.two.start()
    for cp in sent:
        cp.wait_recv()
    gain_sum[1] = gain_sum[0] + gain_buf[0, 0] + gain_buf[0, 1] + gain_buf[0, 2]
    sent_y = gain_copies(1, "y")
    for cp in sent_y:
        cp.start()
    for piece in pieces:
        piece.two.mid()
    for cp in sent_y:
        cp.wait_recv()
    gain_sum[2] = gain_sum[1] + gain_buf[1, 0] + gain_buf[1, 1] + gain_buf[1, 2]
    sent_z = gain_copies(2, "zl")
    for cp in sent_z:
        cp.start()
    for piece in pieces:
        piece.two.fin()
        piece.zcp().start()
    for cp in sent_z:
        cp.wait_recv()
    gains[...] = gain_sum[2] + gain_buf[2, 0]
    for piece, (_, lo, w) in zip(pieces, TAIL_PIECES):
        sums[:, lo : lo + w] = piece.total()
    for cp in [*sent, *sent_y, *sent_z]:
        cp.wait_send()
    for piece in pieces:
        piece.end()
    sum4.end()


def tail(lengths, freq, tokens, gain, normed, dqkv, wq, wk, wv, mixed_grad, ffn_gain_grad):
    vm = pl.BlockSpec(memory_space=pltpu.VMEM)
    dma = pltpu.SemaphoreType.DMA
    shape = (2, AR_PIECES, AR_ROWS, WIDTH)
    return pl.pallas_call(
        tail_kernel,
        out_shape=(
            jax.ShapeDtypeStruct((ROWS, WIDTH), BF16),
            jax.ShapeDtypeStruct((48, W_TAIL), F32),
            jax.ShapeDtypeStruct((2, WIDTH), F32),
        ),
        in_specs=[pl.BlockSpec(memory_space=pltpu.SMEM)] + [vm] * 10,
        out_specs=(vm,) * 3,
        scratch_shapes=[
            pltpu.VMEM((W_TAIL, ROWS), BF16),
            pltpu.VMEM((WIDTH, ROWS), BF16),
            pltpu.VMEM((2, 4, 4, 48, W_TAIL), BF16),
            pltpu.VMEM(shape, BF16),
            pltpu.VMEM(shape, BF16),
            *tp_scratch(),
            *grad_scratch(W_TAIL, len(TAIL_PIECES)),
            pltpu.VMEM((3, 3, 2, WIDTH), F32),
            pltpu.VMEM((3, 2, WIDTH), F32),
            dma((3, 3)),
            dma((3, 3)),
        ],
        compiler_params=pltpu.CompilerParams(
            collective_id=3, has_side_effects=True, vmem_limit_bytes=VMEM_LIMIT
        ),
        name="tail",
    )(lengths, freq, tokens, gain, normed, dqkv, wq, wk, wv, mixed_grad, ffn_gain_grad)


def local(
    tokens, norm_gain, query_weight, key_matrix, value_matrix, out_weight,
    ffn_gain, gate_weight, up_weight, down_weight, cotangent, lengths,
):
    freq = jnp.asarray(
        (THETA ** (-2.0 * np.arange(HALF) / HEAD)).astype(np.float32).reshape(HALF, 1)
    )
    gain1, gain2 = norm_gain.reshape(1, WIDTH), ffn_gain.reshape(1, WIDTH)
    normed, qkv, kvall, att, o, lse, wo_full = front(
        lengths, freq, tokens, gain1, query_weight, key_matrix, value_matrix, out_weight
    )
    result, grads, mixed_grad, dout, ffn_gain_grad = middle(
        tokens, cotangent, att, wo_full, gain2, gate_weight, up_weight, down_weight
    )
    dqkv, mid_sums = back(lengths, qkv, kvall, o, lse, dout, grads)
    tokens_grad, sums, gains = tail(
        lengths, freq, tokens, gain1, normed, dqkv, query_weight, key_matrix, value_matrix,
        mixed_grad, ffn_gain_grad,
    )
    block = (lax.axis_index("zl") * 4 + lax.axis_index("x")) * 4 + lax.axis_index("y")
    own = lax.dynamic_slice(gains, (0, block * 48), (2, 48))
    return (
        result,
        tokens_grad,
        own[0],
        sums[:, :HEADS_LOCAL],
        sums[:, HEADS_LOCAL : HEADS_LOCAL + PAIRS_LOCAL],
        sums[:, HEADS_LOCAL + PAIRS_LOCAL :],
        mid_sums[:, W_FFN:].T,
        own[1],
        mid_sums[:, :FFL],
        mid_sums[:, FFL : 2 * FFL],
        mid_sums[:, 2 * FFL : W_FFN].T,
    )


def solution(mesh):
    split = Mesh(mesh.devices.reshape(2, 4, 4, 2, 2), AXES)
    in_specs = (
        P(BLK, None),
        P(),
        P(None, TP),
        P(None, TP),
        P(None, TP),
        P(TP, None),
        P(),
        P(None, TP),
        P(None, TP),
        P(TP, None),
        P(BLK, None),
        P(),
    )
    out_specs = (
        P(BLK, None),
        P(BLK, None),
        P(BLK),
        P(BLK, TP),
        P(BLK, TP),
        P(BLK, TP),
        P(TP, BLK),
        P(BLK),
        P(BLK, TP),
        P(BLK, TP),
        P(TP, BLK),
    )
    return jax.shard_map(local, mesh=split, in_specs=in_specs, out_specs=out_specs, check_vma=False)
```

```python
import jax
import jax.numpy as jnp
import numpy as np
from jax import lax
from jax.experimental import pallas as pl
from jax.experimental.pallas import tpu as pltpu
from jax.sharding import Mesh
from jax.sharding import PartitionSpec as P

AXES = ("zl", "x", "y", "zh", "c")
BLK = ("zl", "x", "y")
TP = ("zh", "c")
HEAD = 96
HALF = HEAD // 2
ROWS = 256
WIDTH = 1536
HEADS_LOCAL = 384
PAIRS_LOCAL = 192
FFL = 1024
EPS = 1e-05
THETA = 100000.0
SCALE = HEAD**-0.5
LOG2E = float(np.log2(np.e))
LN2 = float(np.log(2.0))
BIG = 1e30
SEG = 16
MESH = pl.DeviceIdType.MESH
F32 = jnp.float32
BF16 = jnp.bfloat16
VMEM_LIMIT = 60 * 2**20


def dot(a, b, ca=1, cb=0):
    return lax.dot_general(a, b, (((ca,), (cb,)), ((), ())), preferred_element_type=F32)


class Place:
    def __init__(self):
        self.zl, self.x, self.y, self.zh, self.c = (lax.axis_index(a) for a in AXES)

    def at(self, **changes):
        own = dict(zl=self.zl, x=self.x, y=self.y, zh=self.zh, c=self.c)
        own.update(changes)
        return tuple(own[a] for a in AXES)

    def along(self, axis, step):
        return self.at(**{axis: lax.rem(getattr(self, axis) + (step + 4), 4)})

    @property
    def pair(self):
        return dict(zl=1 - self.zl, x=3 - self.x, y=3 - self.y)

    def low_block(self, x, y):
        p = x * 4 + y
        return jnp.where(self.zl == 0, p, 15 - p)


def call(peers):
    barrier = pltpu.get_barrier_semaphore()
    for peer in peers:
        pl.semaphore_signal(barrier, inc=1, device_id=peer, device_id_type=MESH)


def answer(peers):
    pl.semaphore_wait(pltpu.get_barrier_semaphore(), len(peers))


def remote(src, dst, send, recv, device):
    return pltpu.make_async_remote_copy(
        src_ref=src, dst_ref=dst, send_sem=send, recv_sem=recv, device_id=device, device_id_type=MESH
    )


def seg_rows(ends, base):
    token = base + lax.broadcasted_iota(jnp.int32, (SEG, ROWS), 1)
    row = lax.broadcasted_iota(jnp.int32, (SEG, ROWS), 0)
    inside = jnp.zeros((SEG, ROWS), F32)
    start = 0
    for d in range(5):
        hit = (row == d) & (token >= start) & (token < ends[d])
        inside = jnp.where(hit, 1.0, inside)
        start = ends[d]
    return inside, row


def key_segments(ends, base):
    return seg_rows(ends, base)[0].astype(BF16)


def query_segments(ends, base):
    inside, row = seg_rows(ends, base)
    return jnp.where(row < 5, (inside - 1.0) * BIG, 0.0).astype(BF16)


def ends_of(lengths_ref):
    ends, total = [], 0
    for d in range(5):
        total = total + lengths_ref[d]
        ends.append(total)
    return ends


def rotation(ends, lengths_ref, base, freq):
    token = base + lax.broadcasted_iota(jnp.int32, (1, ROWS), 1)
    begin = jnp.zeros((1, ROWS), jnp.int32)
    for d in range(5):
        begin = begin + jnp.where(token >= ends[d], lengths_ref[d], 0)
    angle = (token - begin).astype(F32) * freq
    return jnp.cos(angle), jnp.sin(angle)


class RingSum:
    def __init__(self, place, axis, half, bufs, out, send, recv, add2, add3):
        self.half, self.bufs, self.out, self.add2, self.add3 = half, bufs, out, add2, add3
        me = getattr(place, axis)
        self.me = me
        self.r, self.l, self.o = (lax.rem(me + k, 4) for k in (1, 3, 2))
        self.right, self.left = place.along(axis, 1), place.along(axis, -1)
        self.send, self.recv = send, recv

    def cp(self, k):
        src = (
            lambda: self.half(self.o, 0),
            lambda: self.half(self.o, 1),
            lambda: self.half(self.r, 1),
            lambda: self.half(self.l, 0),
            lambda: self.bufs(0),
            lambda: self.bufs(1),
        )[k]()
        return remote(
            src, self.bufs(k), self.send(k), self.recv(k), (self.right, self.left)[k % 2]
        )

    def start(self):
        for k in range(4):
            self.cp(k).start()

    def mid(self):
        self.cp(0).wait_recv()
        self.cp(0).wait_send()
        self.add2(self.bufs(0), self.half(self.r, 0))
        self.cp(4).start()
        self.cp(1).wait_recv()
        self.cp(1).wait_send()
        self.add2(self.bufs(1), self.half(self.l, 1))
        self.cp(5).start()

    def fin(self):
        self.cp(4).wait_recv()
        self.cp(3).wait_recv()
        self.add3(self.out(0), self.half(self.me, 0), self.bufs(4), self.bufs(3))
        self.cp(5).wait_recv()
        self.cp(2).wait_recv()
        self.add3(self.out(1), self.half(self.me, 1), self.bufs(5), self.bufs(2))

    def end(self):
        for k in range(2, 6):
            self.cp(k).wait_send()


def add2_lead(dst, src):
    for i in range(dst.shape[0]):
        dst[i] = dst[i] + src[i]


def add3_lead(out, a, b, d):
    for i in range(out.shape[0]):
        out[i] = (a[i].astype(F32) + b[i].astype(F32) + d[i].astype(F32)).astype(BF16)


def add2_flat(dst, src):
    dst[...] = dst[...] + src[...]


def add3_flat(out, a, b, d):
    out[...] = (a[...].astype(F32) + b[...].astype(F32) + d[...].astype(F32)).astype(BF16)


class GradSum:
    def __init__(self, place, first, lo, w, g, bufs, sems, n):
        b1, r1, b2, r2, zb = bufs
        send, recv = sems
        self.place, self.cols, self.r2, self.zb, self.n = place, pl.ds(lo, w), r2, zb, n
        self.send, self.recv = send, recv
        cols = self.cols
        second = "y" if first == "x" else "x"
        if first == "x":
            half1 = lambda d, h: g.at[h, d, :, :, cols]
        else:
            half1 = lambda d, h: g.at[h, :, d, :, cols]
        self.one = RingSum(
            place, first, half1, lambda k: b1.at[k, :, :, cols], lambda h: r1.at[h, :, :, cols],
            lambda k: send.at[n, k], lambda k: recv.at[n, k], add2_lead, add3_lead,
        )
        self.two = RingSum(
            place, second, lambda d, h: r1.at[h, d, :, cols], lambda k: b2.at[k, :, cols],
            lambda h: r2.at[h, :, cols], lambda k: send.at[n, 6 + k], lambda k: recv.at[n, 6 + k],
            add2_flat, add3_flat,
        )

    def zcp(self):
        other = 1 - self.place.zl
        return remote(
            self.r2.at[other, :, self.cols], self.zb.at[:, self.cols], self.send.at[self.n, 12],
            self.recv.at[self.n, 12], self.place.at(zl=other),
        )

    def total(self):
        self.zcp().wait_recv()
        own = self.r2[self.place.zl, :, self.cols].astype(F32)
        return own + self.zb[:, self.cols].astype(F32)

    def end(self):
        self.one.end()
        self.two.end()
        self.zcp().wait_send()


def grad_scratch(width, pieces):
    return [
        pltpu.VMEM((6, 4, 48, width), BF16),
        pltpu.VMEM((2, 4, 48, width), BF16),
        pltpu.VMEM((6, 48, width), BF16),
        pltpu.VMEM((2, 48, width), BF16),
        pltpu.VMEM((48, width), BF16),
        pltpu.SemaphoreType.DMA((pieces, 13)),
        pltpu.SemaphoreType.DMA((pieces, 13)),
    ]


AR_PIECES = 4
AR_ROWS = ROWS // 2 // AR_PIECES


class TpSum:
    def __init__(self, place, part, total, buf, sems):
        self.place, self.part, self.total, self.buf = place, part, total, buf
        self.send, self.recv = sems
        self.core = place.at(c=1 - place.c)
        self.far = place.at(zh=1 - place.zh)

    def a(self, k):
        return remote(
            self.part.at[1 - self.place.c, k], self.buf.at[0, k], self.send.at[0, k], self.recv.at[0, k], self.core
        )

    def b(self, k):
        return remote(self.buf.at[0, k], self.buf.at[1, k], self.send.at[1, k], self.recv.at[1, k], self.far)

    def d(self, k):
        rows = self.total.at[self.place.c, k]
        return remote(rows, rows, self.send.at[2, k], self.recv.at[2, k], self.core)

    def start(self):
        for k in range(AR_PIECES):
            self.a(k).start()

    def mid(self):
        for k in range(AR_PIECES):
            self.a(k).wait_recv()
            self.buf[0, k] = self.buf[0, k] + self.part[self.place.c, k]
            self.b(k).start()

    def fin(self):
        for k in range(AR_PIECES):
            self.b(k).wait_recv()
            self.total[self.place.c, k] = self.buf[0, k] + self.buf[1, k]
            self.d(k).start()

    def landed(self):
        for k in range(AR_PIECES):
            rows = self.total.at[1 - self.place.c, k]
            remote(rows, rows, self.send.at[2, k], self.recv.at[2, k], self.core).wait_recv()

    def end(self):
        for k in range(AR_PIECES):
            self.a(k).wait_send()
            self.b(k).wait_send()
            self.d(k).wait_send()


def tp_scratch():
    return [
        pltpu.VMEM((2, AR_PIECES, AR_ROWS, WIDTH), BF16),
        pltpu.SemaphoreType.DMA((3, AR_PIECES)),
        pltpu.SemaphoreType.DMA((3, AR_PIECES)),
    ]


def ar_view(value):
    return value.reshape(2, AR_PIECES, AR_ROWS, WIDTH)


def ar_load(ref):
    return ref[...].reshape(ROWS, WIDTH)


def front_kernel(
    lengths, freq, tokens, gain, wq, wkt, wvt, wo,
    normed_out, qkv, kvall, att, o_out, lse_out, wo_full,
    grp, qaug, acc, peak, total, mine,
    pair_sem, ag_send, ag_recv, o_send, o_recv, w_send, w_recv,
):
    place = Place()
    zl, x, y, zh, c = place.zl, place.x, place.y, place.zh, place.c
    partner = place.at(**place.pair)
    far_partner = place.at(**place.pair, zh=1 - zh)
    far = place.at(zh=1 - zh)
    core = place.at(c=1 - c)
    xr, xl, yr, yl = place.along("x", 1), place.along("x", -1), place.along("y", 1), place.along("y", -1)
    peers = [partner, far_partner, far, core, xr, xl, yr, yl]
    call(peers)
    ends = ends_of(lengths)
    block = zl * 16 + x * 4 + y
    cosine, sine = rotation(ends, lengths, block * ROWS, freq[...])
    source = tokens[...].astype(F32)
    inverse = lax.rsqrt(jnp.mean(source * source, -1, keepdims=True) + EPS)
    normed = (source * inverse * gain[...].reshape(1, WIDTH)).astype(BF16)
    normed_out[...] = normed

    def turned(u, factor):
        a, b = u[:HALF], u[HALF:]
        if factor is None:
            return a * cosine - b * sine, b * cosine + a * sine
        return (a * cosine - b * sine) * factor, (b * cosine + a * sine) * factor

    qt = dot(normed, wq[...]).T
    kt = dot(wkt[...], normed, 1, 1)
    vt = dot(wvt[...], normed, 1, 1)
    for g in range(2):
        for h in range(2):
            a, b = turned(qt[(2 * g + h) * HEAD : (2 * g + h + 1) * HEAD], SCALE * LOG2E)
            grp[g, h * HEAD : h * HEAD + HALF] = a.astype(BF16)
            grp[g, h * HEAD + HALF : (h + 1) * HEAD] = b.astype(BF16)
        a, b = turned(kt[g * HEAD : (g + 1) * HEAD], None)
        grp[g, 2 * HEAD : 2 * HEAD + HALF] = a.astype(BF16)
        grp[g, 2 * HEAD + HALF : 3 * HEAD] = b.astype(BF16)
        grp[g, 3 * HEAD :] = vt[g * HEAD : (g + 1) * HEAD].astype(BF16)

    answer(peers)
    pair_cp = remote(grp.at[1 - zl], qkv.at[zl], pair_sem.at[0], pair_sem.at[1], partner)
    pair_cp.start()
    qkv[zl] = grp[zl]
    kvall[x, y, zl] = grp[zl, 2 * HEAD :]

    def gather(n, slot, swap):
        me1, me2 = (y, x) if swap else (x, y)
        r1, l1, r2, l2 = (yr, yl, xr, xl) if swap else (xr, xl, yr, yl)

        def ref(i, j, part=None):
            i, j = lax.rem(i + 4, 4), lax.rem(j + 4, 4)
            v = kvall.at[j, i, slot] if swap else kvall.at[i, j, slot]
            return v if part is None else v.at[pl.ds(part * HEAD, HEAD)]

        def cp(k, view, dev):
            return remote(view, view, ag_send.at[n, k], ag_recv.at[n, k], dev)

        def stage(base, i, j, di, dj, r, l):
            return dict(
                right=cp(base, ref(i, j), r),
                left=cp(base + 1, ref(i, j), l),
                from_left=cp(base, ref(i - di, j - dj), r),
                from_right=cp(base + 1, ref(i + di, j + dj), l),
                on_right=cp(base + 2, ref(i - di, j - dj, 0), r),
                on_left=cp(base + 3, ref(i + di, j + dj, 1), l),
                from_left2=cp(base + 2, ref(i + 2 * di, j + 2 * dj, 0), r),
                from_right2=cp(base + 3, ref(i + 2 * di, j + 2 * dj, 1), l),
            )

        s1 = stage(0, me1, me2, 1, 0, r1, l1)
        s2 = [stage(4 + 4 * k, me1 + k, me2, 0, 1, r2, l2) for k in range(4)]
        return s1, s2

    def begin(st):
        st["right"].start()
        st["left"].start()

    def hand_on(st):
        st["from_left"].wait_recv()
        st["on_right"].start()
        st["from_right"].wait_recv()
        st["on_left"].start()

    def complete(st):
        st["from_left2"].wait_recv()
        st["from_right2"].wait_recv()

    own, other = gather(0, zl, False), gather(1, 1 - zl, True)
    both = (own, other)
    begin(own[0])
    begin(own[1][0])
    pair_cp.wait_recv()
    kvall[x, y, 1 - zl] = qkv[1 - zl, 2 * HEAD :]
    begin(other[0])
    begin(other[1][0])
    me_t = zh * 2 + c
    wo_cps = [
        remote(wo, wo_full.at[me_t], w_send.at[0], w_recv.at[0], far),
        remote(wo, wo_full.at[me_t], w_send.at[1], w_recv.at[1], core),
    ]
    for cp in wo_cps:
        cp.start()

    low = place.low_block(x, y)
    for s in range(2):
        base = jnp.where(s == 0, low, 31 - low) * ROWS
        segs = query_segments(ends, base)
        for h in range(2):
            qaug[s, :HEAD, h * ROWS : (h + 1) * ROWS] = qkv[s, h * HEAD : (h + 1) * HEAD]
            qaug[s, HEAD:, h * ROWS : (h + 1) * ROWS] = segs
    peak[...] = jnp.full(peak.shape, -BIG, F32)
    total[...] = jnp.zeros(total.shape, F32)
    acc[...] = jnp.zeros(acc.shape, F32)

    def unit(qs, kx, ky, ks, kbase, causal):
        kv = kvall[kx, ky, ks]
        ka = jnp.concatenate([kv[:HEAD], key_segments(ends, kbase)], 0)
        s = dot(ka, qaug[qs], 0, 0)
        if causal:
            key = lax.broadcasted_iota(jnp.int32, (ROWS, 2 * ROWS), 0)
            query = lax.broadcasted_iota(jnp.int32, (ROWS, 2 * ROWS), 1)
            s = jnp.where(key <= jnp.where(query >= ROWS, query - ROWS, query), s, -BIG)
        old = peak[qs]
        new = jnp.maximum(old, jnp.max(s, 0, keepdims=True))
        p = jnp.exp2(s - new)
        fade = jnp.exp2(old - new)
        peak[qs] = new
        total[qs] = total[qs] * fade + jnp.sum(p, 0, keepdims=True)
        acc[qs] = acc[qs] * fade + dot(kv[HEAD:], p.astype(BF16))

    def shard(dx, dy):
        kx, ky = lax.rem(x + dx, 4), lax.rem(y + dy, 4)
        there = place.low_block(kx, ky)
        unit(1, kx, ky, 0, there * ROWS, False)
        sel = jnp.where(there < low, 0, 1)
        unit(sel, kx, ky, sel, jnp.where(there < low, there, 31 - there) * ROWS, False)

    def shards(count, offsets):
        def step(i, carry):
            shard(*offsets(i))
            return carry

        lax.fori_loop(0, count, step, 0)

    unit(0, x, y, 0, low * ROWS, True)
    unit(1, x, y, 1, (31 - low) * ROWS, True)
    unit(1, x, y, 0, low * ROWS, False)
    for s1, s2 in both:
        hand_on(s1)
        begin(s2[3])
        begin(s2[1])
    for s1, s2 in both:
        hand_on(s2[0])
    shards(4, lambda i: ((1 - i // 2) * (2 * i + 1), (i // 2) * (2 * i - 3)))
    for s1, s2 in both:
        complete(s1)
        begin(s2[2])
    for s1, s2 in both:
        hand_on(s2[3])
        hand_on(s2[1])
    shards(4, lambda i: (2 * (i // 2) + 1, 2 * lax.rem(i, 2) + 1))
    for s1, s2 in both:
        complete(s2[0])
        hand_on(s2[2])
    shards(2, lambda i: (2 * i, 2 - 2 * i))
    for s1, s2 in both:
        complete(s2[3])
        complete(s2[1])
    shards(4, lambda i: ((1 - i // 2) * (2 * i + 1) + 2 * (i // 2), (i // 2) * (2 * i - 3) + 2 * (1 - i // 2)))
    for s1, s2 in both:
        complete(s2[2])
    shard(2, 2)
    for s in range(2):
        out = acc[s] / total[s]
        lse_out[s] = peak[s] + jnp.log2(total[s])
        for h in range(2):
            part = out[:, h * ROWS : (h + 1) * ROWS]
            o_out[s, h * HEAD : (h + 1) * HEAD] = part
            mine[s, h * HEAD : (h + 1) * HEAD] = part.astype(BF16)

    group = me_t * 2 + zl
    att[group] = mine[zl]
    sends = [
        remote(mine.at[1 - zl], att.at[group], o_send.at[0], o_recv.at[0], partner),
        remote(mine.at[1 - zl], att.at[group], o_send.at[1], o_recv.at[1], far_partner),
        remote(mine.at[zl], att.at[group], o_send.at[2], o_recv.at[2], far),
    ]
    for cp in sends:
        cp.start()
    there_t = (1 - zh) * 2 + c
    wo_far = wo_full.at[there_t]
    remote(wo_far, wo_far, w_send.at[0], w_recv.at[0], far).wait_recv()
    wo_relay = remote(wo_far, wo_far, w_send.at[2], w_recv.at[2], core)
    wo_relay.start()
    order = [
        (None, group), (0, me_t * 2 + 1 - zl), (1, there_t * 2 + 1 - zl), (2, there_t * 2 + zl),
    ]
    relays = []
    for n, (sem, which) in enumerate(order):
        if sem is not None:
            remote(att.at[which], att.at[which], o_send.at[sem], o_recv.at[sem], far).wait_recv()
        cp = remote(att.at[which], att.at[which], o_send.at[3 + n], o_recv.at[3 + n], core)
        cp.start()
        relays.append(cp)
    mine_t, other_t = zh * 2 + (1 - c), (1 - zh) * 2 + (1 - c)
    for n, which in enumerate([mine_t * 2 + zl, mine_t * 2 + 1 - zl, other_t * 2 + 1 - zl, other_t * 2 + zl]):
        remote(att.at[which], att.at[which], o_send.at[3 + n], o_recv.at[3 + n], core).wait_recv()
    w1, w2 = wo_full.at[mine_t], wo_full.at[other_t]
    remote(w1, w1, w_send.at[1], w_recv.at[1], core).wait_recv()
    remote(w2, w2, w_send.at[2], w_recv.at[2], core).wait_recv()
    pair_cp.wait_send()
    for s1, s2 in both:
        for st in [s1, *s2]:
            for name in ("right", "left", "on_right", "on_left"):
                st[name].wait_send()
    for cp in [*wo_cps, wo_relay, *sends, *relays]:
        cp.wait_send()


def front(lengths, freq, tokens, gain, wq, wkt, wvt, wo):
    vm = pl.BlockSpec(memory_space=pltpu.VMEM)
    anywhere = pl.BlockSpec(memory_space=pl.ANY)
    dma = pltpu.SemaphoreType.DMA
    return pl.pallas_call(
        front_kernel,
        out_shape=(
            jax.ShapeDtypeStruct((ROWS, WIDTH), BF16),
            jax.ShapeDtypeStruct((2, 4 * HEAD, ROWS), BF16),
            jax.ShapeDtypeStruct((4, 4, 2, 2 * HEAD, ROWS), BF16),
            jax.ShapeDtypeStruct((8, 2 * HEAD, ROWS), BF16),
            jax.ShapeDtypeStruct((2, 2 * HEAD, ROWS), F32),
            jax.ShapeDtypeStruct((2, 1, 2 * ROWS), F32),
            jax.ShapeDtypeStruct((4, HEADS_LOCAL, WIDTH), BF16),
        ),
        in_specs=[pl.BlockSpec(memory_space=pltpu.SMEM), vm, vm, vm, vm, vm, vm, anywhere],
        out_specs=(vm, vm, vm, vm, vm, vm, anywhere),
        scratch_shapes=[
            pltpu.VMEM((2, 4 * HEAD, ROWS), BF16),
            pltpu.VMEM((2, HEAD + SEG, 2 * ROWS), BF16),
            pltpu.VMEM((2, HEAD, 2 * ROWS), F32),
            pltpu.VMEM((2, 1, 2 * ROWS), F32),
            pltpu.VMEM((2, 1, 2 * ROWS), F32),
            pltpu.VMEM((2, 2 * HEAD, ROWS), BF16),
            dma((2,)),
            dma((2, 20)),
            dma((2, 20)),
            dma((7,)),
            dma((7,)),
            dma((3,)),
            dma((3,)),
        ],
        compiler_params=pltpu.CompilerParams(
            collective_id=0, has_side_effects=True, vmem_limit_bytes=VMEM_LIMIT
        ),
        name="front",
    )(lengths, freq, tokens, gain, wq, wkt, wvt, wo)


W_FFN = 3 * FFL
W_MID = W_FFN + HEADS_LOCAL
FF_CHUNKS = 4
FF_CHUNK = FFL // FF_CHUNKS


def norm_back(source, inverse, gain, grad):
    scaled = grad * gain
    gain_grad = jnp.sum(grad * source * inverse, 0, keepdims=True)
    mean = jnp.mean(scaled * source, -1, keepdims=True)
    return inverse * scaled - source * (inverse * inverse * inverse) * mean, gain_grad


def cut(lo, width, sizes, order):
    pieces, end, n = [], lo + width, 0
    while lo < end:
        w = min(sizes[n % len(sizes)] * 128, end - lo)
        pieces.append((order[n % len(order)], lo, w))
        lo += w
        n += 1
    return pieces


DOWN_PIECES = cut(2 * FFL, FFL, (4, 4), "xy")
GATE_PIECES = cut(0, FFL, (4, 4), "xy")
UP_PIECES = cut(FFL, FFL, (4, 4), "xy")
OUT_PIECES = cut(W_FFN, HEADS_LOCAL, (1, 2), "xy")
MID_PIECES = DOWN_PIECES + GATE_PIECES + UP_PIECES + OUT_PIECES


def middle_kernel(
    lengths, tokens, cot, att, wo_full, wo_own, gain1, wg, wu, wd, qkv, kv_hbm, o_in, lse,
    mixed_out, feed_out, mixed_grad_out, gain_grad_out, dqkv, sums,
    wo_buf, gu_buf, d_buf, mixed, back, feed, normed, hidden, gate_grad, upper_grad, left, grads,
    part3, tot3, buf3, s3, r3, part2, buf2, s2, r2,
    kv, qaug, dot_t, delta, dq, dgrp, dout, mine,
    kb1, kr1, kb2, kr2, ksend, krecv,
    b1, r1, b2, r2_, zb, gsend, grecv, pair_sem, load_sem, ff_sem, wo_sem,
):
    place = Place()
    zl, x, y = place.zl, place.x, place.y
    partner = place.at(**place.pair)
    peers = [partner, place.at(zl=1 - zl), place.at(zh=1 - place.zh), place.at(c=1 - place.c)]
    peers += [place.along(a, s) for a in ("x", "y") for s in (1, -1)]
    call(peers)
    me_t = place.zh * 2 + place.c

    def load_wo(t, slot, own=False):
        if own:
            pltpu.make_async_copy(wo_own, wo_buf.at[slot], wo_sem.at[slot]).start()
            return

        @pl.when(me_t == t)
        def _():
            pltpu.make_async_copy(wo_own, wo_buf.at[slot], wo_sem.at[slot]).start()

        @pl.when(me_t != t)
        def _():
            pltpu.make_async_copy(wo_full.at[t], wo_buf.at[slot], wo_sem.at[slot]).start()

    def wo_ready(slot):
        pltpu.make_async_copy(wo_own, wo_buf.at[slot], wo_sem.at[slot]).wait()

    def ff_loads(k):
        slot, cols = k % 2, pl.ds(k * FF_CHUNK, FF_CHUNK)
        return [
            pltpu.make_async_copy(wg.at[:, cols], gu_buf.at[slot, :, pl.ds(0, FF_CHUNK)], ff_sem.at[slot, 0]),
            pltpu.make_async_copy(wu.at[:, cols], gu_buf.at[slot, :, pl.ds(FF_CHUNK, FF_CHUNK)], ff_sem.at[slot, 1]),
            pltpu.make_async_copy(wd.at[cols], d_buf.at[slot], ff_sem.at[slot, 2]),
        ]

    load_wo(0, 0)
    load_wo(1, 1)
    for k in range(2):
        for cp in ff_loads(k):
            cp.start()
    kv_load = pltpu.make_async_copy(kv_hbm, kv, load_sem.at[0])
    kv_load.start()

    mixed[...] = tokens[...].astype(F32)
    for t in range(4):
        wo_ready(t % 2)
        heads = att[2 * t : 2 * t + 2].reshape(HEADS_LOCAL, ROWS)
        mixed[...] = mixed[...] + dot(heads, wo_buf[t % 2], 0, 0)
        if t < 2:
            load_wo(t + 2, t % 2)
        elif t == 2:
            load_wo(0, 0, own=True)
    gain = gain1[...].reshape(1, WIDTH)
    inverse = lax.rsqrt(jnp.mean(mixed[...] * mixed[...], -1, keepdims=True) + EPS)
    normed[...] = (mixed[...] * inverse * gain).astype(BF16)
    mixed_save = pltpu.make_async_copy(mixed, mixed_out, load_sem.at[1])
    mixed_save.start()

    for k in range(FF_CHUNKS):
        slot, cols = k % 2, slice(k * FF_CHUNK, (k + 1) * FF_CHUNK)
        for cp in ff_loads(k):
            cp.wait()
        both = dot(normed[...], gu_buf[slot])
        gate, upper = both[:, :FF_CHUNK], both[:, FF_CHUNK:]
        hidden_grad = dot(cot[...], d_buf[slot], 1, 1)
        sig = jax.nn.sigmoid(gate)
        silu = gate * sig
        hid = (silu * upper).astype(BF16)
        gg = (hidden_grad * upper * sig * (1.0 + gate * (1.0 - sig))).astype(BF16)
        ug = (hidden_grad * silu).astype(BF16)
        hidden[:, cols], gate_grad[:, cols], upper_grad[:, cols] = hid, gg, ug
        add_back = dot(jnp.concatenate([gg, ug], 1), gu_buf[slot], 1, 1)
        add_feed = dot(hid, d_buf[slot])
        if k == 0:
            back[...], feed[...] = add_back, add_feed
        else:
            back[...] = back[...] + add_back
            feed[...] = feed[...] + add_feed
        if k + 2 < FF_CHUNKS:
            for cp in ff_loads(k + 2):
                cp.start()
    part3[...] = ar_view(back[...].astype(BF16))
    answer(peers)
    sum3 = TpSum(place, part3, tot3, buf3, (s3, r3))
    sum3.start()
    part2[...] = ar_view(feed[...].astype(BF16))

    def weight_grad(lhs, rhs, lo, cb=0):
        left[...] = lhs.T
        w = rhs.shape[1 - cb]

        def rows(i, carry):
            piece = dot(left[pl.ds(pl.multiple_of(i * 192, 192), 192)], rhs[...], 1, cb)
            grads[i // 4, i % 4, :, :, lo : lo + w] = piece.astype(BF16).reshape(4, 48, w)
            return carry

        lax.fori_loop(0, 8, rows, 0)

    pieces = [
        GradSum(place, first, lo, w, grads, (b1, r1, b2, r2_, zb), (gsend, grecv), n)
        for n, (first, lo, w) in enumerate(MID_PIECES)
    ]
    n_down, n_gate, n_up = len(DOWN_PIECES), len(GATE_PIECES), len(UP_PIECES)
    ready = 0

    def start_pieces(count):
        nonlocal ready
        for piece in pieces[ready : ready + count]:
            piece.one.start()
        ready += count

    sum3.mid()
    weight_grad(cot[...], hidden, 2 * FFL)
    start_pieces(n_down)
    weight_grad(normed[...], gate_grad, 0)
    start_pieces(n_gate)
    weight_grad(normed[...], upper_grad, FFL)
    start_pieces(n_up)
    sum2 = TpSum(place, part2, feed_out, buf2, (s2, r2))
    sum2.start()
    ends = ends_of(lengths)
    low = place.low_block(x, y)
    for s in range(2):
        segs = query_segments(ends, jnp.where(s == 0, low, 31 - low) * ROWS)
        for h in range(2):
            lanes = slice(h * ROWS, (h + 1) * ROWS)
            qaug[s, :HEAD, lanes] = qkv[s, h * HEAD : (h + 1) * HEAD]
            qaug[s, HEAD:, lanes] = segs
    dq[...] = jnp.zeros(dq.shape, F32)
    sum3.fin()
    sum3.landed()
    mixed_part, gain_grad = norm_back(mixed[...], inverse, gain, ar_load(tot3).astype(F32))
    gain_grad_out[...] = gain_grad
    back[...] = cot[...].astype(F32) + mixed_part
    mixed_grad_save = pltpu.make_async_copy(back, mixed_grad_out, load_sem.at[2])
    mixed_grad_save.start()
    branch = back[...].astype(BF16)
    wo_ready(0)
    own = dot(wo_buf[0], branch, 1, 1).astype(BF16)
    dgrp[0] = own[: 2 * HEAD]
    dgrp[1] = own[2 * HEAD :]
    pair_cp = remote(dgrp.at[1 - zl], dout.at[zl], pair_sem.at[0], pair_sem.at[1], partner)
    pair_cp.start()
    dout[zl] = dgrp[zl]
    normed[...] = branch
    weight_grad(normed[...], att.at[pl.ds(me_t * 2, 2)][...].reshape(HEADS_LOCAL, ROWS), W_FFN, 1)
    start_pieces(len(OUT_PIECES))
    sum2.mid()
    kv_load.wait()
    for piece in pieces[:2]:
        piece.one.mid()
    pair_cp.wait_recv()
    for s in range(2):
        for h in range(2):
            lanes, feats = slice(h * ROWS, (h + 1) * ROWS), slice(h * HEAD, (h + 1) * HEAD)
            d = dout[s, feats]
            dot_t[s, :, lanes] = d
            delta[s, :, lanes] = jnp.sum(d.astype(F32) * o_in[s, feats], 0, keepdims=True)

    def unit(qs, kx, ky, ks, kbase, causal):
        pair = kv[kx, ky, ks]
        q = qaug[qs]
        do = dot_t[qs]
        ka = jnp.concatenate([pair[:HEAD], key_segments(ends, kbase)], 0)
        s = dot(ka, q, 0, 0)
        p = jnp.exp2(s - lse[qs])
        if causal:
            key = lax.broadcasted_iota(jnp.int32, (ROWS, 2 * ROWS), 0)
            query = lax.broadcasted_iota(jnp.int32, (ROWS, 2 * ROWS), 1)
            p = jnp.where(key <= jnp.where(query >= ROWS, query - ROWS, query), p, 0.0)
        dp = dot(pair[HEAD:], do, 0, 0)
        ds = (p * (dp - delta[qs])).astype(BF16)
        dq[qs] = dq[qs] + dot(pair[:HEAD], ds)
        dk = dot(q[:HEAD], ds, 1, 1)
        dv = dot(do, p.astype(BF16), 1, 1)
        return jnp.concatenate([dk, dv], 0)

    first = unit(0, x, y, 0, low * ROWS, True) + unit(1, x, y, 0, low * ROWS, False)
    kv[x, y, 0] = first.astype(BF16)
    kv[x, y, 1] = unit(1, x, y, 1, (31 - low) * ROWS, True).astype(BF16)

    def step(i, carry):
        kx, ky = lax.rem(x + i // 4, 4), lax.rem(y + i % 4, 4)
        there = place.low_block(kx, ky)
        one = unit(1, kx, ky, 0, there * ROWS, False)
        before = there < low
        sel = jnp.where(before, 0, 1)
        two = unit(sel, kx, ky, sel, jnp.where(before, there, 31 - there) * ROWS, False)
        share = jnp.where(before, 1.0, 0.0)
        kv[kx, ky, 0] = (one + two * share).astype(BF16)
        kv[kx, ky, 1] = (two * (1.0 - share)).astype(BF16)
        return carry

    def fin(group):
        for piece in group:
            piece.one.fin()
            piece.two.start()

    lax.fori_loop(1, 4, step, 0)
    for piece in pieces[2:4]:
        piece.one.mid()
    lax.fori_loop(4, 7, step, 0)
    for piece in pieces[4:]:
        piece.one.mid()
    lax.fori_loop(7, 10, step, 0)
    fin(pieces[:2])
    lax.fori_loop(10, 13, step, 0)
    fin(pieces[2:4])
    lax.fori_loop(13, 16, step, 0)

    def key_sum(slot, axis):
        other = "y" if axis == "x" else "x"
        if axis == "x":
            half = lambda d, h: kv.at[d, :, slot, pl.ds(h * HEAD, HEAD)]
        else:
            half = lambda d, h: kv.at[:, d, slot, pl.ds(h * HEAD, HEAD)]
        one = RingSum(
            place, axis, half, lambda k: kb1.at[slot, k], lambda h: kr1.at[slot, h],
            lambda k: ksend.at[slot, k], lambda k: krecv.at[slot, k], add2_lead, add3_lead,
        )
        two = RingSum(
            place, other, lambda d, h: kr1.at[slot, h, d], lambda k: kb2.at[slot, k],
            lambda h: kr2.at[slot, h], lambda k: ksend.at[slot, 6 + k], lambda k: krecv.at[slot, 6 + k],
            add2_flat, add3_flat,
        )
        return one, two

    ka, kb = key_sum(0, "x"), key_sum(1, "y")
    ka[0].start()
    kb[0].start()
    fin(pieces[4:])
    sum2.fin()
    ka[0].mid()
    kb[0].mid()
    for piece in pieces:
        piece.two.mid()
    ka[0].fin()
    kb[0].fin()
    ka[1].start()
    kb[1].start()
    for piece in pieces:
        piece.two.fin()
        piece.zcp().start()
    ka[1].mid()
    kb[1].mid()
    ka[1].fin()
    kb[1].fin()
    for s in range(2):
        for h in range(2):
            mine[s, h * HEAD : (h + 1) * HEAD] = (dq[s, :, h * ROWS : (h + 1) * ROWS] * SCALE).astype(BF16)
            mine[s, (2 + h) * HEAD : (3 + h) * HEAD] = kr2[s, h]
    back_cp = remote(mine.at[1 - zl], dqkv.at[zl], pair_sem.at[2], pair_sem.at[3], partner)
    back_cp.start()
    dqkv[zl] = mine[zl]
    for piece, (_, lo, w) in zip(pieces, MID_PIECES):
        sums[:, lo : lo + w] = piece.total()
    landing = dqkv.at[1 - zl]
    remote(landing, landing, pair_sem.at[2], pair_sem.at[3], partner).wait_recv()
    sum2.landed()
    mixed_save.wait()
    mixed_grad_save.wait()
    pair_cp.wait_send()
    back_cp.wait_send()
    sum3.end()
    sum2.end()
    for piece in pieces:
        piece.end()
    for one, two in (ka, kb):
        one.end()
        two.end()


def middle(lengths, tokens, cot, att, wo_full, wo_own, gain, wg, wu, wd, qkv, kvall, o, lse):
    vm = pl.BlockSpec(memory_space=pltpu.VMEM)
    hbm = pl.BlockSpec(memory_space=pl.ANY)
    dma = pltpu.SemaphoreType.DMA
    shape = (2, AR_PIECES, AR_ROWS, WIDTH)
    wide = pltpu.VMEM((ROWS, WIDTH), F32)
    return pl.pallas_call(
        middle_kernel,
        out_shape=(
            jax.ShapeDtypeStruct((ROWS, WIDTH), F32),
            jax.ShapeDtypeStruct(shape, BF16),
            jax.ShapeDtypeStruct((ROWS, WIDTH), F32),
            jax.ShapeDtypeStruct((1, WIDTH), F32),
            jax.ShapeDtypeStruct((2, 4 * HEAD, ROWS), BF16),
            jax.ShapeDtypeStruct((48, W_MID), F32),
        ),
        in_specs=[pl.BlockSpec(memory_space=pltpu.SMEM), vm, vm, vm, hbm, hbm, vm, hbm, hbm, hbm, vm, hbm, vm, vm],
        out_specs=(hbm, vm, hbm, vm, vm, vm),
        scratch_shapes=[
            pltpu.VMEM((2, HEADS_LOCAL, WIDTH), BF16),
            pltpu.VMEM((2, WIDTH, 2 * FF_CHUNK), BF16),
            pltpu.VMEM((2, FF_CHUNK, WIDTH), BF16),
            wide,
            wide,
            wide,
            pltpu.VMEM((ROWS, WIDTH), BF16),
            pltpu.VMEM((ROWS, FFL), BF16),
            pltpu.VMEM((ROWS, FFL), BF16),
            pltpu.VMEM((ROWS, FFL), BF16),
            pltpu.VMEM((WIDTH, ROWS), BF16),
            pltpu.VMEM((2, 4, 4, 48, W_MID), BF16),
            pltpu.VMEM(shape, BF16),
            pltpu.VMEM(shape, BF16),
            *tp_scratch(),
            pltpu.VMEM(shape, BF16),
            *tp_scratch(),
            pltpu.VMEM((4, 4, 2, 2 * HEAD, ROWS), BF16),
            pltpu.VMEM((2, HEAD + SEG, 2 * ROWS), BF16),
            pltpu.VMEM((2, HEAD, 2 * ROWS), BF16),
            pltpu.VMEM((2, 1, 2 * ROWS), F32),
            pltpu.VMEM((2, HEAD, 2 * ROWS), F32),
            pltpu.VMEM((2, 2 * HEAD, ROWS), BF16),
            pltpu.VMEM((2, 2 * HEAD, ROWS), BF16),
            pltpu.VMEM((2, 4 * HEAD, ROWS), BF16),
            pltpu.VMEM((2, 6, 4, HEAD, ROWS), BF16),
            pltpu.VMEM((2, 2, 4, HEAD, ROWS), BF16),
            pltpu.VMEM((2, 6, HEAD, ROWS), BF16),
            pltpu.VMEM((2, 2, HEAD, ROWS), BF16),
            dma((2, 12)),
            dma((2, 12)),
            *grad_scratch(W_MID, len(MID_PIECES)),
            dma((4,)),
            dma((3,)),
            dma((2, 3)),
            dma((2,)),
        ],
        compiler_params=pltpu.CompilerParams(
            collective_id=1, has_side_effects=True, vmem_limit_bytes=VMEM_LIMIT
        ),
        name="middle",
    )(lengths, tokens, cot, att, wo_full, wo_own, gain, wg, wu, wd, qkv, kvall, o, lse)


W_TAIL = HEADS_LOCAL + 2 * PAIRS_LOCAL
TAIL_PIECES = cut(0, W_TAIL, (1, 1, 2, 2), "xy")
GAIN_ROWS = 2 * WIDTH // 128


def tail_kernel(
    lengths, freq, tokens, gain, normed, dqkv, wq, wkt, wvt, mixed_grad, ffn_gain_grad,
    tokens_grad, sums, gains,
    rows, left, grads, part, total, buf, s4, r4,
    b1, r1, b2, r2, zb, gsend, grecv, gain_buf, gain_sum, gn_send, gn_recv,
):
    place = Place()
    zl, x, y = place.zl, place.x, place.y
    others = [place.along(a, s) for a in ("x", "y") for s in (1, 2, 3)]
    peers = others + [place.at(zl=1 - zl), place.at(zh=1 - place.zh), place.at(c=1 - place.c)]
    call(peers)
    answer(peers)
    ends = ends_of(lengths)
    block = zl * 16 + x * 4 + y
    cosine, sine = rotation(ends, lengths, block * ROWS, freq[...])
    for g in range(2):
        for h in range(3):
            a = dqkv[g, h * HEAD : h * HEAD + HALF].astype(F32)
            b = dqkv[g, h * HEAD + HALF : (h + 1) * HEAD].astype(F32)
            if h == 2:
                a, b = a * LN2, b * LN2
            at = (2 * g + h) * HEAD if h < 2 else HEADS_LOCAL + g * HEAD
            rows[at : at + HALF] = (a * cosine + b * sine).astype(BF16)
            rows[at + HALF : at + HEAD] = (b * cosine - a * sine).astype(BF16)
        at = HEADS_LOCAL + PAIRS_LOCAL + g * HEAD
        rows[at : at + HEAD] = dqkv[g, 3 * HEAD :]
    back = dot(rows[:HEADS_LOCAL], wq[...], 0, 1)
    back = back + dot(rows[HEADS_LOCAL : HEADS_LOCAL + PAIRS_LOCAL], wkt[...], 0, 0)
    back = back + dot(rows[HEADS_LOCAL + PAIRS_LOCAL :], wvt[...], 0, 0)
    part[...] = ar_view(back.astype(BF16))
    sum4 = TpSum(place, part, total, buf, (s4, r4))
    sum4.start()
    left[...] = normed[...].T

    def weight_rows(i, carry):
        piece = dot(left[pl.ds(pl.multiple_of(i * 192, 192), 192)], rows[...], 1, 1)
        grads[i // 4, i % 4] = piece.astype(BF16).reshape(4, 48, W_TAIL)
        return carry

    lax.fori_loop(0, 8, weight_rows, 0)
    pieces = [
        GradSum(place, first, lo, w, grads, (b1, r1, b2, r2, zb), (gsend, grecv), n)
        for n, (first, lo, w) in enumerate(TAIL_PIECES)
    ]
    for piece in pieces:
        piece.one.start()
    sum4.mid()
    for piece in pieces:
        piece.one.mid()
    sum4.fin()
    sum4.landed()
    source = tokens[...].astype(F32)
    inverse = lax.rsqrt(jnp.mean(source * source, -1, keepdims=True) + EPS)
    grad = ar_load(total).astype(F32)
    source_part, gain_grad = norm_back(source, inverse, gain[...].reshape(1, WIDTH), grad)
    tokens_grad[...] = (mixed_grad[...] + source_part).astype(BF16)
    gain_sum[0, 0:1] = gain_grad
    gain_sum[0, 1:2] = ffn_gain_grad[...]

    def gain_copies(stage, axis):
        if axis == "zl":
            peers = [place.at(zl=1 - zl)]
        else:
            peers = [place.along(axis, s) for s in (1, 2, 3)]
        return [
            remote(gain_sum.at[stage], gain_buf.at[stage, k], gn_send.at[stage, k], gn_recv.at[stage, k], peer)
            for k, peer in enumerate(peers)
        ]

    sent = gain_copies(0, "x")
    for cp in sent:
        cp.start()
    for piece in pieces:
        piece.one.fin()
        piece.two.start()
    for cp in sent:
        cp.wait_recv()
    gain_sum[1] = gain_sum[0] + gain_buf[0, 0] + gain_buf[0, 1] + gain_buf[0, 2]
    sent_y = gain_copies(1, "y")
    for cp in sent_y:
        cp.start()
    for piece in pieces:
        piece.two.mid()
    for cp in sent_y:
        cp.wait_recv()
    gain_sum[2] = gain_sum[1] + gain_buf[1, 0] + gain_buf[1, 1] + gain_buf[1, 2]
    sent_z = gain_copies(2, "zl")
    for cp in sent_z:
        cp.start()
    for piece in pieces:
        piece.two.fin()
        piece.zcp().start()
    for cp in sent_z:
        cp.wait_recv()
    gains[...] = gain_sum[2] + gain_buf[2, 0]
    for piece, (_, lo, w) in zip(pieces, TAIL_PIECES):
        sums[:, lo : lo + w] = piece.total()
    for cp in [*sent, *sent_y, *sent_z]:
        cp.wait_send()
    for piece in pieces:
        piece.end()
    sum4.end()


def tail(lengths, freq, tokens, gain, normed, dqkv, wq, wkt, wvt, mixed_grad, ffn_gain_grad):
    vm = pl.BlockSpec(memory_space=pltpu.VMEM)
    dma = pltpu.SemaphoreType.DMA
    shape = (2, AR_PIECES, AR_ROWS, WIDTH)
    return pl.pallas_call(
        tail_kernel,
        out_shape=(
            jax.ShapeDtypeStruct((ROWS, WIDTH), BF16),
            jax.ShapeDtypeStruct((48, W_TAIL), F32),
            jax.ShapeDtypeStruct((2, WIDTH), F32),
        ),
        in_specs=[pl.BlockSpec(memory_space=pltpu.SMEM)] + [vm] * 10,
        out_specs=(vm,) * 3,
        scratch_shapes=[
            pltpu.VMEM((W_TAIL, ROWS), BF16),
            pltpu.VMEM((WIDTH, ROWS), BF16),
            pltpu.VMEM((2, 4, 4, 48, W_TAIL), BF16),
            pltpu.VMEM(shape, BF16),
            pltpu.VMEM(shape, BF16),
            *tp_scratch(),
            *grad_scratch(W_TAIL, len(TAIL_PIECES)),
            pltpu.VMEM((3, 3, 2, WIDTH), F32),
            pltpu.VMEM((3, 2, WIDTH), F32),
            dma((3, 3)),
            dma((3, 3)),
        ],
        compiler_params=pltpu.CompilerParams(
            collective_id=2, has_side_effects=True, vmem_limit_bytes=VMEM_LIMIT
        ),
        name="tail",
    )(lengths, freq, tokens, gain, normed, dqkv, wq, wkt, wvt, mixed_grad, ffn_gain_grad)


def local(
    tokens, norm_gain, query_weight, key_matrix, value_matrix, out_weight,
    ffn_gain, gate_weight, up_weight, down_weight, cotangent, lengths,
):
    freq = jnp.asarray(
        (THETA ** (-2.0 * np.arange(HALF) / HEAD)).astype(np.float32).reshape(HALF, 1)
    )
    key_t, value_t = key_matrix.T, value_matrix.T
    normed, qkv, kvall, att, o, lse, wo_full = front(
        lengths, freq, tokens, norm_gain, query_weight, key_t, value_t, out_weight
    )
    mixed, feed, mixed_grad, ffn_gain_grad, dqkv, mid_sums = middle(
        lengths, tokens, cotangent, att, wo_full, out_weight, ffn_gain, gate_weight, up_weight, down_weight,
        qkv, kvall, o, lse,
    )
    result = (mixed + feed.reshape(ROWS, WIDTH).astype(F32)).astype(BF16)
    tokens_grad, sums, gains = tail(
        lengths, freq, tokens, norm_gain, normed, dqkv, query_weight, key_t, value_t,
        mixed_grad, ffn_gain_grad,
    )
    block = (lax.axis_index("zl") * 4 + lax.axis_index("x")) * 4 + lax.axis_index("y")
    own = lax.dynamic_slice(gains, (0, block * 48), (2, 48))
    return (
        result,
        tokens_grad,
        own[0],
        sums[:, :HEADS_LOCAL],
        sums[:, HEADS_LOCAL : HEADS_LOCAL + PAIRS_LOCAL],
        sums[:, HEADS_LOCAL + PAIRS_LOCAL :],
        mid_sums[:, W_FFN:].T,
        own[1],
        mid_sums[:, :FFL],
        mid_sums[:, FFL : 2 * FFL],
        mid_sums[:, 2 * FFL : W_FFN].T,
    )


def solution(mesh):
    split = Mesh(mesh.devices.reshape(2, 4, 4, 2, 2), AXES)
    in_specs = (
        P(BLK, None),
        P(),
        P(None, TP),
        P(None, TP),
        P(None, TP),
        P(TP, None),
        P(),
        P(None, TP),
        P(None, TP),
        P(TP, None),
        P(BLK, None),
        P(),
    )
    out_specs = (
        P(BLK, None),
        P(BLK, None),
        P(BLK),
        P(BLK, TP),
        P(BLK, TP),
        P(BLK, TP),
        P(TP, BLK),
        P(BLK),
        P(BLK, TP),
        P(BLK, TP),
        P(TP, BLK),
    )
    return jax.shard_map(local, mesh=split, in_specs=in_specs, out_specs=out_specs, check_vma=False)
```

```python
import jax
import jax.numpy as jnp
import numpy as np
from jax import lax
from jax.experimental import pallas as pl
from jax.experimental.pallas import tpu as pltpu
from jax.sharding import Mesh
from jax.sharding import PartitionSpec as P

AXES = ("zl", "x", "y", "zh", "c")
BLK = ("zl", "x", "y")
TP = ("zh", "c")
HEAD = 96
HALF = HEAD // 2
ROWS = 256
WIDTH = 1536
HEADS_LOCAL = 384
PAIRS_LOCAL = 192
FFL = 1024
EPS = 1e-05
THETA = 100000.0
SCALE = HEAD**-0.5
LOG2E = float(np.log2(np.e))
LN2 = float(np.log(2.0))
BIG = 1e30
SEG = 16
MESH = pl.DeviceIdType.MESH
F32 = jnp.float32
BF16 = jnp.bfloat16
VMEM_LIMIT = 63 * 2**20


def dot(a, b, ca=1, cb=0):
    return lax.dot_general(a, b, (((ca,), (cb,)), ((), ())), preferred_element_type=F32)


class Place:
    def __init__(self):
        self.zl, self.x, self.y, self.zh, self.c = (lax.axis_index(a) for a in AXES)

    def at(self, **changes):
        own = dict(zl=self.zl, x=self.x, y=self.y, zh=self.zh, c=self.c)
        own.update(changes)
        return tuple(own[a] for a in AXES)

    def along(self, axis, step):
        return self.at(**{axis: lax.rem(getattr(self, axis) + (step + 4), 4)})

    @property
    def pair(self):
        return dict(zl=1 - self.zl, x=3 - self.x, y=3 - self.y)

    def low_block(self, x, y):
        p = x * 4 + y
        return jnp.where(self.zl == 0, p, 15 - p)


def call(peers):
    barrier = pltpu.get_barrier_semaphore()
    for peer in peers:
        pl.semaphore_signal(barrier, inc=1, device_id=peer, device_id_type=MESH)


def answer(peers):
    pl.semaphore_wait(pltpu.get_barrier_semaphore(), len(peers))


def remote(src, dst, send, recv, device):
    return pltpu.make_async_remote_copy(
        src_ref=src, dst_ref=dst, send_sem=send, recv_sem=recv, device_id=device, device_id_type=MESH
    )


def seg_rows(ends, base):
    token = base + lax.broadcasted_iota(jnp.int32, (SEG, ROWS), 1)
    row = lax.broadcasted_iota(jnp.int32, (SEG, ROWS), 0)
    inside = jnp.zeros((SEG, ROWS), F32)
    start = 0
    for d in range(5):
        hit = (row == d) & (token >= start) & (token < ends[d])
        inside = jnp.where(hit, 1.0, inside)
        start = ends[d]
    return inside, row


def key_segments(ends, base):
    return seg_rows(ends, base)[0].astype(BF16)


def query_segments(ends, base):
    inside, row = seg_rows(ends, base)
    return jnp.where(row < 5, (inside - 1.0) * BIG, 0.0).astype(BF16)


def ends_of(lengths_ref):
    ends, total = [], 0
    for d in range(5):
        total = total + lengths_ref[d]
        ends.append(total)
    return ends


def rotation(ends, lengths_ref, base, freq):
    token = base + lax.broadcasted_iota(jnp.int32, (1, ROWS), 1)
    begin = jnp.zeros((1, ROWS), jnp.int32)
    for d in range(5):
        begin = begin + jnp.where(token >= ends[d], lengths_ref[d], 0)
    angle = (token - begin).astype(F32) * freq
    return jnp.cos(angle), jnp.sin(angle)


class RingSum:
    def __init__(self, place, axis, half, bufs, out, send, recv):
        self.half, self.bufs, self.out = half, bufs, out
        me = getattr(place, axis)
        self.me = me
        self.r, self.l, self.o = (lax.rem(me + k, 4) for k in (1, 3, 2))
        self.right, self.left = place.along(axis, 1), place.along(axis, -1)
        self.send, self.recv = send, recv
        self.ended = False

    def cp(self, k):
        src = (
            lambda: self.half(self.o, 0),
            lambda: self.half(self.o, 1),
            lambda: self.half(self.r, 1),
            lambda: self.half(self.l, 0),
            lambda: self.bufs(0),
            lambda: self.bufs(1),
        )[k]()
        return remote(src, self.bufs(k), self.send(k), self.recv(k), (self.right, self.left)[k % 2])

    def start(self):
        for k in range(4):
            self.cp(k).start()

    def mid(self):
        self.cp(0).wait_recv()
        add_two(self.bufs(0), self.half(self.r, 0))
        self.cp(4).start()
        self.cp(1).wait_recv()
        add_two(self.bufs(1), self.half(self.l, 1))
        self.cp(5).start()

    def fin(self):
        self.cp(4).wait_recv()
        self.cp(3).wait_recv()
        add_three(self.out(0), self.half(self.me, 0), self.bufs(4), self.bufs(3))
        self.cp(5).wait_recv()
        self.cp(2).wait_recv()
        add_three(self.out(1), self.half(self.me, 1), self.bufs(5), self.bufs(2))

    def end(self):
        if not self.ended:
            self.ended = True
            for k in range(6):
                self.cp(k).wait_send()


def add_two(dst, src):
    if len(dst.shape) == 3:
        for i in range(dst.shape[0]):
            dst[i] = dst[i] + src[i]
    else:
        dst[...] = dst[...] + src[...]


def add_three(out, a, b, d):
    if len(out.shape) == 3:
        for i in range(out.shape[0]):
            out[i] = (a[i].astype(F32) + b[i].astype(F32) + d[i].astype(F32)).astype(out.dtype)
    else:
        out[...] = (a[...].astype(F32) + b[...].astype(F32) + d[...].astype(F32)).astype(out.dtype)


class Steps:
    at = 0

    def next(self):
        self.steps[self.at]()
        self.at += 1


class PlaneSum(Steps):
    def __init__(self, place, first, g, glo, blo, slo, w, bufs, sems, n, sums):
        b1, r1, b2, r2, zb = bufs
        send, recv = sems
        gc, bc = pl.ds(glo, w), pl.ds(blo, w)
        self.place, self.r2, self.zb, self.bc, self.sc = place, r2, zb, bc, slice(slo, slo + w)
        self.send, self.recv, self.n, self.sums = send, recv, n, sums
        if first == "x":
            half1 = lambda d, h: g.at[h, d, :, :, gc]
        else:
            half1 = lambda d, h: g.at[h, :, d, :, gc]
        self.one = RingSum(
            place, first, half1, lambda k: b1.at[k, :, :, bc], lambda h: r1.at[h, :, :, bc],
            lambda k: send.at[n, k], lambda k: recv.at[n, k],
        )
        self.two = RingSum(
            place, "y" if first == "x" else "x", lambda d, h: r1.at[h, d, :, bc], lambda k: b2.at[k, :, bc],
            lambda h: r2.at[h, :, bc], lambda k: send.at[n, 6 + k], lambda k: recv.at[n, 6 + k],
        )
        self.steps = [self.one.start, self.one.mid, self.turn, self.two.mid, self.cross, self.total]

    def zcp(self):
        other = 1 - self.place.zl
        return remote(
            self.r2.at[other, :, self.bc], self.zb.at[:, self.bc], self.send.at[self.n, 12],
            self.recv.at[self.n, 12], self.place.at(zl=other),
        )

    def turn(self):
        self.one.fin()
        self.two.start()

    def cross(self):
        self.two.fin()
        self.zcp().start()

    def total(self):
        self.zcp().wait_recv()
        own = self.r2[self.place.zl, :, self.bc].astype(F32)
        self.sums[:, self.sc] = own + self.zb[:, self.bc].astype(F32)

    def end(self):
        self.one.end()
        self.two.end()
        self.zcp().wait_send()


class DepthSum(Steps):
    def __init__(self, place, first, g, glo, blo, slo, w, bufs, sems, n, sums):
        z0, b1, r1, b2 = bufs
        send, recv = sems
        h_w = w // 2
        self.place, self.g, self.z0 = place, g, z0
        self.gc, self.zc = pl.ds(glo, w), pl.ds(blo, w)
        self.send, self.recv, self.n = send, recv, n
        zl = place.zl
        part = lambda lo, h: pl.ds(lo + h * h_w, h_w)
        if first == "x":
            half1 = lambda d, h: g.at[zl, d, :, :, part(glo, h)]
        else:
            half1 = lambda d, h: g.at[zl, :, d, :, part(glo, h)]
        bc = pl.ds(blo // 2, h_w)
        self.one = RingSum(
            place, first, half1, lambda k: b1.at[k, :, :, bc], lambda h: r1.at[:, :, part(blo, h)],
            lambda k: send.at[n, k], lambda k: recv.at[n, k],
        )
        self.two = RingSum(
            place, "y" if first == "x" else "x", lambda d, h: r1.at[d, :, part(blo, h)], lambda k: b2.at[k, :, bc],
            lambda h: sums.at[:, part(slo, h)], lambda k: send.at[n, 6 + k], lambda k: recv.at[n, 6 + k],
        )
        self.steps = [self.cross, self.join, self.one.mid, self.turn, self.two.mid, self.two.fin]

    def zcp(self):
        other = 1 - self.place.zl
        return remote(
            self.g.at[other, :, :, :, self.gc], self.z0.at[:, :, :, self.zc], self.send.at[self.n, 12],
            self.recv.at[self.n, 12], self.place.at(zl=other),
        )

    def cross(self):
        self.zcp().start()

    def join(self):
        self.zcp().wait_recv()
        mine = self.g.at[self.place.zl, :, :, :, self.gc]
        came = self.z0.at[:, :, :, self.zc]

        def add(i, carry):
            for j in range(4):
                mine[i, j] = mine[i, j] + came[i, j]
            return carry

        lax.fori_loop(0, 4, add, 0)
        self.one.start()

    def turn(self):
        self.one.fin()
        self.two.start()

    def end(self):
        self.one.end()
        self.two.end()
        self.zcp().wait_send()


AR_PIECES = 4
AR_ROWS = ROWS // 2 // AR_PIECES


class TpSum:
    def __init__(self, place, part, buf, sems):
        self.place, self.part, self.buf = place, part, buf
        self.send, self.recv = sems
        self.core = place.at(c=1 - place.c)
        self.far = place.at(zh=1 - place.zh)

    def a(self, k):
        return remote(
            self.part.at[1 - self.place.c, k], self.buf.at[0, k], self.send.at[0, k], self.recv.at[0, k], self.core
        )

    def b(self, k):
        return remote(self.buf.at[0, k], self.buf.at[1, k], self.send.at[1, k], self.recv.at[1, k], self.far)

    def d(self, k):
        return remote(
            self.part.at[self.place.c, k], self.buf.at[2, k], self.send.at[2, k], self.recv.at[2, k], self.core
        )

    def start(self):
        for k in range(AR_PIECES):
            self.a(k).start()

    def mid(self):
        for k in range(AR_PIECES):
            self.a(k).wait_recv()
            self.buf[0, k] = self.buf[0, k] + self.part[self.place.c, k]
            self.b(k).start()

    def fin(self):
        for k in range(AR_PIECES):
            self.b(k).wait_recv()
            self.part[self.place.c, k] = self.buf[0, k] + self.buf[1, k]
            self.d(k).start()

    def landed(self):
        for k in range(AR_PIECES):
            self.a(k).wait_send()
            self.d(k).wait_recv()
            self.part[1 - self.place.c, k] = self.buf[2, k]

    def end(self):
        for k in range(AR_PIECES):
            self.b(k).wait_send()
            self.d(k).wait_send()


def tp_scratch():
    return [
        pltpu.VMEM((3, AR_PIECES, AR_ROWS, WIDTH), BF16),
        pltpu.SemaphoreType.DMA((3, AR_PIECES)),
        pltpu.SemaphoreType.DMA((3, AR_PIECES)),
    ]


def ar_view(value):
    return value.reshape(2, AR_PIECES, AR_ROWS, WIDTH)


def ar_load(ref):
    return ref[...].reshape(ROWS, WIDTH)


def norm_back(source, inverse, gain, grad):
    scaled = grad * gain
    gain_grad = jnp.sum(grad * source * inverse, 0, keepdims=True)
    mean = jnp.mean(scaled * source, -1, keepdims=True)
    return inverse * scaled - source * (inverse * inverse * inverse) * mean, gain_grad


W_FFN = 3 * FFL
W_MID = W_FFN + HEADS_LOCAL
W_TAIL = HEADS_LOCAL + 2 * PAIRS_LOCAL
W_ALL = W_MID + W_TAIL
FF_CHUNKS = 4
FF_CHUNK = FFL // FF_CHUNKS

PLAN = [
    ("down", "plane", "x", 2048, 256, 2048),
    ("down", "plane", "y", 2304, 256, 2304),
    ("down_z", "depth", "x", 2560, 256, 2560),
    ("down_z", "depth", "y", 2816, 256, 2816),
    ("gate", "plane", "x", 0, 384, 0),
    ("gate", "plane", "y", 384, 384, 384),
    ("gate_z", "depth", "x", 768, 256, 768),
    ("up", "plane", "x", 1024, 384, 1024),
    ("up", "plane", "y", 1408, 384, 1408),
    ("up_z", "depth", "y", 1792, 256, 1792),
    ("out", "plane", "x", 3072, 128, 3072),
    ("out", "plane", "y", 3200, 256, 3200),
    ("query", "plane", "x", 3456, 256, 2048),
    ("query", "plane", "y", 3712, 128, 2304),
    ("pair", "plane", "x", 3840, 128, 0),
    ("pair", "plane", "y", 3968, 256, 128),
]
W_PLANE = sum(p[4] for p in PLAN if p[1] == "plane")
W_DEPTH = sum(p[4] for p in PLAN if p[1] == "depth")


def layer_kernel(
    lengths, freq, tokens, cot, gain1, gain2, wq, wkt, wvt, wo, wg, wu, wd,
    mixed_out, normed_out, wo_full, feed_out, tokens_grad, sums, gains,
    wo_buf, gu_buf, d_buf, mixed, back, normed, hidden, gate_grad, upper_grad, left, grads,
    b1, r1, b2, r2, zb, z0, b1z, r1z, b2z, gsend, grecv,
    part3, buf3, send3, recv3, buf2, send2, recv2, buf4, send4, recv4,
    kv, kb1, kr1, kb2, kr2, ksend, krecv,
    grp, qkv, att, o, lse, qaug, acc, peak, total, mine, dgrp, dout, dot_t, delta, dqkv, rows,
    gain_sum, gain_buf, gn_send, gn_recv,
    pair_send, pair_recv, ag_send, ag_recv, o_send, o_recv, w_send, w_recv, load_sem, ff_sem, wo_sem,
):
    place = Place()
    zl, x, y, zh, c = place.zl, place.x, place.y, place.zh, place.c
    partner = place.at(**place.pair)
    far_partner = place.at(**place.pair, zh=1 - zh)
    far = place.at(zh=1 - zh)
    core = place.at(c=1 - c)
    diagonal = place.at(zl=1 - zl, zh=1 - zh)
    xr, xl, yr, yl = place.along("x", 1), place.along("x", -1), place.along("y", 1), place.along("y", -1)
    peers = [partner, far_partner, far, core, diagonal, place.at(zl=1 - zl), xr, xl, yr, yl]
    peers += [place.along("x", 2), place.along("y", 2)]
    call(peers)
    me_t = zh * 2 + c
    there_t = (1 - zh) * 2 + c
    mine_t, other_t = zh * 2 + (1 - c), (1 - zh) * 2 + (1 - c)

    def projections():
        return [
            pltpu.make_async_copy(wq, gu_buf.at[0, :, pl.ds(0, HEADS_LOCAL)], ff_sem.at[0, 0]),
            pltpu.make_async_copy(wkt, d_buf.at[0, pl.ds(0, PAIRS_LOCAL)], ff_sem.at[0, 1]),
            pltpu.make_async_copy(wvt, d_buf.at[1, pl.ds(0, PAIRS_LOCAL)], ff_sem.at[0, 2]),
        ]

    def ff_loads(k):
        slot, cols = k % 2, pl.ds(k * FF_CHUNK, FF_CHUNK)
        return [
            pltpu.make_async_copy(wg.at[:, cols], gu_buf.at[slot, :, pl.ds(0, FF_CHUNK)], ff_sem.at[slot, 0]),
            pltpu.make_async_copy(wu.at[:, cols], gu_buf.at[slot, :, pl.ds(FF_CHUNK, FF_CHUNK)], ff_sem.at[slot, 1]),
            pltpu.make_async_copy(wd.at[cols], d_buf.at[slot], ff_sem.at[slot, 2]),
        ]

    for cp in projections():
        cp.start()
    ends = ends_of(lengths)
    block = zl * 16 + x * 4 + y
    source = tokens[...].astype(F32)
    inverse = lax.rsqrt(jnp.mean(source * source, -1, keepdims=True) + EPS)
    normed[...] = (source * inverse * gain1[...].reshape(1, WIDTH)).astype(BF16)
    normed_save = pltpu.make_async_copy(normed, normed_out, load_sem.at[0])
    normed_save.start()
    cosine, sine = rotation(ends, lengths, block * ROWS, freq[...])
    answer(peers)
    wo_cps = [
        remote(wo, wo_full.at[me_t], w_send.at[0], w_recv.at[0], diagonal),
        remote(wo, wo_full.at[me_t], w_send.at[1], w_recv.at[1], core),
    ]
    for cp in wo_cps:
        cp.start()

    def turned(u, factor):
        a, b = u[:HALF], u[HALF:]
        if factor is None:
            return a * cosine - b * sine, b * cosine + a * sine
        return (a * cosine - b * sine) * factor, (b * cosine + a * sine) * factor

    for cp in projections():
        cp.wait()
    kt = dot(d_buf[0, :PAIRS_LOCAL], normed[...], 1, 1)
    vt = dot(d_buf[1, :PAIRS_LOCAL], normed[...], 1, 1)
    qt = dot(normed[...], gu_buf[0, :, :HEADS_LOCAL]).T
    for g in range(2):
        for h in range(2):
            a, b = turned(qt[(2 * g + h) * HEAD : (2 * g + h + 1) * HEAD], SCALE * LOG2E)
            grp[g, h * HEAD : h * HEAD + HALF] = a.astype(BF16)
            grp[g, h * HEAD + HALF : (h + 1) * HEAD] = b.astype(BF16)
        a, b = turned(kt[g * HEAD : (g + 1) * HEAD], None)
        grp[g, 2 * HEAD : 2 * HEAD + HALF] = a.astype(BF16)
        grp[g, 2 * HEAD + HALF : 3 * HEAD] = b.astype(BF16)
        grp[g, 3 * HEAD :] = vt[g * HEAD : (g + 1) * HEAD].astype(BF16)
    pair_cp = remote(grp.at[1 - zl], qkv.at[zl], pair_send.at[0], pair_recv.at[0], partner)
    pair_cp.start()
    for k in range(2):
        for cp in ff_loads(k):
            cp.start()
    qkv[zl] = grp[zl]
    kv[x, y, zl] = grp[zl, 2 * HEAD :]

    def gather(n, slot, swap):
        me1, me2 = (y, x) if swap else (x, y)
        r1, l1, r2, l2 = (yr, yl, xr, xl) if swap else (xr, xl, yr, yl)

        def ref(i, j, part=None):
            i, j = lax.rem(i + 4, 4), lax.rem(j + 4, 4)
            v = kv.at[j, i, slot] if swap else kv.at[i, j, slot]
            return v if part is None else v.at[pl.ds(part * HEAD, HEAD)]

        def cp(k, view, dev):
            return remote(view, view, ag_send.at[n, k], ag_recv.at[n, k], dev)

        def stage(base, i, j, di, dj, r, l):
            return dict(
                right=cp(base, ref(i, j), r),
                left=cp(base + 1, ref(i, j), l),
                from_left=cp(base, ref(i - di, j - dj), r),
                from_right=cp(base + 1, ref(i + di, j + dj), l),
                on_right=cp(base + 2, ref(i - di, j - dj, 0), r),
                on_left=cp(base + 3, ref(i + di, j + dj, 1), l),
                from_left2=cp(base + 2, ref(i + 2 * di, j + 2 * dj, 0), r),
                from_right2=cp(base + 3, ref(i + 2 * di, j + 2 * dj, 1), l),
            )

        s1 = stage(0, me1, me2, 1, 0, r1, l1)
        s2 = [stage(4 + 4 * k, me1 + k, me2, 0, 1, r2, l2) for k in range(4)]
        return s1, s2

    def begin(st):
        st["right"].start()
        st["left"].start()

    def hand_on(st):
        st["from_left"].wait_recv()
        st["on_right"].start()
        st["from_right"].wait_recv()
        st["on_left"].start()

    def complete(st):
        st["from_left2"].wait_recv()
        st["from_right2"].wait_recv()

    own, other = gather(0, zl, False), gather(1, 1 - zl, True)
    both = (own, other)
    begin(own[0])
    begin(own[1][0])
    pair_cp.wait_recv()
    kv[x, y, 1 - zl] = qkv[1 - zl, 2 * HEAD :]
    begin(other[0])
    begin(other[1][0])
    low = place.low_block(x, y)
    for s in range(2):
        base = jnp.where(s == 0, low, 31 - low) * ROWS
        segs = query_segments(ends, base)
        for h in range(2):
            qaug[s, :HEAD, h * ROWS : (h + 1) * ROWS] = qkv[s, h * HEAD : (h + 1) * HEAD]
            qaug[s, HEAD:, h * ROWS : (h + 1) * ROWS] = segs
    peak[...] = jnp.full(peak.shape, -BIG, F32)
    total[...] = jnp.zeros(total.shape, F32)
    acc[...] = jnp.zeros(acc.shape, F32)

    def attend(qs, kx, ky, ks, kbase, causal):
        pair = kv[kx, ky, ks]
        ka = jnp.concatenate([pair[:HEAD], key_segments(ends, kbase)], 0)
        s = dot(ka, qaug[qs], 0, 0)
        if causal:
            key = lax.broadcasted_iota(jnp.int32, (ROWS, 2 * ROWS), 0)
            query = lax.broadcasted_iota(jnp.int32, (ROWS, 2 * ROWS), 1)
            s = jnp.where(key <= jnp.where(query >= ROWS, query - ROWS, query), s, -BIG)
        old = peak[qs]
        new = jnp.maximum(old, jnp.max(s, 0, keepdims=True))
        p = jnp.exp2(s - new)
        fade = jnp.exp2(old - new)
        peak[qs] = new
        total[qs] = total[qs] * fade + jnp.sum(p, 0, keepdims=True)
        acc[qs] = acc[qs] * fade + dot(pair[HEAD:], p.astype(BF16))

    def shard(dx, dy):
        kx, ky = lax.rem(x + dx, 4), lax.rem(y + dy, 4)
        there = place.low_block(kx, ky)
        attend(1, kx, ky, 0, there * ROWS, False)
        sel = jnp.where(there < low, 0, 1)
        attend(sel, kx, ky, sel, jnp.where(there < low, there, 31 - there) * ROWS, False)

    def shards(count, offsets):
        def step(i, carry):
            shard(*offsets(i))
            return carry

        lax.fori_loop(0, count, step, 0)

    attend(0, x, y, 0, low * ROWS, True)
    attend(1, x, y, 1, (31 - low) * ROWS, True)
    attend(1, x, y, 0, low * ROWS, False)
    for s1, s2 in both:
        hand_on(s1)
        begin(s2[3])
        begin(s2[1])
    for s1, s2 in both:
        hand_on(s2[0])
    shards(4, lambda i: ((1 - i // 2) * (2 * i + 1), (i // 2) * (2 * i - 3)))
    for s1, s2 in both:
        complete(s1)
        begin(s2[2])
    for s1, s2 in both:
        hand_on(s2[3])
        hand_on(s2[1])
    shards(4, lambda i: (2 * (i // 2) + 1, 2 * lax.rem(i, 2) + 1))
    for s1, s2 in both:
        complete(s2[0])
        hand_on(s2[2])
    shards(2, lambda i: (2 * i, 2 - 2 * i))
    for s1, s2 in both:
        complete(s2[3])
        complete(s2[1])
    shards(4, lambda i: ((1 - i // 2) * (2 * i + 1) + 2 * (i // 2), (i // 2) * (2 * i - 3) + 2 * (1 - i // 2)))
    for s1, s2 in both:
        complete(s2[2])
    shard(2, 2)
    for s in range(2):
        out = acc[s] / total[s]
        lse[s] = peak[s] + jnp.log2(total[s])
        for h in range(2):
            part = out[:, h * ROWS : (h + 1) * ROWS]
            o[s, h * HEAD : (h + 1) * HEAD] = part
            mine[s, h * HEAD : (h + 1) * HEAD] = part.astype(BF16)

    for s1, s2 in both:
        for st in [s1, *s2]:
            for name in ("right", "left", "on_right", "on_left"):
                st[name].wait_send()
    pair_cp.wait_send()

    group = me_t * 2 + zl
    att[group] = mine[zl]
    sends = [
        remote(mine.at[1 - zl], att.at[group], o_send.at[0], o_recv.at[0], partner),
        remote(mine.at[1 - zl], att.at[group], o_send.at[1], o_recv.at[1], far_partner),
        remote(mine.at[zl], att.at[group], o_send.at[2], o_recv.at[2], far),
    ]
    for cp in sends:
        cp.start()
    wo_far = wo_full.at[there_t]
    remote(wo_far, wo_far, w_send.at[0], w_recv.at[0], far).wait_recv()
    wo_relay = remote(wo_far, wo_far, w_send.at[2], w_recv.at[2], core)
    wo_relay.start()
    order = [
        (None, group), (0, me_t * 2 + 1 - zl), (1, there_t * 2 + 1 - zl), (2, there_t * 2 + zl),
    ]
    relays = []
    for n, (sem, which) in enumerate(order):
        if sem is not None:
            remote(att.at[which], att.at[which], o_send.at[sem], o_recv.at[sem], far).wait_recv()
        cp = remote(att.at[which], att.at[which], o_send.at[3 + n], o_recv.at[3 + n], core)
        cp.start()
        relays.append(cp)

    def load_wo(t, slot, own=False):
        if own:
            pltpu.make_async_copy(wo, wo_buf.at[slot], wo_sem.at[slot]).start()
            return

        @pl.when(me_t == t)
        def _():
            pltpu.make_async_copy(wo, wo_buf.at[slot], wo_sem.at[slot]).start()

        @pl.when(me_t != t)
        def _():
            pltpu.make_async_copy(wo_full.at[t], wo_buf.at[slot], wo_sem.at[slot]).start()

    def wo_ready(slot):
        pltpu.make_async_copy(wo, wo_buf.at[slot], wo_sem.at[slot]).wait()

    w1, w2 = wo_full.at[mine_t], wo_full.at[other_t]
    remote(w1, w1, w_send.at[1], w_recv.at[1], core).wait_recv()
    remote(w2, w2, w_send.at[2], w_recv.at[2], core).wait_recv()
    load_wo(0, 0)
    load_wo(1, 1)
    mixed[...] = tokens[...].astype(F32)
    for n, which in enumerate([mine_t * 2 + zl, mine_t * 2 + 1 - zl, other_t * 2 + 1 - zl, other_t * 2 + zl]):
        remote(att.at[which], att.at[which], o_send.at[3 + n], o_recv.at[3 + n], core).wait_recv()

    for t in range(4):
        wo_ready(t % 2)
        heads = att[2 * t : 2 * t + 2].reshape(HEADS_LOCAL, ROWS)
        mixed[...] = mixed[...] + dot(heads, wo_buf[t % 2], 0, 0)
        if t < 2:
            load_wo(t + 2, t % 2)
        elif t == 2:
            load_wo(0, 0, own=True)
    normed_save.wait()
    gain = gain2[...].reshape(1, WIDTH)
    inverse_two = lax.rsqrt(jnp.mean(mixed[...] * mixed[...], -1, keepdims=True) + EPS)
    normed[...] = (mixed[...] * inverse_two * gain).astype(BF16)
    mixed_save = pltpu.make_async_copy(mixed, mixed_out, load_sem.at[1])
    mixed_save.start()

    for k in range(FF_CHUNKS):
        slot, cols = k % 2, slice(k * FF_CHUNK, (k + 1) * FF_CHUNK)
        for cp in ff_loads(k):
            cp.wait()
        both_ff = dot(normed[...], gu_buf[slot])
        gate, upper = both_ff[:, :FF_CHUNK], both_ff[:, FF_CHUNK:]
        hidden_grad = dot(cot[...], d_buf[slot], 1, 1)
        sig = jax.nn.sigmoid(gate)
        silu = gate * sig
        hid = (silu * upper).astype(BF16)
        gg = (hidden_grad * upper * sig * (1.0 + gate * (1.0 - sig))).astype(BF16)
        ug = (hidden_grad * silu).astype(BF16)
        hidden[:, cols], gate_grad[:, cols], upper_grad[:, cols] = hid, gg, ug
        add_back = dot(jnp.concatenate([gg, ug], 1), gu_buf[slot], 1, 1)
        add_feed = dot(hid, d_buf[slot])
        if k == 0:
            mixed_save.wait()
            back[...], mixed[...] = add_back, add_feed
        else:
            back[...] = back[...] + add_back
            mixed[...] = mixed[...] + add_feed
        if k + 2 < FF_CHUNKS:
            for cp in ff_loads(k + 2):
                cp.start()
    part3[...] = ar_view(back[...].astype(BF16))
    sum3 = TpSum(place, part3, buf3, (send3, recv3))
    sum3.start()
    feed_out[...] = ar_view(mixed[...].astype(BF16))
    mixed_load = pltpu.make_async_copy(mixed_out, mixed, load_sem.at[1])
    mixed_load.start()

    def weight_grad(rhs, lo, cb=0):
        w = rhs.shape[1 - cb]

        def slab(i, carry):
            piece = dot(left[pl.ds(pl.multiple_of(i * 192, 192), 192)], rhs[...], 1, cb)
            grads[i // 4, i % 4, :, :, lo : lo + w] = piece.astype(BF16).reshape(4, 48, w)
            return carry

        lax.fori_loop(0, 8, slab, 0)

    groups, blo = {}, dict(plane=0, depth=0)
    for n, (name, kind, first, slo, w, glo) in enumerate(PLAN):
        if kind == "plane":
            piece = PlaneSum(place, first, grads, glo, blo[kind], slo, w, (b1, r1, b2, r2, zb), (gsend, grecv), n, sums)
        else:
            piece = DepthSum(place, first, grads, glo, blo[kind], slo, w, (z0, b1z, r1z, b2z), (gsend, grecv), n, sums)
        blo[kind] += w
        groups.setdefault(name, []).append(piece)
    pieces = [p for group_ in groups.values() for p in group_]

    def go(*names):
        for name in names:
            for piece in groups[name]:
                piece.next()

    left[...] = cot[...].T
    weight_grad(hidden, 2 * FFL)
    go("down")
    sum3.mid()
    left[...] = normed[...].T
    weight_grad(gate_grad, 0)
    go("gate")
    weight_grad(upper_grad, FFL)
    go("up")
    sum2 = TpSum(place, feed_out, buf2, (send2, recv2))
    sum2.start()
    for s in range(2):
        for h in range(2):
            dot_t[s, :, h * ROWS : (h + 1) * ROWS] = jnp.zeros((HEAD, ROWS), BF16)
    acc[...] = jnp.zeros(acc.shape, F32)
    dq = acc
    mixed_load.wait()
    sum3.fin()
    go("down_z", "gate_z", "up_z")
    sum3.landed()
    mixed_part, ffn_gain_grad = norm_back(mixed[...], inverse_two, gain, ar_load(part3).astype(F32))
    gain_sum[0, 1:2] = ffn_gain_grad
    back[...] = cot[...].astype(F32) + mixed_part
    normed[...] = back[...].astype(BF16)
    wo_ready(0)
    own_grad = dot(wo_buf[0], normed[...], 1, 1).astype(BF16)
    dgrp[0] = own_grad[: 2 * HEAD]
    dgrp[1] = own_grad[2 * HEAD :]
    grad_cp = remote(dgrp.at[1 - zl], dout.at[zl], pair_send.at[1], pair_recv.at[1], partner)
    grad_cp.start()
    dout[zl] = dgrp[zl]
    left[...] = normed[...].T
    weight_grad(att.at[pl.ds(me_t * 2, 2)][...].reshape(HEADS_LOCAL, ROWS), W_FFN, 1)
    go("out")
    normed_load = pltpu.make_async_copy(normed_out, normed, load_sem.at[0])
    normed_load.start()
    for cp in projections():
        cp.start()
    go("down")
    grad_cp.wait_recv()
    for s in range(2):
        for h in range(2):
            lanes, feats = slice(h * ROWS, (h + 1) * ROWS), slice(h * HEAD, (h + 1) * HEAD)
            d = dout[s, feats]
            dot_t[s, :, lanes] = d
            delta[s, :, lanes] = jnp.sum(d.astype(F32) * o[s, feats], 0, keepdims=True)

    def attend_back(qs, kx, ky, ks, kbase, causal):
        pair = kv[kx, ky, ks]
        q = qaug[qs]
        do = dot_t[qs]
        ka = jnp.concatenate([pair[:HEAD], key_segments(ends, kbase)], 0)
        s = dot(ka, q, 0, 0)
        p = jnp.exp2(s - lse[qs])
        if causal:
            key = lax.broadcasted_iota(jnp.int32, (ROWS, 2 * ROWS), 0)
            query = lax.broadcasted_iota(jnp.int32, (ROWS, 2 * ROWS), 1)
            p = jnp.where(key <= jnp.where(query >= ROWS, query - ROWS, query), p, 0.0)
        dp = dot(pair[HEAD:], do, 0, 0)
        ds = (p * (dp - delta[qs])).astype(BF16)
        dq[qs] = dq[qs] + dot(pair[:HEAD], ds)
        dk = dot(q[:HEAD], ds, 1, 1)
        dv = dot(do, p.astype(BF16), 1, 1)
        return jnp.concatenate([dk, dv], 0)

    first = attend_back(0, x, y, 0, low * ROWS, True) + attend_back(1, x, y, 0, low * ROWS, False)
    kv[x, y, 0] = first.astype(BF16)
    kv[x, y, 1] = attend_back(1, x, y, 1, (31 - low) * ROWS, True).astype(BF16)

    def step(i, carry):
        kx, ky = lax.rem(x + i // 4, 4), lax.rem(y + i % 4, 4)
        there = place.low_block(kx, ky)
        one = attend_back(1, kx, ky, 0, there * ROWS, False)
        before = there < low
        sel = jnp.where(before, 0, 1)
        two = attend_back(sel, kx, ky, sel, jnp.where(before, there, 31 - there) * ROWS, False)
        share = jnp.where(before, 1.0, 0.0)
        kv[kx, ky, 0] = (one + two * share).astype(BF16)
        kv[kx, ky, 1] = (two * (1.0 - share)).astype(BF16)
        return carry

    lax.fori_loop(1, 4, step, 0)
    go("gate")
    lax.fori_loop(4, 7, step, 0)
    go("up", "out", "down_z")
    lax.fori_loop(7, 10, step, 0)
    go("down")
    lax.fori_loop(10, 13, step, 0)
    go("gate", "gate_z")
    lax.fori_loop(13, 16, step, 0)

    for s in range(2):
        for h in range(2):
            grp[s, h * HEAD : (h + 1) * HEAD] = (dq[s, :, h * ROWS : (h + 1) * ROWS] * SCALE).astype(BF16)
    q_rows, k_rows = pl.ds(0, 2 * HEAD), pl.ds(2 * HEAD, 2 * HEAD)
    dq_cp = remote(grp.at[1 - zl, q_rows], dqkv.at[zl, q_rows], pair_send.at[2], pair_recv.at[2], partner)
    dq_cp.start()
    dqkv[zl, : 2 * HEAD] = grp[zl, : 2 * HEAD]

    def key_sum(slot, axis):
        other_axis = "y" if axis == "x" else "x"
        if axis == "x":
            half = lambda d, h: kv.at[d, :, slot, pl.ds(h * HEAD, HEAD)]
        else:
            half = lambda d, h: kv.at[:, d, slot, pl.ds(h * HEAD, HEAD)]
        one = RingSum(
            place, axis, half, lambda k: kb1.at[slot, k], lambda h: kr1.at[slot, h],
            lambda k: ksend.at[slot, k], lambda k: krecv.at[slot, k],
        )
        two = RingSum(
            place, other_axis, lambda d, h: kr1.at[slot, h, d], lambda k: kb2.at[slot, k],
            lambda h: kr2.at[slot, h], lambda k: ksend.at[slot, 6 + k], lambda k: krecv.at[slot, 6 + k],
        )
        return one, two

    ka, kb = key_sum(0, "x"), key_sum(1, "y")
    ka[0].start()
    kb[0].start()
    go("up", "out", "up_z", "down_z")
    sum2.mid()
    ka[0].mid()
    kb[0].mid()
    go("down", "gate", "gate_z", "down_z")

    def unturned(g, h, at):
        a = dqkv[g, h * HEAD : h * HEAD + HALF].astype(F32)
        b = dqkv[g, h * HEAD + HALF : (h + 1) * HEAD].astype(F32)
        if h == 2:
            a, b = a * LN2, b * LN2
        rows[at : at + HALF] = (a * cosine + b * sine).astype(BF16)
        rows[at + HALF : at + HEAD] = (b * cosine - a * sine).astype(BF16)

    dq_there = dqkv.at[1 - zl, q_rows]
    remote(dq_there, dq_there, pair_send.at[2], pair_recv.at[2], partner).wait_recv()
    for g in range(2):
        for h in range(2):
            unturned(g, h, (2 * g + h) * HEAD)
    normed_load.wait()
    for piece in groups["down"]:
        piece.one.end()
    left[...] = normed[...].T
    weight_grad(rows.at[pl.ds(0, HEADS_LOCAL)], 2 * FFL, 1)
    go("query")
    ka[0].fin()
    kb[0].fin()
    ka[1].start()
    kb[1].start()
    for cp in projections():
        cp.wait()
    mixed[...] = dot(rows[:HEADS_LOCAL], gu_buf[0, :, :HEADS_LOCAL], 0, 1)
    go("up", "out", "up_z", "gate_z", "down_z")
    ka[1].mid()
    kb[1].mid()
    go("down", "gate")
    sum2.fin()
    ka[1].fin()
    kb[1].fin()
    for s in range(2):
        for h in range(2):
            grp[s, (2 + h) * HEAD : (3 + h) * HEAD] = kr2[s, h]
    dk_cp = remote(grp.at[1 - zl, k_rows], dqkv.at[zl, k_rows], pair_send.at[3], pair_recv.at[3], partner)
    dk_cp.start()
    dqkv[zl, 2 * HEAD :] = grp[zl, 2 * HEAD :]
    go("query", "up", "out", "up_z", "gate_z", "down_z")
    go("down", "gate")
    for piece in groups["gate"]:
        piece.one.end()
    sum3.end()
    dk_there = dqkv.at[1 - zl, k_rows]
    remote(dk_there, dk_there, pair_send.at[3], pair_recv.at[3], partner).wait_recv()
    for g in range(2):
        unturned(g, 2, HEADS_LOCAL + g * HEAD)
        at = HEADS_LOCAL + PAIRS_LOCAL + g * HEAD
        rows[at : at + HEAD] = dqkv[g, 3 * HEAD :]
    grad_in = mixed[...] + dot(rows[HEADS_LOCAL : HEADS_LOCAL + PAIRS_LOCAL], d_buf[0, :PAIRS_LOCAL], 0, 0)
    grad_in = grad_in + dot(rows[HEADS_LOCAL + PAIRS_LOCAL :], d_buf[1, :PAIRS_LOCAL], 0, 0)
    part3[...] = ar_view(grad_in.astype(BF16))
    sum4 = TpSum(place, part3, buf4, (send4, recv4))
    sum4.start()
    weight_grad(rows.at[pl.ds(HEADS_LOCAL, 2 * PAIRS_LOCAL)], 0, 1)
    go("pair")
    sum4.mid()
    go("query", "up", "out", "up_z", "gate_z")
    go("pair")
    go("query")
    sum4.fin()
    sum4.landed()
    source = tokens[...].astype(F32)
    source_part, gain_grad = norm_back(source, inverse, gain1[...].reshape(1, WIDTH), ar_load(part3).astype(F32))
    tokens_grad[...] = (back[...] + source_part).astype(BF16)
    gain_sum[0, 0:1] = gain_grad

    def gain_copies(stage, axis):
        if axis == "zl":
            there = [place.at(zl=1 - zl)]
        else:
            there = [place.along(axis, s) for s in (1, 2, 3)]
        return [
            remote(gain_sum.at[stage], gain_buf.at[stage, k], gn_send.at[stage, k], gn_recv.at[stage, k], peer)
            for k, peer in enumerate(there)
        ]

    sent_x = gain_copies(0, "x")
    for cp in sent_x:
        cp.start()
    go("pair")
    go("query", "up_z")
    for cp in sent_x:
        cp.wait_recv()
    gain_sum[1] = gain_sum[0] + gain_buf[0, 0] + gain_buf[0, 1] + gain_buf[0, 2]
    sent_y = gain_copies(1, "y")
    for cp in sent_y:
        cp.start()
    go("pair")
    for cp in sent_y:
        cp.wait_recv()
    gain_sum[2] = gain_sum[1] + gain_buf[1, 0] + gain_buf[1, 1] + gain_buf[1, 2]
    sent_z = gain_copies(2, "zl")
    for cp in sent_z:
        cp.start()
    go("pair")
    go("query")
    for cp in sent_z:
        cp.wait_recv()
    gains[...] = gain_sum[2] + gain_buf[2, 0]
    go("pair")
    sum2.landed()
    for cp in [grad_cp, dq_cp, dk_cp, *wo_cps, wo_relay, *sends, *relays, *sent_x, *sent_y, *sent_z]:
        cp.wait_send()
    sum2.end()
    sum4.end()
    for piece in pieces:
        assert piece.at == len(piece.steps)
        piece.end()
    for one, two in (ka, kb):
        one.end()
        two.end()


def layer(lengths, freq, tokens, cot, gain1, gain2, wq, wkt, wvt, wo, wg, wu, wd):
    vm = pl.BlockSpec(memory_space=pltpu.VMEM)
    hbm = pl.BlockSpec(memory_space=pl.ANY)
    dma = pltpu.SemaphoreType.DMA
    shape = (2, AR_PIECES, AR_ROWS, WIDTH)
    group = pltpu.VMEM((2, 4 * HEAD, ROWS), BF16)
    two_heads = pltpu.VMEM((2, 2 * HEAD, ROWS), BF16)
    line = pltpu.VMEM((2, 1, 2 * ROWS), F32)
    return pl.pallas_call(
        layer_kernel,
        out_shape=(
            jax.ShapeDtypeStruct((ROWS, WIDTH), F32),
            jax.ShapeDtypeStruct((ROWS, WIDTH), BF16),
            jax.ShapeDtypeStruct((4, HEADS_LOCAL, WIDTH), BF16),
            jax.ShapeDtypeStruct(shape, BF16),
            jax.ShapeDtypeStruct((ROWS, WIDTH), BF16),
            jax.ShapeDtypeStruct((48, W_ALL), F32),
            jax.ShapeDtypeStruct((2, WIDTH), F32),
        ),
        in_specs=[pl.BlockSpec(memory_space=pltpu.SMEM)] + [vm] * 5 + [hbm] * 7,
        out_specs=(hbm, hbm, hbm, vm, vm, vm, vm),
        scratch_shapes=[
            pltpu.VMEM((2, HEADS_LOCAL, WIDTH), BF16),
            pltpu.VMEM((2, WIDTH, 2 * FF_CHUNK), BF16),
            pltpu.VMEM((2, FF_CHUNK, WIDTH), BF16),
            pltpu.VMEM((ROWS, WIDTH), F32),
            pltpu.VMEM((ROWS, WIDTH), F32),
            pltpu.VMEM((ROWS, WIDTH), BF16),
            pltpu.VMEM((ROWS, FFL), BF16),
            pltpu.VMEM((ROWS, FFL), BF16),
            pltpu.VMEM((ROWS, FFL), BF16),
            pltpu.VMEM((WIDTH, ROWS), BF16),
            pltpu.VMEM((2, 4, 4, 48, W_MID), BF16),
            pltpu.VMEM((6, 4, 48, W_PLANE), BF16),
            pltpu.VMEM((2, 4, 48, W_PLANE), BF16),
            pltpu.VMEM((6, 48, W_PLANE), BF16),
            pltpu.VMEM((2, 48, W_PLANE), BF16),
            pltpu.VMEM((48, W_PLANE), BF16),
            pltpu.VMEM((4, 4, 48, W_DEPTH), BF16),
            pltpu.VMEM((6, 4, 48, W_DEPTH // 2), BF16),
            pltpu.VMEM((4, 48, W_DEPTH), BF16),
            pltpu.VMEM((6, 48, W_DEPTH // 2), BF16),
            dma((len(PLAN), 13)),
            dma((len(PLAN), 13)),
            pltpu.VMEM(shape, BF16),
            *tp_scratch(),
            *tp_scratch(),
            *tp_scratch(),
            pltpu.VMEM((4, 4, 2, 2 * HEAD, ROWS), BF16),
            pltpu.VMEM((2, 6, 4, HEAD, ROWS), BF16),
            pltpu.VMEM((2, 2, 4, HEAD, ROWS), BF16),
            pltpu.VMEM((2, 6, HEAD, ROWS), BF16),
            pltpu.VMEM((2, 2, HEAD, ROWS), BF16),
            dma((2, 12)),
            dma((2, 12)),
            group,
            group,
            pltpu.VMEM((8, 2 * HEAD, ROWS), BF16),
            pltpu.VMEM((2, 2 * HEAD, ROWS), F32),
            line,
            pltpu.VMEM((2, HEAD + SEG, 2 * ROWS), BF16),
            pltpu.VMEM((2, HEAD, 2 * ROWS), F32),
            line,
            line,
            two_heads,
            two_heads,
            two_heads,
            pltpu.VMEM((2, HEAD, 2 * ROWS), BF16),
            line,
            group,
            pltpu.VMEM((W_TAIL, ROWS), BF16),
            pltpu.VMEM((3, 2, WIDTH), F32),
            pltpu.VMEM((3, 3, 2, WIDTH), F32),
            dma((3, 3)),
            dma((3, 3)),
            dma((4,)),
            dma((4,)),
            dma((2, 20)),
            dma((2, 20)),
            dma((7,)),
            dma((7,)),
            dma((3,)),
            dma((3,)),
            dma((2,)),
            dma((2, 3)),
            dma((2,)),
        ],
        compiler_params=pltpu.CompilerParams(
            collective_id=0, has_side_effects=True, vmem_limit_bytes=VMEM_LIMIT
        ),
        name="layer",
    )(lengths, freq, tokens, cot, gain1, gain2, wq, wkt, wvt, wo, wg, wu, wd)


def finish_kernel(
    mixed, feed, tokens_grad, sums, gains,
    result, tokens_grad_out, norm_gain, query, key, value, out, ffn_gain, gate, up, down,
):
    result[...] = (mixed[...] + ar_load(feed).astype(F32)).astype(BF16)
    tokens_grad_out[...] = tokens_grad[...]
    block = (lax.axis_index("zl") * 4 + lax.axis_index("x")) * 4 + lax.axis_index("y")
    own = jnp.zeros((2, 48), F32)
    for b in range(32):
        own = own + jnp.where(block == b, gains[:, 48 * b : 48 * b + 48], 0.0)
    norm_gain[...] = own[0:1]
    ffn_gain[...] = own[1:2]
    gate[...] = sums[:, :FFL]
    up[...] = sums[:, FFL : 2 * FFL]
    down[...] = sums[:, 2 * FFL : W_FFN]
    out[...] = sums[:, W_FFN:W_MID]
    query[...] = sums[:, W_MID : W_MID + HEADS_LOCAL]
    key[...] = sums[:, W_MID + HEADS_LOCAL : W_MID + HEADS_LOCAL + PAIRS_LOCAL]
    value[...] = sums[:, W_MID + HEADS_LOCAL + PAIRS_LOCAL :]


def finish(mixed, feed, tokens_grad, sums, gains):
    vm = pl.BlockSpec(memory_space=pltpu.VMEM)
    shapes = [(ROWS, WIDTH)] * 2 + [
        (1, 48), (48, HEADS_LOCAL), (48, PAIRS_LOCAL), (48, PAIRS_LOCAL), (48, HEADS_LOCAL), (1, 48),
        (48, FFL), (48, FFL), (48, FFL),
    ]
    return pl.pallas_call(
        finish_kernel,
        out_shape=[jax.ShapeDtypeStruct(s, BF16 if n < 2 else F32) for n, s in enumerate(shapes)],
        in_specs=[vm] * 5,
        out_specs=[vm] * len(shapes),
        compiler_params=pltpu.CompilerParams(vmem_limit_bytes=VMEM_LIMIT),
        name="finish",
    )(mixed, feed, tokens_grad, sums, gains)


def local(
    tokens, norm_gain, query_weight, key_matrix, value_matrix, out_weight,
    ffn_gain, gate_weight, up_weight, down_weight, cotangent, lengths,
):
    freq = jnp.asarray(
        (THETA ** (-2.0 * np.arange(HALF) / HEAD)).astype(np.float32).reshape(HALF, 1)
    )
    mixed, _, _, feed, tokens_grad, sums, gains = layer(
        lengths, freq, tokens, cotangent, norm_gain, ffn_gain, query_weight, key_matrix.T, value_matrix.T,
        out_weight, gate_weight, up_weight, down_weight,
    )
    result, tokens_grad, norm_gain_grad, query, key, value, out, ffn_gain_grad, gate, up, down = finish(
        mixed, feed, tokens_grad, sums, gains
    )
    return (
        result, tokens_grad, norm_gain_grad.reshape(48), query, key, value, out.T,
        ffn_gain_grad.reshape(48), gate, up, down.T,
    )


def solution(mesh):
    split = Mesh(mesh.devices.reshape(2, 4, 4, 2, 2), AXES)
    in_specs = (
        P(BLK, None),
        P(),
        P(None, TP),
        P(None, TP),
        P(None, TP),
        P(TP, None),
        P(),
        P(None, TP),
        P(None, TP),
        P(TP, None),
        P(BLK, None),
        P(),
    )
    out_specs = (
        P(BLK, None),
        P(BLK, None),
        P(BLK),
        P(BLK, TP),
        P(BLK, TP),
        P(BLK, TP),
        P(TP, BLK),
        P(BLK),
        P(BLK, TP),
        P(BLK, TP),
        P(TP, BLK),
    )
    return jax.shard_map(local, mesh=split, in_specs=in_specs, out_specs=out_specs, check_vma=False)
```

```python
import jax
import jax.numpy as jnp
import numpy as np
from jax import lax
from jax.experimental import pallas as pl
from jax.experimental.pallas import tpu as pltpu
from jax.sharding import Mesh
from jax.sharding import PartitionSpec as P

AXES = ("zl", "x", "y", "zh", "c")
BLK = ("zl", "x", "y")
TP = ("zh", "c")
HEAD = 96
HALF = HEAD // 2
ROWS = 256
WIDTH = 1536
HEADS_LOCAL = 384
PAIRS_LOCAL = 192
FFL = 1024
EPS = 1e-05
THETA = 100000.0
SCALE = HEAD**-0.5
LOG2E = float(np.log2(np.e))
LN2 = float(np.log(2.0))
BIG = 1e30
SEG = 16
MESH = pl.DeviceIdType.MESH
F32 = jnp.float32
BF16 = jnp.bfloat16
VMEM_LIMIT = 63 * 2**20


def dot(a, b, ca=1, cb=0):
    return lax.dot_general(a, b, (((ca,), (cb,)), ((), ())), preferred_element_type=F32)


class Place:
    def __init__(self):
        self.zl, self.x, self.y, self.zh, self.c = (lax.axis_index(a) for a in AXES)

    def at(self, **changes):
        own = dict(zl=self.zl, x=self.x, y=self.y, zh=self.zh, c=self.c)
        own.update(changes)
        return tuple(own[a] for a in AXES)

    def along(self, axis, step):
        return self.at(**{axis: lax.rem(getattr(self, axis) + (step + 4), 4)})

    @property
    def pair(self):
        return dict(zl=1 - self.zl, x=3 - self.x, y=3 - self.y)

    def low_block(self, x, y):
        p = x * 4 + y
        return jnp.where(self.zl == 0, p, 15 - p)


def call(peers):
    barrier = pltpu.get_barrier_semaphore()
    for peer in peers:
        pl.semaphore_signal(barrier, inc=1, device_id=peer, device_id_type=MESH)


def answer(peers):
    pl.semaphore_wait(pltpu.get_barrier_semaphore(), len(peers))


def remote(src, dst, send, recv, device):
    return pltpu.make_async_remote_copy(
        src_ref=src, dst_ref=dst, send_sem=send, recv_sem=recv, device_id=device, device_id_type=MESH
    )


def seg_rows(ends, base):
    token = base + lax.broadcasted_iota(jnp.int32, (SEG, ROWS), 1)
    row = lax.broadcasted_iota(jnp.int32, (SEG, ROWS), 0)
    inside = jnp.zeros((SEG, ROWS), F32)
    start = 0
    for d in range(5):
        hit = (row == d) & (token >= start) & (token < ends[d])
        inside = jnp.where(hit, 1.0, inside)
        start = ends[d]
    return inside, row


def key_segments(ends, base):
    return seg_rows(ends, base)[0].astype(BF16)


def query_segments(ends, base):
    inside, row = seg_rows(ends, base)
    return jnp.where(row < 5, (inside - 1.0) * BIG, 0.0).astype(BF16)


def ends_of(lengths_ref):
    ends, total = [], 0
    for d in range(5):
        total = total + lengths_ref[d]
        ends.append(total)
    return ends


def rotation(ends, lengths_ref, base, freq):
    token = base + lax.broadcasted_iota(jnp.int32, (1, ROWS), 1)
    begin = jnp.zeros((1, ROWS), jnp.int32)
    for d in range(5):
        begin = begin + jnp.where(token >= ends[d], lengths_ref[d], 0)
    angle = (token - begin).astype(F32) * freq
    return jnp.cos(angle), jnp.sin(angle)


class RingSum:
    def __init__(self, place, axis, half, bufs, out, send, recv):
        self.half, self.bufs, self.out = half, bufs, out
        me = getattr(place, axis)
        self.me = me
        self.r, self.l, self.o = (lax.rem(me + k, 4) for k in (1, 3, 2))
        self.right, self.left = place.along(axis, 1), place.along(axis, -1)
        self.send, self.recv = send, recv
        self.ended = False

    def cp(self, k):
        src = (
            lambda: self.half(self.o, 0),
            lambda: self.half(self.o, 1),
            lambda: self.half(self.r, 1),
            lambda: self.half(self.l, 0),
            lambda: self.bufs(0),
            lambda: self.bufs(1),
        )[k]()
        return remote(src, self.bufs(k), self.send(k), self.recv(k), (self.right, self.left)[k % 2])

    def start_far(self):
        self.cp(0).start()
        self.cp(1).start()

    def start_near(self):
        self.cp(2).start()
        self.cp(3).start()

    def start(self):
        self.start_far()
        self.start_near()

    def mid(self):
        self.cp(0).wait_recv()
        add_two(self.bufs(0), self.half(self.r, 0))
        self.cp(4).start()
        self.cp(1).wait_recv()
        add_two(self.bufs(1), self.half(self.l, 1))
        self.cp(5).start()

    def fin(self):
        self.cp(4).wait_recv()
        self.cp(3).wait_recv()
        add_three(self.out(0), self.half(self.me, 0), self.bufs(4), self.bufs(3))
        self.cp(5).wait_recv()
        self.cp(2).wait_recv()
        add_three(self.out(1), self.half(self.me, 1), self.bufs(5), self.bufs(2))

    def end(self):
        if not self.ended:
            self.ended = True
            for k in range(6):
                self.cp(k).wait_send()


def add_two(dst, src):
    if len(dst.shape) == 3:
        for i in range(dst.shape[0]):
            dst[i] = dst[i] + src[i]
    else:
        dst[...] = dst[...] + src[...]


def add_three(out, a, b, d):
    if len(out.shape) == 3:
        for i in range(out.shape[0]):
            out[i] = (a[i].astype(F32) + b[i].astype(F32) + d[i].astype(F32)).astype(out.dtype)
    else:
        out[...] = (a[...].astype(F32) + b[...].astype(F32) + d[...].astype(F32)).astype(out.dtype)


class Steps:
    at = 0

    def next(self):
        self.steps[self.at]()
        self.at += 1


class PlaneSum(Steps):
    def __init__(self, place, first, g, glo, blo, slo, w, bufs, sems, n, sums):
        b1, r1, b2, r2, zb = bufs
        send, recv = sems
        gc, bc = pl.ds(glo, w), pl.ds(blo, w)
        self.place, self.r2, self.zb, self.bc, self.sc = place, r2, zb, bc, slice(slo, slo + w)
        self.send, self.recv, self.n, self.sums = send, recv, n, sums
        if first == "x":
            half1 = lambda d, h: g.at[h, d, :, :, gc]
        else:
            half1 = lambda d, h: g.at[h, :, d, :, gc]
        self.one = RingSum(
            place, first, half1, lambda k: b1.at[k, :, :, bc], lambda h: r1.at[h, :, :, bc],
            lambda k: send.at[n, k], lambda k: recv.at[n, k],
        )
        self.two = RingSum(
            place, "y" if first == "x" else "x", lambda d, h: r1.at[h, d, :, bc], lambda k: b2.at[k, :, bc],
            lambda h: r2.at[h, :, bc], lambda k: send.at[n, 6 + k], lambda k: recv.at[n, 6 + k],
        )
        self.steps = [self.one.start, self.one.mid, self.turn, self.two.mid, self.cross, self.total]

    def zcp(self):
        other = 1 - self.place.zl
        return remote(
            self.r2.at[other, :, self.bc], self.zb.at[:, self.bc], self.send.at[self.n, 12],
            self.recv.at[self.n, 12], self.place.at(zl=other),
        )

    def turn(self):
        self.one.fin()
        self.two.start()

    def cross(self):
        self.two.fin()
        self.zcp().start()

    def total(self):
        self.zcp().wait_recv()
        own = self.r2[self.place.zl, :, self.bc].astype(F32)
        self.sums[:, self.sc] = own + self.zb[:, self.bc].astype(F32)

    def end(self):
        self.one.end()
        self.two.end()
        self.zcp().wait_send()


class DepthSum(Steps):
    def __init__(self, place, first, g, glo, blo, slo, w, bufs, sems, n, sums):
        z0, b1, r1, b2 = bufs
        send, recv = sems
        h_w = w // 2
        self.place, self.g, self.z0 = place, g, z0
        self.gc, self.zc = pl.ds(glo, w), pl.ds(blo, w)
        self.send, self.recv, self.n = send, recv, n
        zl = place.zl
        part = lambda lo, h: pl.ds(lo + h * h_w, h_w)
        if first == "x":
            half1 = lambda d, h: g.at[zl, d, :, :, part(glo, h)]
        else:
            half1 = lambda d, h: g.at[zl, :, d, :, part(glo, h)]
        bc = pl.ds(blo // 2, h_w)
        self.one = RingSum(
            place, first, half1, lambda k: b1.at[k, :, :, bc], lambda h: r1.at[:, :, part(blo, h)],
            lambda k: send.at[n, k], lambda k: recv.at[n, k],
        )
        self.two = RingSum(
            place, "y" if first == "x" else "x", lambda d, h: r1.at[d, :, part(blo, h)], lambda k: b2.at[k, :, bc],
            lambda h: sums.at[:, part(slo, h)], lambda k: send.at[n, 6 + k], lambda k: recv.at[n, 6 + k],
        )
        self.steps = [self.cross, self.join, self.one.mid, self.turn, self.two.mid, self.two.fin]

    def zcp(self):
        other = 1 - self.place.zl
        return remote(
            self.g.at[other, :, :, :, self.gc], self.z0.at[:, :, :, self.zc], self.send.at[self.n, 12],
            self.recv.at[self.n, 12], self.place.at(zl=other),
        )

    def cross(self):
        self.zcp().start()

    def join(self):
        self.zcp().wait_recv()
        mine = self.g.at[self.place.zl, :, :, :, self.gc]
        came = self.z0.at[:, :, :, self.zc]

        def add(i, carry):
            for j in range(4):
                mine[i, j] = mine[i, j] + came[i, j]
            return carry

        lax.fori_loop(0, 4, add, 0)
        self.one.start()

    def turn(self):
        self.one.fin()
        self.two.start()

    def end(self):
        self.one.end()
        self.two.end()
        self.zcp().wait_send()


AR_PIECES = 2
AR_ROWS = ROWS // 2 // AR_PIECES


class TpSum:
    def __init__(self, place, part, buf, sems):
        self.place, self.part, self.buf = place, part, buf
        self.send, self.recv = sems
        self.core = place.at(c=1 - place.c)
        self.far = place.at(zh=1 - place.zh)

    def a(self, k):
        return remote(
            self.part.at[1 - self.place.c, k], self.buf.at[0, k], self.send.at[0, k], self.recv.at[0, k], self.core
        )

    def b(self, k):
        return remote(self.buf.at[0, k], self.buf.at[1, k], self.send.at[1, k], self.recv.at[1, k], self.far)

    def d(self, k):
        return remote(
            self.part.at[self.place.c, k], self.buf.at[2, k], self.send.at[2, k], self.recv.at[2, k], self.core
        )

    def start(self):
        for k in range(AR_PIECES):
            self.a(k).start()

    def mid(self):
        for k in range(AR_PIECES):
            self.a(k).wait_recv()
            self.buf[0, k] = self.buf[0, k] + self.part[self.place.c, k]
            self.b(k).start()

    def fin(self):
        for k in range(AR_PIECES):
            self.b(k).wait_recv()
            self.part[self.place.c, k] = self.buf[0, k] + self.buf[1, k]
            self.d(k).start()

    def landed(self):
        for k in range(AR_PIECES):
            self.a(k).wait_send()
            self.d(k).wait_recv()
            self.part[1 - self.place.c, k] = self.buf[2, k]

    def end(self):
        for k in range(AR_PIECES):
            self.b(k).wait_send()
            self.d(k).wait_send()


def tp_scratch():
    return [
        pltpu.VMEM((3, AR_PIECES, AR_ROWS, WIDTH), BF16),
        pltpu.SemaphoreType.DMA((3, AR_PIECES)),
        pltpu.SemaphoreType.DMA((3, AR_PIECES)),
    ]


def ar_view(value):
    return value.reshape(2, AR_PIECES, AR_ROWS, WIDTH)


def ar_load(ref):
    return ref[...].reshape(ROWS, WIDTH)


def norm_back(source, inverse, gain, grad):
    scaled = grad * gain
    gain_grad = jnp.sum(grad * source * inverse, 0, keepdims=True)
    mean = jnp.mean(scaled * source, -1, keepdims=True)
    return inverse * scaled - source * (inverse * inverse * inverse) * mean, gain_grad


W_FFN = 3 * FFL
W_MID = W_FFN + HEADS_LOCAL
W_TAIL = HEADS_LOCAL + 2 * PAIRS_LOCAL
W_ALL = W_MID + W_TAIL
FF_CHUNKS = 4
FF_CHUNK = FFL // FF_CHUNKS

PLAN = [
    ("down", "plane", "x", 2048, 256, 2048),
    ("down", "plane", "y", 2304, 256, 2304),
    ("down_z", "depth", "x", 2560, 256, 2560),
    ("down_z", "depth", "y", 2816, 256, 2816),
    ("gate", "plane", "x", 0, 256, 0),
    ("gate", "plane", "y", 256, 256, 256),
    ("gate_z", "depth", "x", 512, 256, 512),
    ("gate_z", "depth", "y", 768, 256, 768),
    ("up", "plane", "x", 1024, 384, 1024),
    ("up", "plane", "y", 1408, 384, 1408),
    ("up_z", "depth", "y", 1792, 256, 1792),
    ("out", "plane", "x", 3072, 128, 3072),
    ("out", "plane", "y", 3200, 256, 3200),
    ("query", "plane", "x", 3456, 256, 2048),
    ("query", "plane", "y", 3712, 128, 2304),
    ("pair", "plane", "x", 3840, 128, 0),
    ("pair", "plane", "y", 3968, 256, 128),
]
W_PLANE = sum(p[4] for p in PLAN if p[1] == "plane")
W_DEPTH = sum(p[4] for p in PLAN if p[1] == "depth")


def layer_kernel(
    lengths, freq, tokens, cot, gain1, gain2, wq, wkt, wvt, wo, wg, wu, wd,
    mixed_out, normed_out, wo_full, feed_out, tokens_grad, sums, gains,
    wo_buf, gu_buf, d_buf, mixed, back, normed, hidden, gate_grad, upper_grad, left, grads,
    b1, r1, b2, r2, zb, z0, b1z, r1z, b2z, gsend, grecv,
    part3, buf3, send3, recv3, buf2, send2, recv2, buf4, send4, recv4,
    kv, kb1, kr1, kb2, kr2, ksend, krecv,
    grp, qkv, att, o, lse, qaug, acc, peak, total, mine, dgrp, dout, dot_t, delta, dqkv, rows,
    gain_sum, gain_buf, gn_send, gn_recv,
    pair_send, pair_recv, ag_send, ag_recv, o_send, o_recv, w_send, w_recv, load_sem, ff_sem, wo_sem,
):
    place = Place()
    zl, x, y, zh, c = place.zl, place.x, place.y, place.zh, place.c
    partner = place.at(**place.pair)
    far_partner = place.at(**place.pair, zh=1 - zh)
    far = place.at(zh=1 - zh)
    core = place.at(c=1 - c)
    diagonal = place.at(zl=1 - zl, zh=1 - zh)
    xr, xl, yr, yl = place.along("x", 1), place.along("x", -1), place.along("y", 1), place.along("y", -1)
    peers = [partner, far_partner, far, core, diagonal, place.at(zl=1 - zl), xr, xl, yr, yl]
    peers += [place.along("x", 2), place.along("y", 2)]
    call(peers)
    me_t = zh * 2 + c
    there_t = (1 - zh) * 2 + c
    mine_t, other_t = zh * 2 + (1 - c), (1 - zh) * 2 + (1 - c)

    def projections():
        return [
            pltpu.make_async_copy(wq, gu_buf.at[0, :, pl.ds(0, HEADS_LOCAL)], ff_sem.at[0, 0]),
            pltpu.make_async_copy(wkt, d_buf.at[0, pl.ds(0, PAIRS_LOCAL)], ff_sem.at[0, 1]),
            pltpu.make_async_copy(wvt, d_buf.at[1, pl.ds(0, PAIRS_LOCAL)], ff_sem.at[0, 2]),
        ]

    def ff_loads(k):
        slot, cols = k % 2, pl.ds(k * FF_CHUNK, FF_CHUNK)
        return [
            pltpu.make_async_copy(wg.at[:, cols], gu_buf.at[slot, :, pl.ds(0, FF_CHUNK)], ff_sem.at[slot, 0]),
            pltpu.make_async_copy(wu.at[:, cols], gu_buf.at[slot, :, pl.ds(FF_CHUNK, FF_CHUNK)], ff_sem.at[slot, 1]),
            pltpu.make_async_copy(wd.at[cols], d_buf.at[slot], ff_sem.at[slot, 2]),
        ]

    for cp in projections():
        cp.start()
    ends = ends_of(lengths)
    block = zl * 16 + x * 4 + y
    source = tokens[...].astype(F32)
    inverse = lax.rsqrt(jnp.mean(source * source, -1, keepdims=True) + EPS)
    normed[...] = (source * inverse * gain1[...].reshape(1, WIDTH)).astype(BF16)
    normed_save = pltpu.make_async_copy(normed, normed_out, load_sem.at[0])
    normed_save.start()
    cosine, sine = rotation(ends, lengths, block * ROWS, freq[...])

    def turned(u, factor):
        a, b = u[:HALF], u[HALF:]
        if factor is None:
            return a * cosine - b * sine, b * cosine + a * sine
        return (a * cosine - b * sine) * factor, (b * cosine + a * sine) * factor

    for cp in projections():
        cp.wait()
    kt = dot(d_buf[0, :PAIRS_LOCAL], normed[...], 1, 1)
    vt = dot(d_buf[1, :PAIRS_LOCAL], normed[...], 1, 1)
    qt = dot(normed[...], gu_buf[0, :, :HEADS_LOCAL]).T
    for g in range(2):
        for h in range(2):
            a, b = turned(qt[(2 * g + h) * HEAD : (2 * g + h + 1) * HEAD], SCALE * LOG2E)
            grp[g, h * HEAD : h * HEAD + HALF] = a.astype(BF16)
            grp[g, h * HEAD + HALF : (h + 1) * HEAD] = b.astype(BF16)
        a, b = turned(kt[g * HEAD : (g + 1) * HEAD], None)
        grp[g, 2 * HEAD : 2 * HEAD + HALF] = a.astype(BF16)
        grp[g, 2 * HEAD + HALF : 3 * HEAD] = b.astype(BF16)
        grp[g, 3 * HEAD :] = vt[g * HEAD : (g + 1) * HEAD].astype(BF16)
    qkv[zl] = grp[zl]
    kv[x, y, zl] = grp[zl, 2 * HEAD :]
    for k in range(2):
        for cp in ff_loads(k):
            cp.start()
    answer(peers)
    q_rows, k_rows = pl.ds(0, 2 * HEAD), pl.ds(2 * HEAD, 2 * HEAD)
    k_cp = remote(grp.at[1 - zl, k_rows], kv.at[3 - x, 3 - y, zl], pair_send.at[0], pair_recv.at[0], partner)
    q_cp = remote(grp.at[1 - zl, q_rows], qkv.at[zl, q_rows], pair_send.at[4], pair_recv.at[4], partner)
    k_cp.start()

    def gather(n, slot, swap):
        me1, me2 = (y, x) if swap else (x, y)
        r1, l1, r2, l2 = (yr, yl, xr, xl) if swap else (xr, xl, yr, yl)

        def ref(i, j, part=None):
            i, j = lax.rem(i + 4, 4), lax.rem(j + 4, 4)
            v = kv.at[j, i, slot] if swap else kv.at[i, j, slot]
            return v if part is None else v.at[pl.ds(part * HEAD, HEAD)]

        def cp(k, view, dev):
            return remote(view, view, ag_send.at[n, k], ag_recv.at[n, k], dev)

        def stage(base, i, j, di, dj, r, l):
            return dict(
                right=cp(base, ref(i, j), r),
                left=cp(base + 1, ref(i, j), l),
                from_left=cp(base, ref(i - di, j - dj), r),
                from_right=cp(base + 1, ref(i + di, j + dj), l),
                on_right=cp(base + 2, ref(i - di, j - dj, 0), r),
                on_left=cp(base + 3, ref(i + di, j + dj, 1), l),
                from_left2=cp(base + 2, ref(i + 2 * di, j + 2 * dj, 0), r),
                from_right2=cp(base + 3, ref(i + 2 * di, j + 2 * dj, 1), l),
            )

        s1 = stage(0, me1, me2, 1, 0, r1, l1)
        s2 = [stage(4 + 4 * k, me1 + k, me2, 0, 1, r2, l2) for k in range(4)]
        return s1, s2

    def begin(st):
        st["right"].start()
        st["left"].start()

    def hand_on(st):
        st["from_left"].wait_recv()
        st["on_right"].start()
        st["from_right"].wait_recv()
        st["on_left"].start()

    def complete(st):
        st["from_left2"].wait_recv()
        st["from_right2"].wait_recv()

    own, other = gather(0, zl, False), gather(1, 1 - zl, True)
    both = (own, other)
    begin(own[0])
    begin(own[1][0])
    q_cp.start()
    wo_cps = [
        remote(wo, wo_full.at[me_t], w_send.at[0], w_recv.at[0], diagonal),
        remote(wo, wo_full.at[me_t], w_send.at[1], w_recv.at[1], core),
    ]
    for cp in wo_cps:
        cp.start()
    k_there = kv.at[x, y, 1 - zl]
    remote(k_there, k_there, pair_send.at[0], pair_recv.at[0], partner).wait_recv()
    begin(other[0])
    begin(other[1][0])
    q_there = qkv.at[1 - zl, q_rows]
    remote(q_there, q_there, pair_send.at[4], pair_recv.at[4], partner).wait_recv()
    low = place.low_block(x, y)
    for s in range(2):
        base = jnp.where(s == 0, low, 31 - low) * ROWS
        segs = query_segments(ends, base)
        for h in range(2):
            qaug[s, :HEAD, h * ROWS : (h + 1) * ROWS] = qkv[s, h * HEAD : (h + 1) * HEAD]
            qaug[s, HEAD:, h * ROWS : (h + 1) * ROWS] = segs
    peak[...] = jnp.full(peak.shape, -BIG, F32)
    total[...] = jnp.zeros(total.shape, F32)
    acc[...] = jnp.zeros(acc.shape, F32)

    def attend(qs, kx, ky, ks, kbase, causal):
        pair = kv[kx, ky, ks]
        ka = jnp.concatenate([pair[:HEAD], key_segments(ends, kbase)], 0)
        s = dot(ka, qaug[qs], 0, 0)
        if causal:
            key = lax.broadcasted_iota(jnp.int32, (ROWS, 2 * ROWS), 0)
            query = lax.broadcasted_iota(jnp.int32, (ROWS, 2 * ROWS), 1)
            s = jnp.where(key <= jnp.where(query >= ROWS, query - ROWS, query), s, -BIG)
        old = peak[qs]
        new = jnp.maximum(old, jnp.max(s, 0, keepdims=True))
        p = jnp.exp2(s - new)
        fade = jnp.exp2(old - new)
        peak[qs] = new
        total[qs] = total[qs] * fade + jnp.sum(p, 0, keepdims=True)
        acc[qs] = acc[qs] * fade + dot(pair[HEAD:], p.astype(BF16))

    def shard(dx, dy):
        kx, ky = lax.rem(x + dx, 4), lax.rem(y + dy, 4)
        there = place.low_block(kx, ky)
        attend(1, kx, ky, 0, there * ROWS, False)
        sel = jnp.where(there < low, 0, 1)
        attend(sel, kx, ky, sel, jnp.where(there < low, there, 31 - there) * ROWS, False)

    def shards(count, offsets):
        def step(i, carry):
            shard(*offsets(i))
            return carry

        lax.fori_loop(0, count, step, 0)

    attend(0, x, y, 0, low * ROWS, True)
    attend(1, x, y, 1, (31 - low) * ROWS, True)
    attend(1, x, y, 0, low * ROWS, False)
    for s1, s2 in both:
        hand_on(s1)
        begin(s2[3])
        begin(s2[1])
    for s1, s2 in both:
        hand_on(s2[0])
    shards(4, lambda i: ((1 - i // 2) * (2 * i + 1), (i // 2) * (2 * i - 3)))
    for s1, s2 in both:
        complete(s1)
        begin(s2[2])
    for s1, s2 in both:
        hand_on(s2[3])
        hand_on(s2[1])
    shards(4, lambda i: (2 * (i // 2) + 1, 2 * lax.rem(i, 2) + 1))
    for s1, s2 in both:
        complete(s2[0])
        hand_on(s2[2])
    shards(2, lambda i: (2 * i, 2 - 2 * i))
    for s1, s2 in both:
        complete(s2[3])
        complete(s2[1])
    shards(4, lambda i: ((1 - i // 2) * (2 * i + 1) + 2 * (i // 2), (i // 2) * (2 * i - 3) + 2 * (1 - i // 2)))
    for s1, s2 in both:
        complete(s2[2])
    shard(2, 2)
    for s in range(2):
        out = acc[s] / total[s]
        lse[s] = peak[s] + jnp.log2(total[s])
        for h in range(2):
            part = out[:, h * ROWS : (h + 1) * ROWS]
            o[s, h * HEAD : (h + 1) * HEAD] = part
            mine[s, h * HEAD : (h + 1) * HEAD] = part.astype(BF16)

    for s1, s2 in both:
        for st in [s1, *s2]:
            for name in ("right", "left", "on_right", "on_left"):
                st[name].wait_send()
    k_cp.wait_send()
    q_cp.wait_send()

    group = me_t * 2 + zl
    att[group] = mine[zl]
    sends = [
        remote(mine.at[1 - zl], att.at[group], o_send.at[0], o_recv.at[0], partner),
        remote(mine.at[1 - zl], att.at[group], o_send.at[1], o_recv.at[1], far_partner),
        remote(mine.at[zl], att.at[group], o_send.at[2], o_recv.at[2], far),
    ]
    for cp in sends:
        cp.start()
    wo_far = wo_full.at[there_t]
    remote(wo_far, wo_far, w_send.at[0], w_recv.at[0], far).wait_recv()
    wo_relay = remote(wo_far, wo_far, w_send.at[2], w_recv.at[2], core)
    wo_relay.start()
    def load_wo(src, slot):
        pltpu.make_async_copy(src, wo_buf.at[slot], wo_sem.at[slot]).start()

    def wo_ready(slot):
        pltpu.make_async_copy(wo, wo_buf.at[slot], wo_sem.at[slot]).wait()

    def arrived(which, n):
        remote(att.at[which], att.at[which], o_send.at[n], o_recv.at[n], far).wait_recv()

    def relay(which, n):
        cp = remote(att.at[which], att.at[which], o_send.at[n], o_recv.at[n], core)
        cp.start()
        return cp

    def heads_of(t):
        return att[pl.ds(t * 2, 2)].reshape(HEADS_LOCAL, ROWS)

    w1, w2 = wo_full.at[mine_t], wo_full.at[other_t]
    load_wo(wo, 0)
    relays = [relay(group, 3)]
    remote(w1, w1, w_send.at[1], w_recv.at[1], core).wait_recv()
    load_wo(w1, 1)
    arrived(me_t * 2 + 1 - zl, 0)
    relays.append(relay(me_t * 2 + 1 - zl, 4))
    wo_ready(0)
    mixed[...] = dot(heads_of(me_t), wo_buf[0], 0, 0)
    load_wo(wo_far, 0)
    arrived(mine_t * 2 + zl, 3)
    arrived(mine_t * 2 + 1 - zl, 4)
    arrived(there_t * 2 + zl, 2)
    relays.append(relay(there_t * 2 + zl, 5))
    arrived(there_t * 2 + 1 - zl, 1)
    relays.append(relay(there_t * 2 + 1 - zl, 6))
    wo_ready(1)
    mixed[...] = mixed[...] + dot(heads_of(mine_t), wo_buf[1], 0, 0)
    remote(w2, w2, w_send.at[2], w_recv.at[2], core).wait_recv()
    load_wo(w2, 1)
    wo_ready(0)
    back[...] = dot(heads_of(there_t), wo_buf[0], 0, 0)
    load_wo(wo, 0)
    arrived(other_t * 2 + zl, 5)
    arrived(other_t * 2 + 1 - zl, 6)
    wo_ready(1)
    back[...] = back[...] + dot(heads_of(other_t), wo_buf[1], 0, 0)
    mixed[...] = tokens[...].astype(F32) + (mixed[...] + back[...])
    normed_save.wait()
    gain = gain2[...].reshape(1, WIDTH)
    inverse_two = lax.rsqrt(jnp.mean(mixed[...] * mixed[...], -1, keepdims=True) + EPS)
    normed[...] = (mixed[...] * inverse_two * gain).astype(BF16)
    mixed_save = pltpu.make_async_copy(mixed, mixed_out, load_sem.at[1])
    mixed_save.start()

    for k in range(FF_CHUNKS):
        slot, cols = k % 2, slice(k * FF_CHUNK, (k + 1) * FF_CHUNK)
        for cp in ff_loads(k):
            cp.wait()
        both_ff = dot(normed[...], gu_buf[slot])
        gate, upper = both_ff[:, :FF_CHUNK], both_ff[:, FF_CHUNK:]
        hidden_grad = dot(cot[...], d_buf[slot], 1, 1)
        sig = jax.nn.sigmoid(gate)
        silu = gate * sig
        hid = (silu * upper).astype(BF16)
        gg = (hidden_grad * upper * sig * (1.0 + gate * (1.0 - sig))).astype(BF16)
        ug = (hidden_grad * silu).astype(BF16)
        hidden[:, cols], gate_grad[:, cols], upper_grad[:, cols] = hid, gg, ug
        add_back = dot(jnp.concatenate([gg, ug], 1), gu_buf[slot], 1, 1)
        add_feed = dot(hid, d_buf[slot])
        if k == 0:
            mixed_save.wait()
            back[...], mixed[...] = add_back, add_feed
        else:
            back[...] = back[...] + add_back
            mixed[...] = mixed[...] + add_feed
        if k + 2 < FF_CHUNKS:
            for cp in ff_loads(k + 2):
                cp.start()
    part3[...] = ar_view(back[...].astype(BF16))
    sum3 = TpSum(place, part3, buf3, (send3, recv3))
    sum3.start()
    feed_out[...] = ar_view(mixed[...].astype(BF16))
    mixed_load = pltpu.make_async_copy(mixed_out, mixed, load_sem.at[1])
    mixed_load.start()

    def weight_grad(rhs, lo, cb=0):
        w = rhs.shape[1 - cb]

        def slab(i, carry):
            piece = dot(left[pl.ds(pl.multiple_of(i * 192, 192), 192)], rhs[...], 1, cb)
            grads[i // 4, i % 4, :, :, lo : lo + w] = piece.astype(BF16).reshape(4, 48, w)
            return carry

        lax.fori_loop(0, 8, slab, 0)

    groups, blo = {}, dict(plane=0, depth=0)
    for n, (name, kind, first, slo, w, glo) in enumerate(PLAN):
        if kind == "plane":
            piece = PlaneSum(place, first, grads, glo, blo[kind], slo, w, (b1, r1, b2, r2, zb), (gsend, grecv), n, sums)
        else:
            piece = DepthSum(place, first, grads, glo, blo[kind], slo, w, (z0, b1z, r1z, b2z), (gsend, grecv), n, sums)
        blo[kind] += w
        groups.setdefault(name, []).append(piece)
    pieces = [p for group_ in groups.values() for p in group_]

    def go(*names):
        for name in names:
            for piece in groups[name]:
                piece.next()

    left[...] = cot[...].T
    weight_grad(hidden, 2 * FFL)
    go("down")
    sum3.mid()
    left[...] = normed[...].T
    weight_grad(gate_grad, 0)
    go("gate")
    weight_grad(upper_grad, FFL)
    go("up")
    sum2 = TpSum(place, feed_out, buf2, (send2, recv2))
    sum2.start()
    for s in range(2):
        for h in range(2):
            dot_t[s, :, h * ROWS : (h + 1) * ROWS] = jnp.zeros((HEAD, ROWS), BF16)
    acc[...] = jnp.zeros(acc.shape, F32)
    dq = acc
    mixed_load.wait()
    go("down")
    sum3.fin()
    go("down_z", "gate_z", "up_z")
    sum3.landed()
    mixed_part, ffn_gain_grad = norm_back(mixed[...], inverse_two, gain, ar_load(part3).astype(F32))
    gain_sum[0, 1:2] = ffn_gain_grad
    back[...] = cot[...].astype(F32) + mixed_part
    normed[...] = back[...].astype(BF16)
    wo_ready(0)
    own_grad = dot(wo_buf[0], normed[...], 1, 1).astype(BF16)
    dgrp[0] = own_grad[: 2 * HEAD]
    dgrp[1] = own_grad[2 * HEAD :]
    grad_cp = remote(dgrp.at[1 - zl], dout.at[zl], pair_send.at[1], pair_recv.at[1], partner)
    grad_cp.start()
    dout[zl] = dgrp[zl]
    left[...] = normed[...].T
    weight_grad(heads_of(me_t), W_FFN, 1)
    go("out")
    normed_load = pltpu.make_async_copy(normed_out, normed, load_sem.at[0])
    normed_load.start()
    for cp in projections():
        cp.start()
    go("gate")
    grad_cp.wait_recv()
    for s in range(2):
        for h in range(2):
            lanes, feats = slice(h * ROWS, (h + 1) * ROWS), slice(h * HEAD, (h + 1) * HEAD)
            d = dout[s, feats]
            dot_t[s, :, lanes] = d
            delta[s, :, lanes] = jnp.sum(d.astype(F32) * o[s, feats], 0, keepdims=True)

    def attend_back(qs, kx, ky, ks, kbase, causal):
        pair = kv[kx, ky, ks]
        q = qaug[qs]
        do = dot_t[qs]
        ka = jnp.concatenate([pair[:HEAD], key_segments(ends, kbase)], 0)
        s = dot(ka, q, 0, 0)
        p = jnp.exp2(s - lse[qs])
        if causal:
            key = lax.broadcasted_iota(jnp.int32, (ROWS, 2 * ROWS), 0)
            query = lax.broadcasted_iota(jnp.int32, (ROWS, 2 * ROWS), 1)
            p = jnp.where(key <= jnp.where(query >= ROWS, query - ROWS, query), p, 0.0)
        dp = dot(pair[HEAD:], do, 0, 0)
        ds = (p * (dp - delta[qs])).astype(BF16)
        dq[qs] = dq[qs] + dot(pair[:HEAD], ds)
        dk = dot(q[:HEAD], ds, 1, 1)
        dv = dot(do, p.astype(BF16), 1, 1)
        return jnp.concatenate([dk, dv], 0)

    def shard_back(dx, dy):
        kx, ky = lax.rem(x + dx, 4), lax.rem(y + dy, 4)
        there = place.low_block(kx, ky)
        one = attend_back(1, kx, ky, 0, there * ROWS, False)
        before = there < low
        sel = jnp.where(before, 0, 1)
        two = attend_back(sel, kx, ky, sel, jnp.where(before, there, 31 - there) * ROWS, False)
        share = jnp.where(before, 1.0, 0.0)
        kv[kx, ky, 0] = (one + two * share).astype(BF16)
        kv[kx, ky, 1] = (two * (1.0 - share)).astype(BF16)

    def shards_back(count, offsets, events):
        def step(i, carry):
            shard_back(*offsets(i))
            for at, event in events:
                pl.when(i == at)(event)
            return carry

        lax.fori_loop(0, count, step, 0)

    def key_sum(slot, axis):
        other_axis = "y" if axis == "x" else "x"
        if axis == "x":
            half = lambda d, h: kv.at[d, :, slot, pl.ds(h * HEAD, HEAD)]
        else:
            half = lambda d, h: kv.at[:, d, slot, pl.ds(h * HEAD, HEAD)]
        one = RingSum(
            place, axis, half, lambda k: kb1.at[slot, k], lambda h: kr1.at[slot, h],
            lambda k: ksend.at[slot, k], lambda k: krecv.at[slot, k],
        )
        two = RingSum(
            place, other_axis, lambda d, h: kr1.at[slot, h, d], lambda k: kb2.at[slot, k],
            lambda h: kr2.at[slot, h], lambda k: ksend.at[slot, 6 + k], lambda k: krecv.at[slot, 6 + k],
        )
        return one, two

    ka, kb = key_sum(0, "x"), key_sum(1, "y")

    def two_away(i):
        k, j = i // 4, i - 4
        return (1 - k) * 2 + k * (j + j // 2), (1 - k) * i + k * 2

    def one_away(i):
        k, j = i // 4, i - 4
        along_x = (1 - j // 2) * (2 * j + 1)
        along_y = (j // 2) * (2 * j - 3)
        dx = (1 - k) * (2 * (i // 2) + 1) + k * along_x
        dy = (1 - k) * (2 * lax.rem(i, 2) + 1) + k * along_y
        return dx, dy

    shards_back(7, two_away, [(0, lambda: go("up", "out")), (3, lambda: go("down")), (6, lambda: go("gate"))])
    ka[0].start_far()
    kb[0].start_far()

    def near(part):
        part.start_near()
        part.mid()

    shards_back(
        8,
        one_away,
        [
            (1, lambda: go("up", "out")),
            (3, lambda: go("down", "down_z")),
            (5, lambda: near(ka[0])),
            (6, lambda: go("gate")),
        ],
    )
    near(kb[0])
    first = attend_back(0, x, y, 0, low * ROWS, True) + attend_back(1, x, y, 0, low * ROWS, False)
    kv[x, y, 0] = first.astype(BF16)
    kv[x, y, 1] = attend_back(1, x, y, 1, (31 - low) * ROWS, True).astype(BF16)

    for s in range(2):
        for h in range(2):
            grp[s, h * HEAD : (h + 1) * HEAD] = (dq[s, :, h * ROWS : (h + 1) * ROWS] * SCALE).astype(BF16)
    dq_cp = remote(grp.at[1 - zl, q_rows], dqkv.at[zl, q_rows], pair_send.at[2], pair_recv.at[2], partner)
    dq_cp.start()
    dqkv[zl, : 2 * HEAD] = grp[zl, : 2 * HEAD]
    go("up", "out", "down", "gate")

    ka[0].fin()
    kb[0].fin()
    ka[1].start()
    kb[1].start()
    go("gate_z", "down_z")
    sum2.mid()

    def unturned(g, h, at):
        a = dqkv[g, h * HEAD : h * HEAD + HALF].astype(F32)
        b = dqkv[g, h * HEAD + HALF : (h + 1) * HEAD].astype(F32)
        if h == 2:
            a, b = a * LN2, b * LN2
        rows[at : at + HALF] = (a * cosine + b * sine).astype(BF16)
        rows[at + HALF : at + HEAD] = (b * cosine - a * sine).astype(BF16)

    dq_there = dqkv.at[1 - zl, q_rows]
    remote(dq_there, dq_there, pair_send.at[2], pair_recv.at[2], partner).wait_recv()
    for g in range(2):
        for h in range(2):
            unturned(g, h, (2 * g + h) * HEAD)
    normed_load.wait()
    for piece in groups["down"]:
        piece.one.end()
    left[...] = normed[...].T
    weight_grad(rows.at[pl.ds(0, HEADS_LOCAL)], 2 * FFL, 1)
    ka[1].mid()
    kb[1].mid()
    go("query")
    for cp in projections():
        cp.wait()
    mixed[...] = dot(rows[:HEADS_LOCAL], gu_buf[0, :, :HEADS_LOCAL], 0, 1)
    go("down_z", "gate_z", "up", "out", "up_z")
    ka[1].fin()
    kb[1].fin()
    for s in range(2):
        for h in range(2):
            grp[s, (2 + h) * HEAD : (3 + h) * HEAD] = kr2[s, h]
    dk_cp = remote(grp.at[1 - zl, k_rows], dqkv.at[zl, k_rows], pair_send.at[3], pair_recv.at[3], partner)
    dk_cp.start()
    dqkv[zl, 2 * HEAD :] = grp[zl, 2 * HEAD :]
    go("down", "gate", "down_z", "gate_z", "query", "up_z", "up", "out")
    for piece in groups["gate"]:
        piece.one.end()
    sum2.fin()
    sum3.end()
    dk_there = dqkv.at[1 - zl, k_rows]
    remote(dk_there, dk_there, pair_send.at[3], pair_recv.at[3], partner).wait_recv()
    for g in range(2):
        unturned(g, 2, HEADS_LOCAL + g * HEAD)
        at = HEADS_LOCAL + PAIRS_LOCAL + g * HEAD
        rows[at : at + HEAD] = dqkv[g, 3 * HEAD :]
    grad_in = mixed[...] + dot(rows[HEADS_LOCAL : HEADS_LOCAL + PAIRS_LOCAL], d_buf[0, :PAIRS_LOCAL], 0, 0)
    grad_in = grad_in + dot(rows[HEADS_LOCAL + PAIRS_LOCAL :], d_buf[1, :PAIRS_LOCAL], 0, 0)
    part3[...] = ar_view(grad_in.astype(BF16))
    sum4 = TpSum(place, part3, buf4, (send4, recv4))
    sum4.start()
    source = tokens[...].astype(F32)
    gain_sum[0, 0:1] = jnp.sum(grad_in * source * inverse, 0, keepdims=True)
    gain_sum[0, 1:2] = 0.25 * gain_sum[0, 1:2]
    gain_sent = []

    def gain_step(stage):
        if stage:
            came = gain_sum[stage - 1]
            for k, cp in enumerate(gain_sent[-1]):
                cp.wait_recv()
                came = came + gain_buf[stage - 1, k]
            gain_sum[stage] = came
        if stage < 5:
            there = [
                [place.along("x", k) for k in (1, 2, 3)], [place.along("y", k) for k in (1, 2, 3)],
                [place.at(zl=1 - zl)], [far], [core],
            ][stage]
            gain_sent.append(
                [
                    remote(gain_sum.at[stage], gain_buf.at[stage, k], gn_send.at[stage, k], gn_recv.at[stage, k], peer)
                    for k, peer in enumerate(there)
                ]
            )
            for cp in gain_sent[-1]:
                cp.start()

    gain_step(0)
    weight_grad(rows.at[pl.ds(HEADS_LOCAL, 2 * PAIRS_LOCAL)], 0, 1)
    go("pair", "down_z", "gate_z")
    sum4.mid()
    gain_step(1)
    go("query", "up_z", "pair")
    gain_step(2)
    go("gate_z", "query", "up_z")
    gain_step(3)
    go("pair")
    sum4.fin()
    gain_step(4)
    go("up_z", "query", "pair")
    sum4.landed()
    source_part, _ = norm_back(tokens[...].astype(F32), inverse, gain1[...].reshape(1, WIDTH), ar_load(part3).astype(F32))
    tokens_grad[...] = (back[...] + source_part).astype(BF16)
    gain_step(5)
    gains[...] = gain_sum[5]
    go("pair", "query", "pair")
    sum2.landed()
    for cp in [grad_cp, dq_cp, dk_cp, *wo_cps, wo_relay, *sends, *relays, *sum(gain_sent, [])]:
        cp.wait_send()
    sum2.end()
    sum4.end()
    for piece in pieces:
        assert piece.at == len(piece.steps)
        piece.end()
    for one, two in (ka, kb):
        one.end()
        two.end()


def layer(lengths, freq, tokens, cot, gain1, gain2, wq, wkt, wvt, wo, wg, wu, wd):
    vm = pl.BlockSpec(memory_space=pltpu.VMEM)
    hbm = pl.BlockSpec(memory_space=pl.ANY)
    dma = pltpu.SemaphoreType.DMA
    shape = (2, AR_PIECES, AR_ROWS, WIDTH)
    group = pltpu.VMEM((2, 4 * HEAD, ROWS), BF16)
    two_heads = pltpu.VMEM((2, 2 * HEAD, ROWS), BF16)
    line = pltpu.VMEM((2, 1, 2 * ROWS), F32)
    return pl.pallas_call(
        layer_kernel,
        out_shape=(
            jax.ShapeDtypeStruct((ROWS, WIDTH), F32),
            jax.ShapeDtypeStruct((ROWS, WIDTH), BF16),
            jax.ShapeDtypeStruct((4, HEADS_LOCAL, WIDTH), BF16),
            jax.ShapeDtypeStruct(shape, BF16),
            jax.ShapeDtypeStruct((ROWS, WIDTH), BF16),
            jax.ShapeDtypeStruct((48, W_ALL), F32),
            jax.ShapeDtypeStruct((2, WIDTH), F32),
        ),
        in_specs=[pl.BlockSpec(memory_space=pltpu.SMEM)] + [vm] * 5 + [hbm] * 7,
        out_specs=(hbm, hbm, hbm, vm, vm, vm, vm),
        scratch_shapes=[
            pltpu.VMEM((2, HEADS_LOCAL, WIDTH), BF16),
            pltpu.VMEM((2, WIDTH, 2 * FF_CHUNK), BF16),
            pltpu.VMEM((2, FF_CHUNK, WIDTH), BF16),
            pltpu.VMEM((ROWS, WIDTH), F32),
            pltpu.VMEM((ROWS, WIDTH), F32),
            pltpu.VMEM((ROWS, WIDTH), BF16),
            pltpu.VMEM((ROWS, FFL), BF16),
            pltpu.VMEM((ROWS, FFL), BF16),
            pltpu.VMEM((ROWS, FFL), BF16),
            pltpu.VMEM((WIDTH, ROWS), BF16),
            pltpu.VMEM((2, 4, 4, 48, W_MID), BF16),
            pltpu.VMEM((6, 4, 48, W_PLANE), BF16),
            pltpu.VMEM((2, 4, 48, W_PLANE), BF16),
            pltpu.VMEM((6, 48, W_PLANE), BF16),
            pltpu.VMEM((2, 48, W_PLANE), BF16),
            pltpu.VMEM((48, W_PLANE), BF16),
            pltpu.VMEM((4, 4, 48, W_DEPTH), BF16),
            pltpu.VMEM((6, 4, 48, W_DEPTH // 2), BF16),
            pltpu.VMEM((4, 48, W_DEPTH), BF16),
            pltpu.VMEM((6, 48, W_DEPTH // 2), BF16),
            dma((len(PLAN), 13)),
            dma((len(PLAN), 13)),
            pltpu.VMEM(shape, BF16),
            *tp_scratch(),
            *tp_scratch(),
            *tp_scratch(),
            pltpu.VMEM((4, 4, 2, 2 * HEAD, ROWS), BF16),
            pltpu.VMEM((2, 6, 4, HEAD, ROWS), BF16),
            pltpu.VMEM((2, 2, 4, HEAD, ROWS), BF16),
            pltpu.VMEM((2, 6, HEAD, ROWS), BF16),
            pltpu.VMEM((2, 2, HEAD, ROWS), BF16),
            dma((2, 12)),
            dma((2, 12)),
            group,
            group,
            pltpu.VMEM((8, 2 * HEAD, ROWS), BF16),
            pltpu.VMEM((2, 2 * HEAD, ROWS), F32),
            line,
            pltpu.VMEM((2, HEAD + SEG, 2 * ROWS), BF16),
            pltpu.VMEM((2, HEAD, 2 * ROWS), F32),
            line,
            line,
            two_heads,
            two_heads,
            two_heads,
            pltpu.VMEM((2, HEAD, 2 * ROWS), BF16),
            line,
            group,
            pltpu.VMEM((W_TAIL, ROWS), BF16),
            pltpu.VMEM((6, 2, WIDTH), F32),
            pltpu.VMEM((5, 3, 2, WIDTH), F32),
            dma((5, 3)),
            dma((5, 3)),
            dma((5,)),
            dma((5,)),
            dma((2, 20)),
            dma((2, 20)),
            dma((7,)),
            dma((7,)),
            dma((3,)),
            dma((3,)),
            dma((2,)),
            dma((2, 3)),
            dma((2,)),
        ],
        compiler_params=pltpu.CompilerParams(
            collective_id=0, has_side_effects=True, vmem_limit_bytes=VMEM_LIMIT
        ),
        name="layer",
    )(lengths, freq, tokens, cot, gain1, gain2, wq, wkt, wvt, wo, wg, wu, wd)


def finish_kernel(
    mixed, feed, tokens_grad, sums, gains,
    result, tokens_grad_out, norm_gain, query, key, value, out, ffn_gain, gate, up, down,
):
    result[...] = (mixed[...] + ar_load(feed).astype(F32)).astype(BF16)
    tokens_grad_out[...] = tokens_grad[...]
    block = (lax.axis_index("zl") * 4 + lax.axis_index("x")) * 4 + lax.axis_index("y")
    own = jnp.zeros((2, 48), F32)
    for b in range(32):
        own = own + jnp.where(block == b, gains[:, 48 * b : 48 * b + 48], 0.0)
    norm_gain[...] = own[0:1]
    ffn_gain[...] = own[1:2]
    gate[...] = sums[:, :FFL]
    up[...] = sums[:, FFL : 2 * FFL]
    down[...] = sums[:, 2 * FFL : W_FFN]
    out[...] = sums[:, W_FFN:W_MID]
    query[...] = sums[:, W_MID : W_MID + HEADS_LOCAL]
    key[...] = sums[:, W_MID + HEADS_LOCAL : W_MID + HEADS_LOCAL + PAIRS_LOCAL]
    value[...] = sums[:, W_MID + HEADS_LOCAL + PAIRS_LOCAL :]


def finish(mixed, feed, tokens_grad, sums, gains):
    vm = pl.BlockSpec(memory_space=pltpu.VMEM)
    shapes = [(ROWS, WIDTH)] * 2 + [
        (1, 48), (48, HEADS_LOCAL), (48, PAIRS_LOCAL), (48, PAIRS_LOCAL), (48, HEADS_LOCAL), (1, 48),
        (48, FFL), (48, FFL), (48, FFL),
    ]
    return pl.pallas_call(
        finish_kernel,
        out_shape=[jax.ShapeDtypeStruct(s, BF16 if n < 2 else F32) for n, s in enumerate(shapes)],
        in_specs=[vm] * 5,
        out_specs=[vm] * len(shapes),
        compiler_params=pltpu.CompilerParams(vmem_limit_bytes=VMEM_LIMIT),
        name="finish",
    )(mixed, feed, tokens_grad, sums, gains)


def local(
    tokens, norm_gain, query_weight, key_matrix, value_matrix, out_weight,
    ffn_gain, gate_weight, up_weight, down_weight, cotangent, lengths,
):
    freq = jnp.asarray(
        (THETA ** (-2.0 * np.arange(HALF) / HEAD)).astype(np.float32).reshape(HALF, 1)
    )
    mixed, _, _, feed, tokens_grad, sums, gains = layer(
        lengths, freq, tokens, cotangent, norm_gain, ffn_gain, query_weight, key_matrix.T, value_matrix.T,
        out_weight, gate_weight, up_weight, down_weight,
    )
    result, tokens_grad, norm_gain_grad, query, key, value, out, ffn_gain_grad, gate, up, down = finish(
        mixed, feed, tokens_grad, sums, gains
    )
    return (
        result, tokens_grad, norm_gain_grad.reshape(48), query, key, value, out.T,
        ffn_gain_grad.reshape(48), gate, up, down.T,
    )


def solution(mesh):
    split = Mesh(mesh.devices.reshape(2, 4, 4, 2, 2), AXES)
    in_specs = (
        P(BLK, None),
        P(),
        P(None, TP),
        P(None, TP),
        P(None, TP),
        P(TP, None),
        P(),
        P(None, TP),
        P(None, TP),
        P(TP, None),
        P(BLK, None),
        P(),
    )
    out_specs = (
        P(BLK, None),
        P(BLK, None),
        P(BLK),
        P(BLK, TP),
        P(BLK, TP),
        P(BLK, TP),
        P(TP, BLK),
        P(BLK),
        P(BLK, TP),
        P(BLK, TP),
        P(TP, BLK),
    )
    return jax.shard_map(local, mesh=split, in_specs=in_specs, out_specs=out_specs, check_vma=False)
```

```python
import jax
import jax.numpy as jnp
import numpy as np
from jax import lax
from jax.experimental import pallas as pl
from jax.experimental.pallas import tpu as pltpu
from jax.sharding import Mesh
from jax.sharding import PartitionSpec as P

AXES = ("zl", "x", "y", "zh", "c")
BLK = ("zl", "x", "y")
TP = ("zh", "c")
HEAD = 96
HALF = HEAD // 2
ROWS = 256
WIDTH = 1536
HEADS_LOCAL = 384
PAIRS_LOCAL = 192
FFL = 1024
EPS = 1e-05
THETA = 100000.0
SCALE = HEAD**-0.5
LOG2E = float(np.log2(np.e))
LN2 = float(np.log(2.0))
BIG = 1e30
SEG = 16
MESH = pl.DeviceIdType.MESH
F32 = jnp.float32
BF16 = jnp.bfloat16
VMEM_LIMIT = 63 * 2**20


def dot(a, b, ca=1, cb=0):
    return lax.dot_general(a, b, (((ca,), (cb,)), ((), ())), preferred_element_type=F32)


class Place:
    def __init__(self):
        self.zl, self.x, self.y, self.zh, self.c = (lax.axis_index(a) for a in AXES)

    def at(self, **changes):
        own = dict(zl=self.zl, x=self.x, y=self.y, zh=self.zh, c=self.c)
        own.update(changes)
        return tuple(own[a] for a in AXES)

    def along(self, axis, step):
        return self.at(**{axis: lax.rem(getattr(self, axis) + (step + 4), 4)})

    @property
    def pair(self):
        return dict(zl=1 - self.zl, x=3 - self.x, y=3 - self.y)

    def low_block(self, x, y):
        p = x * 4 + y
        return jnp.where(self.zl == 0, p, 15 - p)


def call(peers):
    barrier = pltpu.get_barrier_semaphore()
    for peer in peers:
        pl.semaphore_signal(barrier, inc=1, device_id=peer, device_id_type=MESH)


def answer(peers):
    pl.semaphore_wait(pltpu.get_barrier_semaphore(), len(peers))


def remote(src, dst, send, recv, device):
    return pltpu.make_async_remote_copy(
        src_ref=src, dst_ref=dst, send_sem=send, recv_sem=recv, device_id=device, device_id_type=MESH
    )


def seg_rows(ends, base):
    token = base + lax.broadcasted_iota(jnp.int32, (SEG, ROWS), 1)
    row = lax.broadcasted_iota(jnp.int32, (SEG, ROWS), 0)
    inside = jnp.zeros((SEG, ROWS), F32)
    start = 0
    for d in range(5):
        hit = (row == d) & (token >= start) & (token < ends[d])
        inside = jnp.where(hit, 1.0, inside)
        start = ends[d]
    return inside, row


def key_segments(ends, base):
    return seg_rows(ends, base)[0].astype(BF16)


def query_segments(ends, base):
    inside, row = seg_rows(ends, base)
    return jnp.where(row < 5, (inside - 1.0) * BIG, 0.0).astype(BF16)


def ends_of(lengths_ref):
    ends, total = [], 0
    for d in range(5):
        total = total + lengths_ref[d]
        ends.append(total)
    return ends


def rotation(ends, lengths_ref, base, freq):
    token = base + lax.broadcasted_iota(jnp.int32, (1, ROWS), 1)
    begin = jnp.zeros((1, ROWS), jnp.int32)
    for d in range(5):
        begin = begin + jnp.where(token >= ends[d], lengths_ref[d], 0)
    angle = (token - begin).astype(F32) * freq
    return jnp.cos(angle), jnp.sin(angle)


class RingSum:
    def __init__(self, place, axis, half, bufs, out, send, recv):
        self.half, self.bufs, self.out = half, bufs, out
        me = getattr(place, axis)
        self.me = me
        self.r, self.l, self.o = (lax.rem(me + k, 4) for k in (1, 3, 2))
        self.right, self.left = place.along(axis, 1), place.along(axis, -1)
        self.send, self.recv = send, recv
        self.ended = False

    def cp(self, k):
        src = (
            lambda: self.half(self.o, 0),
            lambda: self.half(self.o, 1),
            lambda: self.half(self.r, 1),
            lambda: self.half(self.l, 0),
            lambda: self.bufs(0),
            lambda: self.bufs(1),
        )[k]()
        return remote(src, self.bufs(k), self.send(k), self.recv(k), (self.right, self.left)[k % 2])

    def start_far(self):
        self.cp(0).start()
        self.cp(1).start()

    def start_near(self):
        self.cp(2).start()
        self.cp(3).start()

    def start(self):
        self.start_far()
        self.start_near()

    def mid(self):
        self.cp(0).wait_recv()
        add_two(self.bufs(0), self.half(self.r, 0))
        self.cp(4).start()
        self.cp(1).wait_recv()
        add_two(self.bufs(1), self.half(self.l, 1))
        self.cp(5).start()

    def fin(self):
        self.cp(4).wait_recv()
        self.cp(3).wait_recv()
        add_three(self.out(0), self.half(self.me, 0), self.bufs(4), self.bufs(3))
        self.cp(5).wait_recv()
        self.cp(2).wait_recv()
        add_three(self.out(1), self.half(self.me, 1), self.bufs(5), self.bufs(2))

    def end(self):
        if not self.ended:
            self.ended = True
            for k in range(6):
                self.cp(k).wait_send()


def add_two(dst, src):
    if len(dst.shape) == 3:
        for i in range(dst.shape[0]):
            dst[i] = dst[i] + src[i]
    else:
        dst[...] = dst[...] + src[...]


def add_three(out, a, b, d):
    if len(out.shape) == 3:
        for i in range(out.shape[0]):
            out[i] = (a[i].astype(F32) + b[i].astype(F32) + d[i].astype(F32)).astype(out.dtype)
    else:
        out[...] = (a[...].astype(F32) + b[...].astype(F32) + d[...].astype(F32)).astype(out.dtype)


class Steps:
    at = 0

    def next(self):
        self.steps[self.at]()
        self.at += 1


class PlaneSum(Steps):
    def __init__(self, place, first, g, glo, blo, slo, w, bufs, sems, n, sums):
        b1, r1, b2, r2, zb = bufs
        send, recv = sems
        gc, bc = pl.ds(glo, w), pl.ds(blo, w)
        self.place, self.r2, self.zb, self.bc, self.sc = place, r2, zb, bc, slice(slo, slo + w)
        self.send, self.recv, self.n, self.sums = send, recv, n, sums
        if first == "x":
            half1 = lambda d, h: g.at[h, d, :, :, gc]
        else:
            half1 = lambda d, h: g.at[h, :, d, :, gc]
        self.one = RingSum(
            place, first, half1, lambda k: b1.at[k, :, :, bc], lambda h: r1.at[h, :, :, bc],
            lambda k: send.at[n, k], lambda k: recv.at[n, k],
        )
        self.two = RingSum(
            place, "y" if first == "x" else "x", lambda d, h: r1.at[h, d, :, bc], lambda k: b2.at[k, :, bc],
            lambda h: r2.at[h, :, bc], lambda k: send.at[n, 6 + k], lambda k: recv.at[n, 6 + k],
        )
        self.steps = [self.one.start, self.one.mid, self.turn, self.two.mid, self.cross, self.total]

    def zcp(self):
        other = 1 - self.place.zl
        return remote(
            self.r2.at[other, :, self.bc], self.zb.at[:, self.bc], self.send.at[self.n, 12],
            self.recv.at[self.n, 12], self.place.at(zl=other),
        )

    def turn(self):
        self.one.fin()
        self.two.start()

    def cross(self):
        self.two.fin()
        self.zcp().start()

    def total(self):
        self.zcp().wait_recv()
        own = self.r2[self.place.zl, :, self.bc].astype(F32)
        self.sums[:, self.sc] = own + self.zb[:, self.bc].astype(F32)

    def end(self):
        self.one.end()
        self.two.end()
        self.zcp().wait_send()


class DepthSum(Steps):
    def __init__(self, place, first, g, glo, blo, slo, w, bufs, sems, n, sums):
        z0, b1, r1, b2 = bufs
        send, recv = sems
        h_w = w // 2
        self.place, self.g, self.z0 = place, g, z0
        self.gc, self.zc = pl.ds(glo, w), pl.ds(blo, w)
        self.send, self.recv, self.n = send, recv, n
        zl = place.zl
        part = lambda lo, h: pl.ds(lo + h * h_w, h_w)
        if first == "x":
            half1 = lambda d, h: g.at[zl, d, :, :, part(glo, h)]
        else:
            half1 = lambda d, h: g.at[zl, :, d, :, part(glo, h)]
        bc = pl.ds(blo // 2, h_w)
        self.one = RingSum(
            place, first, half1, lambda k: b1.at[k, :, :, bc], lambda h: r1.at[:, :, part(blo, h)],
            lambda k: send.at[n, k], lambda k: recv.at[n, k],
        )
        self.two = RingSum(
            place, "y" if first == "x" else "x", lambda d, h: r1.at[d, :, part(blo, h)], lambda k: b2.at[k, :, bc],
            lambda h: sums.at[:, part(slo, h)], lambda k: send.at[n, 6 + k], lambda k: recv.at[n, 6 + k],
        )
        self.steps = [self.cross, self.join, self.one.mid, self.turn, self.two.mid, self.two.fin]

    def zcp(self):
        other = 1 - self.place.zl
        return remote(
            self.g.at[other, :, :, :, self.gc], self.z0.at[:, :, :, self.zc], self.send.at[self.n, 12],
            self.recv.at[self.n, 12], self.place.at(zl=other),
        )

    def cross(self):
        self.zcp().start()

    def join(self):
        self.zcp().wait_recv()
        mine = self.g.at[self.place.zl, :, :, :, self.gc]
        came = self.z0.at[:, :, :, self.zc]

        def add(i, carry):
            for j in range(4):
                mine[i, j] = mine[i, j] + came[i, j]
            return carry

        lax.fori_loop(0, 4, add, 0)
        self.one.start()

    def turn(self):
        self.one.fin()
        self.two.start()

    def end(self):
        self.one.end()
        self.two.end()
        self.zcp().wait_send()


AR_PIECES = 2
AR_ROWS = ROWS // 2 // AR_PIECES


class TpSum:
    def __init__(self, place, part, buf, sems):
        self.place, self.part, self.buf = place, part, buf
        self.send, self.recv = sems
        self.core = place.at(c=1 - place.c)
        self.far = place.at(zh=1 - place.zh)

    def a(self, k):
        return remote(
            self.part.at[1 - self.place.c, k], self.buf.at[0, k], self.send.at[0, k], self.recv.at[0, k], self.core
        )

    def b(self, k):
        return remote(self.buf.at[0, k], self.buf.at[1, k], self.send.at[1, k], self.recv.at[1, k], self.far)

    def d(self, k):
        return remote(
            self.part.at[self.place.c, k], self.buf.at[2, k], self.send.at[2, k], self.recv.at[2, k], self.core
        )

    def start(self):
        for k in range(AR_PIECES):
            self.a(k).start()

    def mid(self):
        for k in range(AR_PIECES):
            self.a(k).wait_recv()
            self.buf[0, k] = self.buf[0, k] + self.part[self.place.c, k]
            self.b(k).start()

    def fin(self):
        for k in range(AR_PIECES):
            self.b(k).wait_recv()
            self.part[self.place.c, k] = self.buf[0, k] + self.buf[1, k]
            self.d(k).start()

    def landed(self):
        for k in range(AR_PIECES):
            self.a(k).wait_send()
            self.d(k).wait_recv()
            self.part[1 - self.place.c, k] = self.buf[2, k]

    def end(self):
        for k in range(AR_PIECES):
            self.b(k).wait_send()
            self.d(k).wait_send()


def tp_scratch():
    return [
        pltpu.VMEM((3, AR_PIECES, AR_ROWS, WIDTH), BF16),
        pltpu.SemaphoreType.DMA((3, AR_PIECES)),
        pltpu.SemaphoreType.DMA((3, AR_PIECES)),
    ]


def ar_view(value):
    return value.reshape(2, AR_PIECES, AR_ROWS, WIDTH)


def ar_load(ref):
    return ref[...].reshape(ROWS, WIDTH)


def norm_back(source, inverse, gain, grad):
    scaled = grad * gain
    gain_grad = jnp.sum(grad * source * inverse, 0, keepdims=True)
    mean = jnp.mean(scaled * source, -1, keepdims=True)
    return inverse * scaled - source * (inverse * inverse * inverse) * mean, gain_grad


W_FFN = 3 * FFL
W_MID = W_FFN + HEADS_LOCAL
W_TAIL = HEADS_LOCAL + 2 * PAIRS_LOCAL
W_ALL = W_MID + W_TAIL
FF_CHUNKS = 4
FF_CHUNK = FFL // FF_CHUNKS

PLAN = [
    ("down", "plane", "x", 2048, 256, 2048),
    ("down", "plane", "y", 2304, 256, 2304),
    ("down_z", "depth", "x", 2560, 256, 2560),
    ("down_z", "depth", "y", 2816, 256, 2816),
    ("gate", "plane", "x", 0, 256, 0),
    ("gate", "plane", "y", 256, 256, 256),
    ("gate_z", "depth", "x", 512, 256, 512),
    ("gate_z", "depth", "y", 768, 256, 768),
    ("up", "plane", "x", 1024, 384, 1024),
    ("up", "plane", "y", 1408, 384, 1408),
    ("up_z", "depth", "y", 1792, 256, 1792),
    ("out", "plane", "x", 3072, 128, 3072),
    ("out", "plane", "y", 3200, 256, 3200),
    ("query", "plane", "x", 3456, 256, 2048),
    ("query", "plane", "y", 3712, 128, 2304),
    ("pair", "plane", "x", 3840, 128, 0),
    ("pair", "plane", "y", 3968, 256, 128),
]
W_PLANE = sum(p[4] for p in PLAN if p[1] == "plane")
W_DEPTH = sum(p[4] for p in PLAN if p[1] == "depth")


def layer_kernel(
    lengths, freq, tokens, cot, gain1, gain2, wq, wkt, wvt, wo, wg, wu, wd,
    mixed_out, normed_out, wo_full, feed_out, tokens_grad, sums, gains,
    wo_buf, gu_buf, d_buf, mixed, back, normed, hidden, back_hidden, gate_grad, upper_grad, left, grads,
    b1, r1, b2, r2, zb, z0, b1z, r1z, b2z, gsend, grecv,
    part3, buf3, send3, recv3, buf2, send2, recv2, buf4, send4, recv4,
    kv, kb1, kr1, kb2, kr2, ksend, krecv,
    grp, qkv, att, o, lse, qaug, acc, peak, total, mine, dgrp, dout, dot_t, delta, dqkv, rows,
    gain_sum, gain_buf, gn_send, gn_recv,
    pair_send, pair_recv, ag_send, ag_recv, o_send, o_recv, w_send, w_recv, load_sem, ff_sem, wo_sem,
):
    place = Place()
    zl, x, y, zh, c = place.zl, place.x, place.y, place.zh, place.c
    partner = place.at(**place.pair)
    far_partner = place.at(**place.pair, zh=1 - zh)
    far = place.at(zh=1 - zh)
    core = place.at(c=1 - c)
    diagonal = place.at(zl=1 - zl, zh=1 - zh)
    xr, xl, yr, yl = place.along("x", 1), place.along("x", -1), place.along("y", 1), place.along("y", -1)
    peers = [partner, far_partner, far, core, diagonal, place.at(zl=1 - zl), xr, xl, yr, yl]
    peers += [place.along("x", 2), place.along("y", 2)]
    call(peers)
    me_t = zh * 2 + c
    there_t = (1 - zh) * 2 + c
    mine_t, other_t = zh * 2 + (1 - c), (1 - zh) * 2 + (1 - c)

    def projections():
        return [
            pltpu.make_async_copy(wq, gu_buf.at[0, :, pl.ds(0, HEADS_LOCAL)], ff_sem.at[0, 0]),
            pltpu.make_async_copy(wkt, d_buf.at[0, pl.ds(0, PAIRS_LOCAL)], ff_sem.at[0, 1]),
            pltpu.make_async_copy(wvt, d_buf.at[1, pl.ds(0, PAIRS_LOCAL)], ff_sem.at[0, 2]),
        ]

    def ff_loads(k):
        slot, cols = k % 2, pl.ds(k * FF_CHUNK, FF_CHUNK)
        return [
            pltpu.make_async_copy(wg.at[:, cols], gu_buf.at[slot, :, pl.ds(0, FF_CHUNK)], ff_sem.at[slot, 0]),
            pltpu.make_async_copy(wu.at[:, cols], gu_buf.at[slot, :, pl.ds(FF_CHUNK, FF_CHUNK)], ff_sem.at[slot, 1]),
        ]

    def down_load(k):
        rows_ = pl.ds(k * FF_CHUNK, FF_CHUNK)
        return pltpu.make_async_copy(wd.at[rows_], d_buf.at[k % 2], ff_sem.at[k % 2, 2])

    def hidden_back(k):
        down_load(k).wait()
        back_hidden[:, k * FF_CHUNK : (k + 1) * FF_CHUNK] = dot(cot[...], d_buf[k % 2], 1, 1).astype(BF16)
        down_load((k + 2) % 4).start()

    for cp in projections():
        cp.start()
    ends = ends_of(lengths)
    block = zl * 16 + x * 4 + y
    source = tokens[...].astype(F32)
    inverse = lax.rsqrt(jnp.mean(source * source, -1, keepdims=True) + EPS)
    normed[...] = (source * inverse * gain1[...].reshape(1, WIDTH)).astype(BF16)
    normed_save = pltpu.make_async_copy(normed, normed_out, load_sem.at[0])
    normed_save.start()
    cosine, sine = rotation(ends, lengths, block * ROWS, freq[...])

    def turned(u, factor):
        a, b = u[:HALF], u[HALF:]
        if factor is None:
            return a * cosine - b * sine, b * cosine + a * sine
        return (a * cosine - b * sine) * factor, (b * cosine + a * sine) * factor

    for cp in projections():
        cp.wait()
    kt = dot(d_buf[0, :PAIRS_LOCAL], normed[...], 1, 1)
    vt = dot(d_buf[1, :PAIRS_LOCAL], normed[...], 1, 1)
    qt = dot(normed[...], gu_buf[0, :, :HEADS_LOCAL]).T
    for g in range(2):
        for h in range(2):
            a, b = turned(qt[(2 * g + h) * HEAD : (2 * g + h + 1) * HEAD], SCALE * LOG2E)
            grp[g, h * HEAD : h * HEAD + HALF] = a.astype(BF16)
            grp[g, h * HEAD + HALF : (h + 1) * HEAD] = b.astype(BF16)
        a, b = turned(kt[g * HEAD : (g + 1) * HEAD], None)
        grp[g, 2 * HEAD : 2 * HEAD + HALF] = a.astype(BF16)
        grp[g, 2 * HEAD + HALF : 3 * HEAD] = b.astype(BF16)
        grp[g, 3 * HEAD :] = vt[g * HEAD : (g + 1) * HEAD].astype(BF16)
    qkv[zl] = grp[zl]
    kv[x, y, zl] = grp[zl, 2 * HEAD :]
    for k in range(2):
        down_load(k).start()
        for cp in ff_loads(k):
            cp.start()
    answer(peers)
    q_rows, k_rows = pl.ds(0, 2 * HEAD), pl.ds(2 * HEAD, 2 * HEAD)
    k_cp = remote(grp.at[1 - zl, k_rows], kv.at[3 - x, 3 - y, zl], pair_send.at[0], pair_recv.at[0], partner)
    q_cp = remote(grp.at[1 - zl, q_rows], qkv.at[zl, q_rows], pair_send.at[4], pair_recv.at[4], partner)
    k_cp.start()

    def gather(n, slot, swap):
        me1, me2 = (y, x) if swap else (x, y)
        r1, l1, r2, l2 = (yr, yl, xr, xl) if swap else (xr, xl, yr, yl)

        def ref(i, j, part=None):
            i, j = lax.rem(i + 4, 4), lax.rem(j + 4, 4)
            v = kv.at[j, i, slot] if swap else kv.at[i, j, slot]
            return v if part is None else v.at[pl.ds(part * HEAD, HEAD)]

        def cp(k, view, dev):
            return remote(view, view, ag_send.at[n, k], ag_recv.at[n, k], dev)

        def stage(base, i, j, di, dj, r, l):
            return dict(
                right=cp(base, ref(i, j), r),
                left=cp(base + 1, ref(i, j), l),
                from_left=cp(base, ref(i - di, j - dj), r),
                from_right=cp(base + 1, ref(i + di, j + dj), l),
                on_right=cp(base + 2, ref(i - di, j - dj, 0), r),
                on_left=cp(base + 3, ref(i + di, j + dj, 1), l),
                from_left2=cp(base + 2, ref(i + 2 * di, j + 2 * dj, 0), r),
                from_right2=cp(base + 3, ref(i + 2 * di, j + 2 * dj, 1), l),
            )

        s1 = stage(0, me1, me2, 1, 0, r1, l1)
        s2 = [stage(4 + 4 * k, me1 + k, me2, 0, 1, r2, l2) for k in range(4)]
        return s1, s2

    def begin(st):
        st["right"].start()
        st["left"].start()

    def hand_on(st):
        st["from_left"].wait_recv()
        st["on_right"].start()
        st["from_right"].wait_recv()
        st["on_left"].start()

    def complete(st):
        st["from_left2"].wait_recv()
        st["from_right2"].wait_recv()

    own, other = gather(0, zl, False), gather(1, 1 - zl, True)
    both = (own, other)
    begin(own[0])
    begin(own[1][0])
    q_cp.start()
    wo_cps = [
        remote(wo, wo_full.at[me_t], w_send.at[0], w_recv.at[0], diagonal),
        remote(wo, wo_full.at[me_t], w_send.at[1], w_recv.at[1], core),
    ]
    for cp in wo_cps:
        cp.start()
    k_there = kv.at[x, y, 1 - zl]
    remote(k_there, k_there, pair_send.at[0], pair_recv.at[0], partner).wait_recv()
    begin(other[0])
    begin(other[1][0])
    q_there = qkv.at[1 - zl, q_rows]
    remote(q_there, q_there, pair_send.at[4], pair_recv.at[4], partner).wait_recv()
    low = place.low_block(x, y)
    for s in range(2):
        base = jnp.where(s == 0, low, 31 - low) * ROWS
        segs = query_segments(ends, base)
        for h in range(2):
            qaug[s, :HEAD, h * ROWS : (h + 1) * ROWS] = qkv[s, h * HEAD : (h + 1) * HEAD]
            qaug[s, HEAD:, h * ROWS : (h + 1) * ROWS] = segs
    peak[...] = jnp.full(peak.shape, -BIG, F32)
    total[...] = jnp.zeros(total.shape, F32)
    acc[...] = jnp.zeros(acc.shape, F32)

    def attend(qs, kx, ky, ks, kbase, causal):
        pair = kv[kx, ky, ks]
        ka = jnp.concatenate([pair[:HEAD], key_segments(ends, kbase)], 0)
        s = dot(ka, qaug[qs], 0, 0)
        if causal:
            key = lax.broadcasted_iota(jnp.int32, (ROWS, 2 * ROWS), 0)
            query = lax.broadcasted_iota(jnp.int32, (ROWS, 2 * ROWS), 1)
            s = jnp.where(key <= jnp.where(query >= ROWS, query - ROWS, query), s, -BIG)
        old = peak[qs]
        new = jnp.maximum(old, jnp.max(s, 0, keepdims=True))
        p = jnp.exp2(s - new)
        fade = jnp.exp2(old - new)
        peak[qs] = new
        total[qs] = total[qs] * fade + jnp.sum(p, 0, keepdims=True)
        acc[qs] = acc[qs] * fade + dot(pair[HEAD:], p.astype(BF16))

    def shard(dx, dy):
        kx, ky = lax.rem(x + dx, 4), lax.rem(y + dy, 4)
        there = place.low_block(kx, ky)
        attend(1, kx, ky, 0, there * ROWS, False)
        sel = jnp.where(there < low, 0, 1)
        attend(sel, kx, ky, sel, jnp.where(there < low, there, 31 - there) * ROWS, False)

    def shards(count, offsets):
        def step(i, carry):
            shard(*offsets(i))
            return carry

        lax.fori_loop(0, count, step, 0)

    attend(0, x, y, 0, low * ROWS, True)
    attend(1, x, y, 1, (31 - low) * ROWS, True)
    attend(1, x, y, 0, low * ROWS, False)
    for s1, s2 in both:
        hand_on(s1)
        begin(s2[3])
        begin(s2[1])
    for s1, s2 in both:
        hand_on(s2[0])
    hidden_back(0)
    shards(4, lambda i: ((1 - i // 2) * (2 * i + 1), (i // 2) * (2 * i - 3)))
    for s1, s2 in both:
        complete(s1)
        begin(s2[2])
    hidden_back(1)
    for s1, s2 in both:
        hand_on(s2[3])
        hand_on(s2[1])
    shards(4, lambda i: (2 * (i // 2) + 1, 2 * lax.rem(i, 2) + 1))
    hidden_back(2)
    for s1, s2 in both:
        complete(s2[0])
        hand_on(s2[2])
    shards(2, lambda i: (2 * i, 2 - 2 * i))
    hidden_back(3)
    for s1, s2 in both:
        complete(s2[3])
        complete(s2[1])
    shards(4, lambda i: ((1 - i // 2) * (2 * i + 1) + 2 * (i // 2), (i // 2) * (2 * i - 3) + 2 * (1 - i // 2)))
    for s1, s2 in both:
        complete(s2[2])
    shard(2, 2)
    for s in range(2):
        out = acc[s] / total[s]
        lse[s] = peak[s] + jnp.log2(total[s])
        for h in range(2):
            part = out[:, h * ROWS : (h + 1) * ROWS]
            o[s, h * HEAD : (h + 1) * HEAD] = part
            mine[s, h * HEAD : (h + 1) * HEAD] = part.astype(BF16)

    for s1, s2 in both:
        for st in [s1, *s2]:
            for name in ("right", "left", "on_right", "on_left"):
                st[name].wait_send()
    k_cp.wait_send()
    q_cp.wait_send()

    group = me_t * 2 + zl
    att[group] = mine[zl]
    sends = [
        remote(mine.at[1 - zl], att.at[group], o_send.at[0], o_recv.at[0], partner),
        remote(mine.at[1 - zl], att.at[group], o_send.at[1], o_recv.at[1], far_partner),
        remote(mine.at[zl], att.at[group], o_send.at[2], o_recv.at[2], far),
    ]
    for cp in sends:
        cp.start()
    wo_far = wo_full.at[there_t]
    remote(wo_far, wo_far, w_send.at[0], w_recv.at[0], far).wait_recv()
    wo_relay = remote(wo_far, wo_far, w_send.at[2], w_recv.at[2], core)
    wo_relay.start()
    def load_wo(src, slot):
        pltpu.make_async_copy(src, wo_buf.at[slot], wo_sem.at[slot]).start()

    def wo_ready(slot):
        pltpu.make_async_copy(wo, wo_buf.at[slot], wo_sem.at[slot]).wait()

    def arrived(which, n):
        remote(att.at[which], att.at[which], o_send.at[n], o_recv.at[n], far).wait_recv()

    def relay(which, n):
        cp = remote(att.at[which], att.at[which], o_send.at[n], o_recv.at[n], core)
        cp.start()
        return cp

    def heads_of(t):
        return att[pl.ds(t * 2, 2)].reshape(HEADS_LOCAL, ROWS)

    w1, w2 = wo_full.at[mine_t], wo_full.at[other_t]
    load_wo(wo, 0)
    relays = [relay(group, 3)]
    left[...] = cot[...].T
    remote(w1, w1, w_send.at[1], w_recv.at[1], core).wait_recv()
    load_wo(w1, 1)
    arrived(me_t * 2 + 1 - zl, 0)
    relays.append(relay(me_t * 2 + 1 - zl, 4))
    wo_ready(0)
    mixed[...] = dot(heads_of(me_t), wo_buf[0], 0, 0)
    load_wo(wo_far, 0)
    arrived(mine_t * 2 + zl, 3)
    arrived(mine_t * 2 + 1 - zl, 4)
    arrived(there_t * 2 + zl, 2)
    relays.append(relay(there_t * 2 + zl, 5))
    arrived(there_t * 2 + 1 - zl, 1)
    relays.append(relay(there_t * 2 + 1 - zl, 6))
    wo_ready(1)
    mixed[...] = mixed[...] + dot(heads_of(mine_t), wo_buf[1], 0, 0)
    remote(w2, w2, w_send.at[2], w_recv.at[2], core).wait_recv()
    load_wo(w2, 1)
    wo_ready(0)
    back[...] = dot(heads_of(there_t), wo_buf[0], 0, 0)
    load_wo(wo, 0)
    arrived(other_t * 2 + zl, 5)
    arrived(other_t * 2 + 1 - zl, 6)
    wo_ready(1)
    back[...] = back[...] + dot(heads_of(other_t), wo_buf[1], 0, 0)
    mixed[...] = tokens[...].astype(F32) + (mixed[...] + back[...])
    normed_save.wait()
    gain = gain2[...].reshape(1, WIDTH)
    inverse_two = lax.rsqrt(jnp.mean(mixed[...] * mixed[...], -1, keepdims=True) + EPS)
    normed[...] = (mixed[...] * inverse_two * gain).astype(BF16)
    mixed_save = pltpu.make_async_copy(mixed, mixed_out, load_sem.at[1])
    mixed_save.start()

    for k in range(FF_CHUNKS):
        slot, cols = k % 2, slice(k * FF_CHUNK, (k + 1) * FF_CHUNK)
        for cp in ff_loads(k):
            cp.wait()
        both_ff = dot(normed[...], gu_buf[slot])
        gate, upper = both_ff[:, :FF_CHUNK], both_ff[:, FF_CHUNK:]
        hidden_grad = back_hidden[:, cols].astype(F32)
        sig = jax.nn.sigmoid(gate)
        silu = gate * sig
        hid = (silu * upper).astype(BF16)
        gg = (hidden_grad * upper * sig * (1.0 + gate * (1.0 - sig))).astype(BF16)
        ug = (hidden_grad * silu).astype(BF16)
        hidden[:, cols], gate_grad[:, cols], upper_grad[:, cols] = hid, gg, ug
        add_back = dot(jnp.concatenate([gg, ug], 1), gu_buf[slot], 1, 1)
        if k == 0:
            back[...] = add_back
        else:
            back[...] = back[...] + add_back
        if k + 2 < FF_CHUNKS:
            for cp in ff_loads(k + 2):
                cp.start()
    part3[...] = ar_view(back[...].astype(BF16))
    sum3 = TpSum(place, part3, buf3, (send3, recv3))
    sum3.start()
    def weight_grad(rhs, lo, cb=0):
        w = rhs.shape[1 - cb]

        def slab(i, carry):
            piece = dot(left[pl.ds(pl.multiple_of(i * 192, 192), 192)], rhs[...], 1, cb)
            grads[i // 4, i % 4, :, :, lo : lo + w] = piece.astype(BF16).reshape(4, 48, w)
            return carry

        lax.fori_loop(0, 8, slab, 0)

    groups, blo = {}, dict(plane=0, depth=0)
    for n, (name, kind, first, slo, w, glo) in enumerate(PLAN):
        if kind == "plane":
            piece = PlaneSum(place, first, grads, glo, blo[kind], slo, w, (b1, r1, b2, r2, zb), (gsend, grecv), n, sums)
        else:
            piece = DepthSum(place, first, grads, glo, blo[kind], slo, w, (z0, b1z, r1z, b2z), (gsend, grecv), n, sums)
        blo[kind] += w
        groups.setdefault(name, []).append(piece)
    pieces = [p for group_ in groups.values() for p in group_]

    def go(*names):
        for name in names:
            for piece in groups[name]:
                piece.next()

    weight_grad(hidden, 2 * FFL)
    go("down")
    sum3.mid()
    left[...] = normed[...].T
    weight_grad(gate_grad, 0)
    go("gate")
    weight_grad(upper_grad, FFL)
    go("up")
    mixed_save.wait()
    for k in range(FF_CHUNKS):
        down_load(k).wait()
        add_feed = dot(hidden[:, k * FF_CHUNK : (k + 1) * FF_CHUNK], d_buf[k % 2])
        mixed[...] = add_feed if k == 0 else mixed[...] + add_feed
        if k < 2:
            down_load(k + 2).start()
    feed_out[...] = ar_view(mixed[...].astype(BF16))
    mixed_load = pltpu.make_async_copy(mixed_out, mixed, load_sem.at[1])
    mixed_load.start()
    sum2 = TpSum(place, feed_out, buf2, (send2, recv2))
    sum2.start()
    for s in range(2):
        for h in range(2):
            dot_t[s, :, h * ROWS : (h + 1) * ROWS] = jnp.zeros((HEAD, ROWS), BF16)
    acc[...] = jnp.zeros(acc.shape, F32)
    dq = acc
    mixed_load.wait()
    go("down")
    sum3.fin()
    go("down_z", "gate_z", "up_z")
    sum3.landed()
    mixed_part, ffn_gain_grad = norm_back(mixed[...], inverse_two, gain, ar_load(part3).astype(F32))
    gain_sum[0, 1:2] = ffn_gain_grad
    back[...] = cot[...].astype(F32) + mixed_part
    normed[...] = back[...].astype(BF16)
    wo_ready(0)
    own_grad = dot(wo_buf[0], normed[...], 1, 1).astype(BF16)
    dgrp[0] = own_grad[: 2 * HEAD]
    dgrp[1] = own_grad[2 * HEAD :]
    grad_cp = remote(dgrp.at[1 - zl], dout.at[zl], pair_send.at[1], pair_recv.at[1], partner)
    grad_cp.start()
    dout[zl] = dgrp[zl]
    left[...] = normed[...].T
    weight_grad(heads_of(me_t), W_FFN, 1)
    go("out")
    normed_load = pltpu.make_async_copy(normed_out, normed, load_sem.at[0])
    normed_load.start()
    for cp in projections():
        cp.start()
    go("gate")
    grad_cp.wait_recv()
    for s in range(2):
        for h in range(2):
            lanes, feats = slice(h * ROWS, (h + 1) * ROWS), slice(h * HEAD, (h + 1) * HEAD)
            d = dout[s, feats]
            dot_t[s, :, lanes] = d
            delta[s, :, lanes] = jnp.sum(d.astype(F32) * o[s, feats], 0, keepdims=True)

    def attend_back(qs, kx, ky, ks, kbase, causal):
        pair = kv[kx, ky, ks]
        q = qaug[qs]
        do = dot_t[qs]
        ka = jnp.concatenate([pair[:HEAD], key_segments(ends, kbase)], 0)
        s = dot(ka, q, 0, 0)
        p = jnp.exp2(s - lse[qs])
        if causal:
            key = lax.broadcasted_iota(jnp.int32, (ROWS, 2 * ROWS), 0)
            query = lax.broadcasted_iota(jnp.int32, (ROWS, 2 * ROWS), 1)
            p = jnp.where(key <= jnp.where(query >= ROWS, query - ROWS, query), p, 0.0)
        dp = dot(pair[HEAD:], do, 0, 0)
        ds = (p * (dp - delta[qs])).astype(BF16)
        dq[qs] = dq[qs] + dot(pair[:HEAD], ds)
        dk = dot(q[:HEAD], ds, 1, 1)
        dv = dot(do, p.astype(BF16), 1, 1)
        return jnp.concatenate([dk, dv], 0)

    def shard_back(dx, dy):
        kx, ky = lax.rem(x + dx, 4), lax.rem(y + dy, 4)
        there = place.low_block(kx, ky)
        one = attend_back(1, kx, ky, 0, there * ROWS, False)
        before = there < low
        sel = jnp.where(before, 0, 1)
        two = attend_back(sel, kx, ky, sel, jnp.where(before, there, 31 - there) * ROWS, False)
        share = jnp.where(before, 1.0, 0.0)
        kv[kx, ky, 0] = (one + two * share).astype(BF16)
        kv[kx, ky, 1] = (two * (1.0 - share)).astype(BF16)

    def shards_back(count, offsets, events):
        def step(i, carry):
            shard_back(*offsets(i))
            for at, event in events:
                pl.when(i == at)(event)
            return carry

        lax.fori_loop(0, count, step, 0)

    def key_sum(slot, axis):
        other_axis = "y" if axis == "x" else "x"
        if axis == "x":
            half = lambda d, h: kv.at[d, :, slot, pl.ds(h * HEAD, HEAD)]
        else:
            half = lambda d, h: kv.at[:, d, slot, pl.ds(h * HEAD, HEAD)]
        one = RingSum(
            place, axis, half, lambda k: kb1.at[slot, k], lambda h: kr1.at[slot, h],
            lambda k: ksend.at[slot, k], lambda k: krecv.at[slot, k],
        )
        two = RingSum(
            place, other_axis, lambda d, h: kr1.at[slot, h, d], lambda k: kb2.at[slot, k],
            lambda h: kr2.at[slot, h], lambda k: ksend.at[slot, 6 + k], lambda k: krecv.at[slot, 6 + k],
        )
        return one, two

    ka, kb = key_sum(0, "x"), key_sum(1, "y")

    def two_away(i):
        k, j = i // 4, i - 4
        return (1 - k) * 2 + k * (j + j // 2), (1 - k) * i + k * 2

    def one_away(i):
        k, j = i // 4, i - 4
        along_x = (1 - j // 2) * (2 * j + 1)
        along_y = (j // 2) * (2 * j - 3)
        dx = (1 - k) * (2 * (i // 2) + 1) + k * along_x
        dy = (1 - k) * (2 * lax.rem(i, 2) + 1) + k * along_y
        return dx, dy

    shards_back(7, two_away, [(0, lambda: go("up", "out")), (3, lambda: go("down")), (6, lambda: go("gate"))])
    ka[0].start_far()
    kb[0].start_far()

    def near(part):
        part.start_near()
        part.mid()

    shards_back(
        8,
        one_away,
        [
            (1, lambda: go("up", "out")),
            (3, lambda: go("down", "down_z")),
            (5, lambda: near(ka[0])),
            (6, lambda: go("gate")),
        ],
    )
    near(kb[0])
    first = attend_back(0, x, y, 0, low * ROWS, True) + attend_back(1, x, y, 0, low * ROWS, False)
    kv[x, y, 0] = first.astype(BF16)
    kv[x, y, 1] = attend_back(1, x, y, 1, (31 - low) * ROWS, True).astype(BF16)

    for s in range(2):
        for h in range(2):
            grp[s, h * HEAD : (h + 1) * HEAD] = (dq[s, :, h * ROWS : (h + 1) * ROWS] * SCALE).astype(BF16)
    dq_cp = remote(grp.at[1 - zl, q_rows], dqkv.at[zl, q_rows], pair_send.at[2], pair_recv.at[2], partner)
    dq_cp.start()
    dqkv[zl, : 2 * HEAD] = grp[zl, : 2 * HEAD]
    go("up", "out", "down", "gate")

    ka[0].fin()
    kb[0].fin()
    ka[1].start()
    kb[1].start()
    go("gate_z", "down_z")
    sum2.mid()

    def unturned(g, h, at):
        a = dqkv[g, h * HEAD : h * HEAD + HALF].astype(F32)
        b = dqkv[g, h * HEAD + HALF : (h + 1) * HEAD].astype(F32)
        if h == 2:
            a, b = a * LN2, b * LN2
        rows[at : at + HALF] = (a * cosine + b * sine).astype(BF16)
        rows[at + HALF : at + HEAD] = (b * cosine - a * sine).astype(BF16)

    dq_there = dqkv.at[1 - zl, q_rows]
    remote(dq_there, dq_there, pair_send.at[2], pair_recv.at[2], partner).wait_recv()
    for g in range(2):
        for h in range(2):
            unturned(g, h, (2 * g + h) * HEAD)
    normed_load.wait()
    for piece in groups["down"]:
        piece.one.end()
    left[...] = normed[...].T
    weight_grad(rows.at[pl.ds(0, HEADS_LOCAL)], 2 * FFL, 1)
    ka[1].mid()
    kb[1].mid()
    go("query")
    for cp in projections():
        cp.wait()
    mixed[...] = dot(rows[:HEADS_LOCAL], gu_buf[0, :, :HEADS_LOCAL], 0, 1)
    go("down_z", "gate_z", "up", "out", "up_z")
    ka[1].fin()
    kb[1].fin()
    for s in range(2):
        for h in range(2):
            grp[s, (2 + h) * HEAD : (3 + h) * HEAD] = kr2[s, h]
    dk_cp = remote(grp.at[1 - zl, k_rows], dqkv.at[zl, k_rows], pair_send.at[3], pair_recv.at[3], partner)
    dk_cp.start()
    dqkv[zl, 2 * HEAD :] = grp[zl, 2 * HEAD :]
    go("down", "gate", "down_z", "gate_z", "query", "up_z", "up", "out")
    for piece in groups["gate"]:
        piece.one.end()
    sum2.fin()
    sum3.end()
    dk_there = dqkv.at[1 - zl, k_rows]
    remote(dk_there, dk_there, pair_send.at[3], pair_recv.at[3], partner).wait_recv()
    for g in range(2):
        unturned(g, 2, HEADS_LOCAL + g * HEAD)
        at = HEADS_LOCAL + PAIRS_LOCAL + g * HEAD
        rows[at : at + HEAD] = dqkv[g, 3 * HEAD :]
    weight_grad(rows.at[pl.ds(HEADS_LOCAL, 2 * PAIRS_LOCAL)], 0, 1)
    go("pair")
    grad_in = mixed[...] + dot(rows[HEADS_LOCAL : HEADS_LOCAL + PAIRS_LOCAL], d_buf[0, :PAIRS_LOCAL], 0, 0)
    grad_in = grad_in + dot(rows[HEADS_LOCAL + PAIRS_LOCAL :], d_buf[1, :PAIRS_LOCAL], 0, 0)
    part3[...] = ar_view(grad_in.astype(BF16))
    sum4 = TpSum(place, part3, buf4, (send4, recv4))
    sum4.start()
    source = tokens[...].astype(F32)
    gain_sum[0, 0:1] = jnp.sum(grad_in * source * inverse, 0, keepdims=True)
    gain_sum[0, 1:2] = 0.25 * gain_sum[0, 1:2]
    gain_sent = []

    def gain_step(stage):
        if stage:
            came = gain_sum[stage - 1]
            for k, cp in enumerate(gain_sent[-1]):
                cp.wait_recv()
                came = came + gain_buf[stage - 1, k]
            gain_sum[stage] = came
        if stage < 5:
            there = [
                [place.along("x", k) for k in (1, 2, 3)], [place.along("y", k) for k in (1, 2, 3)],
                [place.at(zl=1 - zl)], [far], [core],
            ][stage]
            gain_sent.append(
                [
                    remote(gain_sum.at[stage], gain_buf.at[stage, k], gn_send.at[stage, k], gn_recv.at[stage, k], peer)
                    for k, peer in enumerate(there)
                ]
            )
            for cp in gain_sent[-1]:
                cp.start()

    gain_step(0)
    go("down_z", "gate_z")
    sum4.mid()
    gain_step(1)
    go("query", "up_z", "pair")
    gain_step(2)
    go("gate_z", "query", "up_z")
    gain_step(3)
    go("pair")
    sum4.fin()
    gain_step(4)
    go("up_z", "query", "pair")
    sum4.landed()
    source_part, _ = norm_back(tokens[...].astype(F32), inverse, gain1[...].reshape(1, WIDTH), ar_load(part3).astype(F32))
    tokens_grad[...] = (back[...] + source_part).astype(BF16)
    gain_step(5)
    gains[...] = gain_sum[5]
    go("pair", "query", "pair")
    sum2.landed()
    for cp in [grad_cp, dq_cp, dk_cp, *wo_cps, wo_relay, *sends, *relays, *sum(gain_sent, [])]:
        cp.wait_send()
    sum2.end()
    sum4.end()
    for piece in pieces:
        assert piece.at == len(piece.steps)
        piece.end()
    for one, two in (ka, kb):
        one.end()
        two.end()


def layer(lengths, freq, tokens, cot, gain1, gain2, wq, wkt, wvt, wo, wg, wu, wd):
    vm = pl.BlockSpec(memory_space=pltpu.VMEM)
    hbm = pl.BlockSpec(memory_space=pl.ANY)
    dma = pltpu.SemaphoreType.DMA
    shape = (2, AR_PIECES, AR_ROWS, WIDTH)
    group = pltpu.VMEM((2, 4 * HEAD, ROWS), BF16)
    two_heads = pltpu.VMEM((2, 2 * HEAD, ROWS), BF16)
    line = pltpu.VMEM((2, 1, 2 * ROWS), F32)
    return pl.pallas_call(
        layer_kernel,
        out_shape=(
            jax.ShapeDtypeStruct((ROWS, WIDTH), F32),
            jax.ShapeDtypeStruct((ROWS, WIDTH), BF16),
            jax.ShapeDtypeStruct((4, HEADS_LOCAL, WIDTH), BF16),
            jax.ShapeDtypeStruct(shape, BF16),
            jax.ShapeDtypeStruct((ROWS, WIDTH), BF16),
            jax.ShapeDtypeStruct((48, W_ALL), F32),
            jax.ShapeDtypeStruct((2, WIDTH), F32),
        ),
        in_specs=[pl.BlockSpec(memory_space=pltpu.SMEM)] + [vm] * 5 + [hbm] * 7,
        out_specs=(hbm, hbm, hbm, vm, vm, vm, vm),
        scratch_shapes=[
            pltpu.VMEM((2, HEADS_LOCAL, WIDTH), BF16),
            pltpu.VMEM((2, WIDTH, 2 * FF_CHUNK), BF16),
            pltpu.VMEM((2, FF_CHUNK, WIDTH), BF16),
            pltpu.VMEM((ROWS, WIDTH), F32),
            pltpu.VMEM((ROWS, WIDTH), F32),
            pltpu.VMEM((ROWS, WIDTH), BF16),
            pltpu.VMEM((ROWS, FFL), BF16),
            pltpu.VMEM((ROWS, FFL), BF16),
            pltpu.VMEM((ROWS, FFL), BF16),
            pltpu.VMEM((ROWS, FFL), BF16),
            pltpu.VMEM((WIDTH, ROWS), BF16),
            pltpu.VMEM((2, 4, 4, 48, W_MID), BF16),
            pltpu.VMEM((6, 4, 48, W_PLANE), BF16),
            pltpu.VMEM((2, 4, 48, W_PLANE), BF16),
            pltpu.VMEM((6, 48, W_PLANE), BF16),
            pltpu.VMEM((2, 48, W_PLANE), BF16),
            pltpu.VMEM((48, W_PLANE), BF16),
            pltpu.VMEM((4, 4, 48, W_DEPTH), BF16),
            pltpu.VMEM((6, 4, 48, W_DEPTH // 2), BF16),
            pltpu.VMEM((4, 48, W_DEPTH), BF16),
            pltpu.VMEM((6, 48, W_DEPTH // 2), BF16),
            dma((len(PLAN), 13)),
            dma((len(PLAN), 13)),
            pltpu.VMEM(shape, BF16),
            *tp_scratch(),
            *tp_scratch(),
            *tp_scratch(),
            pltpu.VMEM((4, 4, 2, 2 * HEAD, ROWS), BF16),
            pltpu.VMEM((2, 6, 4, HEAD, ROWS), BF16),
            pltpu.VMEM((2, 2, 4, HEAD, ROWS), BF16),
            pltpu.VMEM((2, 6, HEAD, ROWS), BF16),
            pltpu.VMEM((2, 2, HEAD, ROWS), BF16),
            dma((2, 12)),
            dma((2, 12)),
            group,
            group,
            pltpu.VMEM((8, 2 * HEAD, ROWS), BF16),
            pltpu.VMEM((2, 2 * HEAD, ROWS), F32),
            line,
            pltpu.VMEM((2, HEAD + SEG, 2 * ROWS), BF16),
            pltpu.VMEM((2, HEAD, 2 * ROWS), F32),
            line,
            line,
            two_heads,
            two_heads,
            two_heads,
            pltpu.VMEM((2, HEAD, 2 * ROWS), BF16),
            line,
            group,
            pltpu.VMEM((W_TAIL, ROWS), BF16),
            pltpu.VMEM((6, 2, WIDTH), F32),
            pltpu.VMEM((5, 3, 2, WIDTH), F32),
            dma((5, 3)),
            dma((5, 3)),
            dma((5,)),
            dma((5,)),
            dma((2, 20)),
            dma((2, 20)),
            dma((7,)),
            dma((7,)),
            dma((3,)),
            dma((3,)),
            dma((2,)),
            dma((2, 3)),
            dma((2,)),
        ],
        compiler_params=pltpu.CompilerParams(
            collective_id=0, has_side_effects=True, vmem_limit_bytes=VMEM_LIMIT
        ),
        name="layer",
    )(lengths, freq, tokens, cot, gain1, gain2, wq, wkt, wvt, wo, wg, wu, wd)


def finish_kernel(
    mixed, feed, tokens_grad, sums, gains,
    result, tokens_grad_out, norm_gain, query, key, value, out, ffn_gain, gate, up, down,
):
    result[...] = (mixed[...] + ar_load(feed).astype(F32)).astype(BF16)
    tokens_grad_out[...] = tokens_grad[...]
    block = (lax.axis_index("zl") * 4 + lax.axis_index("x")) * 4 + lax.axis_index("y")
    own = jnp.zeros((2, 48), F32)
    for b in range(32):
        own = own + jnp.where(block == b, gains[:, 48 * b : 48 * b + 48], 0.0)
    norm_gain[...] = own[0:1]
    ffn_gain[...] = own[1:2]
    gate[...] = sums[:, :FFL]
    up[...] = sums[:, FFL : 2 * FFL]
    down[...] = sums[:, 2 * FFL : W_FFN]
    out[...] = sums[:, W_FFN:W_MID]
    query[...] = sums[:, W_MID : W_MID + HEADS_LOCAL]
    key[...] = sums[:, W_MID + HEADS_LOCAL : W_MID + HEADS_LOCAL + PAIRS_LOCAL]
    value[...] = sums[:, W_MID + HEADS_LOCAL + PAIRS_LOCAL :]


def finish(mixed, feed, tokens_grad, sums, gains):
    vm = pl.BlockSpec(memory_space=pltpu.VMEM)
    shapes = [(ROWS, WIDTH)] * 2 + [
        (1, 48), (48, HEADS_LOCAL), (48, PAIRS_LOCAL), (48, PAIRS_LOCAL), (48, HEADS_LOCAL), (1, 48),
        (48, FFL), (48, FFL), (48, FFL),
    ]
    return pl.pallas_call(
        finish_kernel,
        out_shape=[jax.ShapeDtypeStruct(s, BF16 if n < 2 else F32) for n, s in enumerate(shapes)],
        in_specs=[vm] * 5,
        out_specs=[vm] * len(shapes),
        compiler_params=pltpu.CompilerParams(vmem_limit_bytes=VMEM_LIMIT),
        name="finish",
    )(mixed, feed, tokens_grad, sums, gains)


def local(
    tokens, norm_gain, query_weight, key_matrix, value_matrix, out_weight,
    ffn_gain, gate_weight, up_weight, down_weight, cotangent, lengths,
):
    freq = jnp.asarray(
        (THETA ** (-2.0 * np.arange(HALF) / HEAD)).astype(np.float32).reshape(HALF, 1)
    )
    mixed, _, _, feed, tokens_grad, sums, gains = layer(
        lengths, freq, tokens, cotangent, norm_gain, ffn_gain, query_weight, key_matrix.T, value_matrix.T,
        out_weight, gate_weight, up_weight, down_weight,
    )
    result, tokens_grad, norm_gain_grad, query, key, value, out, ffn_gain_grad, gate, up, down = finish(
        mixed, feed, tokens_grad, sums, gains
    )
    return (
        result, tokens_grad, norm_gain_grad.reshape(48), query, key, value, out.T,
        ffn_gain_grad.reshape(48), gate, up, down.T,
    )


def solution(mesh):
    split = Mesh(mesh.devices.reshape(2, 4, 4, 2, 2), AXES)
    in_specs = (
        P(BLK, None),
        P(),
        P(None, TP),
        P(None, TP),
        P(None, TP),
        P(TP, None),
        P(),
        P(None, TP),
        P(None, TP),
        P(TP, None),
        P(BLK, None),
        P(),
    )
    out_specs = (
        P(BLK, None),
        P(BLK, None),
        P(BLK),
        P(BLK, TP),
        P(BLK, TP),
        P(BLK, TP),
        P(TP, BLK),
        P(BLK),
        P(BLK, TP),
        P(BLK, TP),
        P(TP, BLK),
    )
    return jax.shard_map(local, mesh=split, in_specs=in_specs, out_specs=out_specs, check_vma=False)
```

```python
import jax
import jax.numpy as jnp
import numpy as np
from jax import lax
from jax.experimental import pallas as pl
from jax.experimental.pallas import tpu as pltpu
from jax.sharding import Mesh
from jax.sharding import PartitionSpec as P

AXES = ("zl", "x", "y", "zh", "c")
BLK = ("zl", "x", "y")
TP = ("zh", "c")
HEAD = 96
HALF = HEAD // 2
ROWS = 256
WIDTH = 1536
HEADS_LOCAL = 384
PAIRS_LOCAL = 192
FFL = 1024
EPS = 1e-05
THETA = 100000.0
SCALE = HEAD**-0.5
LOG2E = float(np.log2(np.e))
LN2 = float(np.log(2.0))
BIG = 1e30
SEG = 16
MESH = pl.DeviceIdType.MESH
F32 = jnp.float32
BF16 = jnp.bfloat16
VMEM_LIMIT = 63 * 2**20


def dot(a, b, ca=1, cb=0):
    return lax.dot_general(a, b, (((ca,), (cb,)), ((), ())), preferred_element_type=F32)


class Place:
    def __init__(self):
        self.zl, self.x, self.y, self.zh, self.c = (lax.axis_index(a) for a in AXES)

    def at(self, **changes):
        own = dict(zl=self.zl, x=self.x, y=self.y, zh=self.zh, c=self.c)
        own.update(changes)
        return tuple(own[a] for a in AXES)

    def along(self, axis, step):
        return self.at(**{axis: lax.rem(getattr(self, axis) + (step + 4), 4)})

    @property
    def pair(self):
        return dict(zl=1 - self.zl, x=3 - self.x, y=3 - self.y)

    def low_block(self, x, y):
        p = x * 4 + y
        return jnp.where(self.zl == 0, p, 15 - p)


def call(peers):
    barrier = pltpu.get_barrier_semaphore()
    for peer in peers:
        pl.semaphore_signal(barrier, inc=1, device_id=peer, device_id_type=MESH)


def answer(peers):
    pl.semaphore_wait(pltpu.get_barrier_semaphore(), len(peers))


def remote(src, dst, send, recv, device):
    return pltpu.make_async_remote_copy(
        src_ref=src, dst_ref=dst, send_sem=send, recv_sem=recv, device_id=device, device_id_type=MESH
    )


def seg_rows(ends, base):
    token = base + lax.broadcasted_iota(jnp.int32, (SEG, ROWS), 1)
    row = lax.broadcasted_iota(jnp.int32, (SEG, ROWS), 0)
    inside = jnp.zeros((SEG, ROWS), F32)
    start = 0
    for d in range(5):
        hit = (row == d) & (token >= start) & (token < ends[d])
        inside = jnp.where(hit, 1.0, inside)
        start = ends[d]
    return inside, row


def key_segments(ends, base):
    return seg_rows(ends, base)[0].astype(BF16)


def query_segments(ends, base):
    inside, row = seg_rows(ends, base)
    return jnp.where(row < 5, (inside - 1.0) * BIG, 0.0).astype(BF16)


def ends_of(lengths_ref):
    ends, total = [], 0
    for d in range(5):
        total = total + lengths_ref[d]
        ends.append(total)
    return ends


def rotation(ends, lengths_ref, base, freq):
    token = base + lax.broadcasted_iota(jnp.int32, (1, ROWS), 1)
    begin = jnp.zeros((1, ROWS), jnp.int32)
    for d in range(5):
        begin = begin + jnp.where(token >= ends[d], lengths_ref[d], 0)
    angle = (token - begin).astype(F32) * freq
    return jnp.cos(angle), jnp.sin(angle)


class RingSum:
    def __init__(self, place, axis, half, bufs, out, send, recv):
        self.half, self.bufs, self.out = half, bufs, out
        me = getattr(place, axis)
        self.me = me
        self.r, self.l, self.o = (lax.rem(me + k, 4) for k in (1, 3, 2))
        self.right, self.left = place.along(axis, 1), place.along(axis, -1)
        self.send, self.recv = send, recv
        self.ended = False

    def cp(self, k):
        src = (
            lambda: self.half(self.o, 0),
            lambda: self.half(self.o, 1),
            lambda: self.half(self.r, 1),
            lambda: self.half(self.l, 0),
            lambda: self.bufs(0),
            lambda: self.bufs(1),
        )[k]()
        return remote(src, self.bufs(k), self.send(k), self.recv(k), (self.right, self.left)[k % 2])

    def start_far(self):
        self.cp(0).start()
        self.cp(1).start()

    def start_near(self):
        self.cp(2).start()
        self.cp(3).start()

    def start(self):
        self.start_far()
        self.start_near()

    def mid(self):
        self.cp(0).wait_recv()
        add_two(self.bufs(0), self.half(self.r, 0))
        self.cp(4).start()
        self.cp(1).wait_recv()
        add_two(self.bufs(1), self.half(self.l, 1))
        self.cp(5).start()

    def fin(self):
        self.cp(4).wait_recv()
        self.cp(3).wait_recv()
        add_three(self.out(0), self.half(self.me, 0), self.bufs(4), self.bufs(3))
        self.cp(5).wait_recv()
        self.cp(2).wait_recv()
        add_three(self.out(1), self.half(self.me, 1), self.bufs(5), self.bufs(2))

    def end(self):
        if not self.ended:
            self.ended = True
            for k in range(6):
                self.cp(k).wait_send()


def add_two(dst, src):
    if len(dst.shape) == 3:
        for i in range(dst.shape[0]):
            dst[i] = dst[i] + src[i]
    else:
        dst[...] = dst[...] + src[...]


def add_three(out, a, b, d):
    if len(out.shape) == 3:
        for i in range(out.shape[0]):
            out[i] = a[i] + (b[i] + d[i])
    else:
        out[...] = (a[...].astype(F32) + b[...].astype(F32) + d[...].astype(F32)).astype(out.dtype)


class Steps:
    at = 0

    def next(self):
        self.steps[self.at]()
        self.at += 1


class PlaneSum(Steps):
    def __init__(self, place, first, g, glo, blo, slo, w, bufs, sems, n, sums):
        b1, r1, b2, r2, zb = bufs
        send, recv = sems
        gc, bc = pl.ds(glo, w), pl.ds(blo, w)
        self.place, self.r2, self.zb, self.bc, self.sc = place, r2, zb, bc, slice(slo, slo + w)
        self.send, self.recv, self.n, self.sums = send, recv, n, sums
        if first == "x":
            half1 = lambda d, h: g.at[h, d, :, :, gc]
        else:
            half1 = lambda d, h: g.at[h, :, d, :, gc]
        self.one = RingSum(
            place, first, half1, lambda k: b1.at[k, :, :, bc], lambda h: r1.at[h, :, :, bc],
            lambda k: send.at[n, k], lambda k: recv.at[n, k],
        )
        self.two = RingSum(
            place, "y" if first == "x" else "x", lambda d, h: r1.at[h, d, :, bc], lambda k: b2.at[k, :, bc],
            lambda h: r2.at[h, :, bc], lambda k: send.at[n, 6 + k], lambda k: recv.at[n, 6 + k],
        )
        self.steps = [self.one.start, self.one.mid, self.turn, self.two.mid, self.cross, self.total]

    def zcp(self):
        other = 1 - self.place.zl
        return remote(
            self.r2.at[other, :, self.bc], self.zb.at[:, self.bc], self.send.at[self.n, 12],
            self.recv.at[self.n, 12], self.place.at(zl=other),
        )

    def turn(self):
        self.one.fin()
        self.two.start()

    def cross(self):
        self.two.fin()
        self.zcp().start()

    def total(self):
        self.zcp().wait_recv()
        own = self.r2[self.place.zl, :, self.bc].astype(F32)
        self.sums[:, self.sc] = own + self.zb[:, self.bc].astype(F32)

    def end(self):
        self.one.end()
        self.two.end()
        self.zcp().wait_send()


class DepthSum(Steps):
    def __init__(self, place, first, g, glo, blo, slo, w, bufs, sems, n, sums):
        z0, b1, r1, b2 = bufs
        send, recv = sems
        h_w = w // 2
        self.place, self.g, self.z0 = place, g, z0
        self.gc, self.zc = pl.ds(glo, w), pl.ds(blo, w)
        self.send, self.recv, self.n = send, recv, n
        zl = place.zl
        part = lambda lo, h: pl.ds(lo + h * h_w, h_w)
        if first == "x":
            half1 = lambda d, h: g.at[zl, d, :, :, part(glo, h)]
        else:
            half1 = lambda d, h: g.at[zl, :, d, :, part(glo, h)]
        bc = pl.ds(blo // 2, h_w)
        self.one = RingSum(
            place, first, half1, lambda k: b1.at[k, :, :, bc], lambda h: r1.at[:, :, part(blo, h)],
            lambda k: send.at[n, k], lambda k: recv.at[n, k],
        )
        self.two = RingSum(
            place, "y" if first == "x" else "x", lambda d, h: r1.at[d, :, part(blo, h)], lambda k: b2.at[k, :, bc],
            lambda h: sums.at[:, part(slo, h)], lambda k: send.at[n, 6 + k], lambda k: recv.at[n, 6 + k],
        )
        self.steps = [self.cross, self.join, self.one.mid, self.turn, self.two.mid, self.two.fin]

    def zcp(self):
        other = 1 - self.place.zl
        return remote(
            self.g.at[other, :, :, :, self.gc], self.z0.at[:, :, :, self.zc], self.send.at[self.n, 12],
            self.recv.at[self.n, 12], self.place.at(zl=other),
        )

    def cross(self):
        self.zcp().start()

    def join(self):
        self.zcp().wait_recv()
        mine = self.g.at[self.place.zl, :, :, :, self.gc]
        came = self.z0.at[:, :, :, self.zc]

        def add(i, carry):
            for j in range(4):
                mine[i, j] = mine[i, j] + came[i, j]
            return carry

        lax.fori_loop(0, 4, add, 0)
        self.one.start()

    def turn(self):
        self.one.fin()
        self.two.start()

    def end(self):
        self.one.end()
        self.two.end()
        self.zcp().wait_send()


AR_PIECES = 2
AR_ROWS = ROWS // 2 // AR_PIECES


class TpSum:
    def __init__(self, place, part, buf, sems):
        self.place, self.part, self.buf = place, part, buf
        self.send, self.recv = sems
        self.core = place.at(c=1 - place.c)
        self.far = place.at(zh=1 - place.zh)

    def a(self, k):
        return remote(
            self.part.at[1 - self.place.c, k], self.buf.at[0, k], self.send.at[0, k], self.recv.at[0, k], self.core
        )

    def b(self, k):
        return remote(self.buf.at[0, k], self.buf.at[1, k], self.send.at[1, k], self.recv.at[1, k], self.far)

    def d(self, k):
        return remote(
            self.part.at[self.place.c, k], self.buf.at[2, k], self.send.at[2, k], self.recv.at[2, k], self.core
        )

    def start(self):
        for k in range(AR_PIECES):
            self.a(k).start()

    def mid(self):
        for k in range(AR_PIECES):
            self.a(k).wait_recv()
            self.buf[0, k] = self.buf[0, k] + self.part[self.place.c, k]
            self.b(k).start()

    def fin(self):
        for k in range(AR_PIECES):
            self.b(k).wait_recv()
            self.part[self.place.c, k] = self.buf[0, k] + self.buf[1, k]
            self.d(k).start()

    def landed(self):
        for k in range(AR_PIECES):
            self.a(k).wait_send()
            self.d(k).wait_recv()
            self.part[1 - self.place.c, k] = self.buf[2, k]

    def end(self):
        for k in range(AR_PIECES):
            self.b(k).wait_send()
            self.d(k).wait_send()


def tp_scratch():
    return [
        pltpu.VMEM((3, AR_PIECES, AR_ROWS, WIDTH), BF16),
        pltpu.SemaphoreType.DMA((3, AR_PIECES)),
        pltpu.SemaphoreType.DMA((3, AR_PIECES)),
    ]


def ar_view(value):
    return value.reshape(2, AR_PIECES, AR_ROWS, WIDTH)


def ar_load(ref):
    return ref[...].reshape(ROWS, WIDTH)


def norm_back(source, inverse, gain, grad):
    scaled = grad * gain
    gain_grad = jnp.sum(grad * source * inverse, 0, keepdims=True)
    mean = jnp.mean(scaled * source, -1, keepdims=True)
    return inverse * scaled - source * (inverse * inverse * inverse) * mean, gain_grad


W_FFN = 3 * FFL
W_MID = W_FFN + HEADS_LOCAL
W_TAIL = HEADS_LOCAL + 2 * PAIRS_LOCAL
W_ALL = W_MID + W_TAIL
FF_CHUNKS = 4
FF_CHUNK = FFL // FF_CHUNKS

PLAN = [
    ("down", "plane", "x", 2048, 256, 2048),
    ("down", "plane", "y", 2304, 256, 2304),
    ("down_z", "depth", "x", 2560, 256, 2560),
    ("down_z", "depth", "y", 2816, 256, 2816),
    ("gate", "plane", "x", 0, 256, 0),
    ("gate", "plane", "y", 256, 256, 256),
    ("gate_z", "depth", "x", 512, 256, 512),
    ("gate_z", "depth", "y", 768, 256, 768),
    ("up", "plane", "x", 1024, 384, 1024),
    ("up", "plane", "y", 1408, 384, 1408),
    ("up_z", "depth", "y", 1792, 256, 1792),
    ("out", "plane", "x", 3072, 128, 3072),
    ("out", "plane", "y", 3200, 256, 3200),
    ("query", "plane", "x", 3456, 256, 2048),
    ("query", "plane", "y", 3712, 128, 2304),
    ("pair", "plane", "x", 3840, 128, 0),
    ("pair", "plane", "y", 3968, 256, 128),
]
W_PLANE = sum(p[4] for p in PLAN if p[1] == "plane")
W_DEPTH = sum(p[4] for p in PLAN if p[1] == "depth")


def layer_kernel(
    lengths, freq, tokens, cot, gain1, gain2, wq, wkt, wvt, wo, wg, wu, wd,
    mixed_out, normed_out, wo_full, feed_out, tokens_grad, sums, gains,
    wo_buf, gu_buf, d_buf, mixed, back, normed, hidden, back_hidden, gate_grad, upper_grad, left, grads,
    b1, r1, b2, r2, zb, z0, b1z, r1z, b2z, gsend, grecv,
    part3, buf3, send3, recv3, buf2, send2, recv2, buf4, send4, recv4,
    kv, kb1, kr1, kb2, kr2, ksend, krecv,
    grp, qkv, att, o, lse, qaug, acc, peak, total, mine, dgrp, dout, dot_t, delta, dqkv, rows,
    gain_sum, gain_buf, gn_send, gn_recv,
    pair_send, pair_recv, ag_send, ag_recv, o_send, o_recv, w_send, w_recv, load_sem, ff_sem, wo_sem,
):
    place = Place()
    zl, x, y, zh, c = place.zl, place.x, place.y, place.zh, place.c
    partner = place.at(**place.pair)
    far_partner = place.at(**place.pair, zh=1 - zh)
    far = place.at(zh=1 - zh)
    core = place.at(c=1 - c)
    diagonal = place.at(zl=1 - zl, zh=1 - zh)
    xr, xl, yr, yl = place.along("x", 1), place.along("x", -1), place.along("y", 1), place.along("y", -1)
    peers = [partner, far_partner, far, core, diagonal, place.at(zl=1 - zl), xr, xl, yr, yl]
    peers += [place.along("x", 2), place.along("y", 2)]
    call(peers)
    me_t = zh * 2 + c
    there_t = (1 - zh) * 2 + c
    mine_t, other_t = zh * 2 + (1 - c), (1 - zh) * 2 + (1 - c)

    def projections():
        return [
            pltpu.make_async_copy(wq, gu_buf.at[0, :, pl.ds(0, HEADS_LOCAL)], ff_sem.at[0, 0]),
            pltpu.make_async_copy(wkt, d_buf.at[0, pl.ds(0, PAIRS_LOCAL)], ff_sem.at[0, 1]),
            pltpu.make_async_copy(wvt, d_buf.at[1, pl.ds(0, PAIRS_LOCAL)], ff_sem.at[0, 2]),
        ]

    def ff_loads(k):
        slot, cols = k % 2, pl.ds(k * FF_CHUNK, FF_CHUNK)
        return [
            pltpu.make_async_copy(wg.at[:, cols], gu_buf.at[slot, :, pl.ds(0, FF_CHUNK)], ff_sem.at[slot, 0]),
            pltpu.make_async_copy(wu.at[:, cols], gu_buf.at[slot, :, pl.ds(FF_CHUNK, FF_CHUNK)], ff_sem.at[slot, 1]),
        ]

    def down_load(k):
        rows_ = pl.ds(k * FF_CHUNK, FF_CHUNK)
        return pltpu.make_async_copy(wd.at[rows_], d_buf.at[k % 2], ff_sem.at[k % 2, 2])

    def hidden_back(k):
        down_load(k).wait()
        back_hidden[:, k * FF_CHUNK : (k + 1) * FF_CHUNK] = dot(cot[...], d_buf[k % 2], 1, 1).astype(BF16)
        down_load((k + 2) % 4).start()

    for cp in projections():
        cp.start()
    ends = ends_of(lengths)
    block = zl * 16 + x * 4 + y
    source = tokens[...].astype(F32)
    inverse = lax.rsqrt(jnp.mean(source * source, -1, keepdims=True) + EPS)
    normed[...] = (source * inverse * gain1[...].reshape(1, WIDTH)).astype(BF16)
    normed_save = pltpu.make_async_copy(normed, normed_out, load_sem.at[0])
    normed_save.start()
    cosine, sine = rotation(ends, lengths, block * ROWS, freq[...])

    def turned(u, factor):
        a, b = u[:HALF], u[HALF:]
        if factor is None:
            return a * cosine - b * sine, b * cosine + a * sine
        return (a * cosine - b * sine) * factor, (b * cosine + a * sine) * factor

    for cp in projections():
        cp.wait()
    kt = dot(d_buf[0, :PAIRS_LOCAL], normed[...], 1, 1)
    vt = dot(d_buf[1, :PAIRS_LOCAL], normed[...], 1, 1)
    qt = dot(normed[...], gu_buf[0, :, :HEADS_LOCAL]).T
    for g in range(2):
        for h in range(2):
            a, b = turned(qt[(2 * g + h) * HEAD : (2 * g + h + 1) * HEAD], SCALE * LOG2E)
            grp[g, h * HEAD : h * HEAD + HALF] = a.astype(BF16)
            grp[g, h * HEAD + HALF : (h + 1) * HEAD] = b.astype(BF16)
        a, b = turned(kt[g * HEAD : (g + 1) * HEAD], None)
        grp[g, 2 * HEAD : 2 * HEAD + HALF] = a.astype(BF16)
        grp[g, 2 * HEAD + HALF : 3 * HEAD] = b.astype(BF16)
        grp[g, 3 * HEAD :] = vt[g * HEAD : (g + 1) * HEAD].astype(BF16)
    qkv[zl] = grp[zl]
    kv[x, y, zl] = grp[zl, 2 * HEAD :]
    for k in range(2):
        down_load(k).start()
        for cp in ff_loads(k):
            cp.start()
    answer(peers)
    q_rows, k_rows = pl.ds(0, 2 * HEAD), pl.ds(2 * HEAD, 2 * HEAD)
    k_cp = remote(grp.at[1 - zl, k_rows], kv.at[3 - x, 3 - y, zl], pair_send.at[0], pair_recv.at[0], partner)
    q_cp = remote(grp.at[1 - zl, q_rows], qkv.at[zl, q_rows], pair_send.at[4], pair_recv.at[4], partner)
    k_cp.start()

    def gather(n, slot, swap):
        me1, me2 = (y, x) if swap else (x, y)
        r1, l1, r2, l2 = (yr, yl, xr, xl) if swap else (xr, xl, yr, yl)

        def ref(i, j, part=None):
            i, j = lax.rem(i + 4, 4), lax.rem(j + 4, 4)
            v = kv.at[j, i, slot] if swap else kv.at[i, j, slot]
            return v if part is None else v.at[pl.ds(part * HEAD, HEAD)]

        def cp(k, view, dev):
            return remote(view, view, ag_send.at[n, k], ag_recv.at[n, k], dev)

        def stage(base, i, j, di, dj, r, l):
            return dict(
                right=cp(base, ref(i, j), r),
                left=cp(base + 1, ref(i, j), l),
                from_left=cp(base, ref(i - di, j - dj), r),
                from_right=cp(base + 1, ref(i + di, j + dj), l),
                on_right=cp(base + 2, ref(i - di, j - dj, 0), r),
                on_left=cp(base + 3, ref(i + di, j + dj, 1), l),
                from_left2=cp(base + 2, ref(i + 2 * di, j + 2 * dj, 0), r),
                from_right2=cp(base + 3, ref(i + 2 * di, j + 2 * dj, 1), l),
            )

        s1 = stage(0, me1, me2, 1, 0, r1, l1)
        s2 = [stage(4 + 4 * k, me1 + k, me2, 0, 1, r2, l2) for k in range(4)]
        return s1, s2

    def begin(st):
        st["right"].start()
        st["left"].start()

    def hand_on(st):
        st["from_left"].wait_recv()
        st["on_right"].start()
        st["from_right"].wait_recv()
        st["on_left"].start()

    def complete(st):
        st["from_left2"].wait_recv()
        st["from_right2"].wait_recv()

    own, other = gather(0, zl, False), gather(1, 1 - zl, True)
    both = (own, other)
    begin(own[0])
    begin(own[1][0])
    q_cp.start()
    wo_cps = [
        remote(wo, wo_full.at[me_t], w_send.at[0], w_recv.at[0], diagonal),
        remote(wo, wo_full.at[me_t], w_send.at[1], w_recv.at[1], core),
    ]
    for cp in wo_cps:
        cp.start()
    k_there = kv.at[x, y, 1 - zl]
    remote(k_there, k_there, pair_send.at[0], pair_recv.at[0], partner).wait_recv()
    begin(other[0])
    begin(other[1][0])
    q_there = qkv.at[1 - zl, q_rows]
    remote(q_there, q_there, pair_send.at[4], pair_recv.at[4], partner).wait_recv()
    low = place.low_block(x, y)
    for s in range(2):
        base = jnp.where(s == 0, low, 31 - low) * ROWS
        segs = query_segments(ends, base)
        for h in range(2):
            qaug[s, :HEAD, h * ROWS : (h + 1) * ROWS] = qkv[s, h * HEAD : (h + 1) * HEAD]
            qaug[s, HEAD:, h * ROWS : (h + 1) * ROWS] = segs
    peak[...] = jnp.full(peak.shape, -BIG, F32)
    total[...] = jnp.zeros(total.shape, F32)
    acc[...] = jnp.zeros(acc.shape, F32)

    def attend(qs, kx, ky, ks, kbase, causal):
        pair = kv[kx, ky, ks]
        ka = jnp.concatenate([pair[:HEAD], key_segments(ends, kbase)], 0)
        s = dot(ka, qaug[qs], 0, 0)
        if causal:
            key = lax.broadcasted_iota(jnp.int32, (ROWS, 2 * ROWS), 0)
            query = lax.broadcasted_iota(jnp.int32, (ROWS, 2 * ROWS), 1)
            s = jnp.where(key <= jnp.where(query >= ROWS, query - ROWS, query), s, -BIG)
        old = peak[qs]
        new = jnp.maximum(old, jnp.max(s, 0, keepdims=True))
        p = jnp.exp2(s - new)
        fade = jnp.exp2(old - new)
        peak[qs] = new
        total[qs] = total[qs] * fade + jnp.sum(p, 0, keepdims=True)
        acc[qs] = acc[qs] * fade + dot(pair[HEAD:], p.astype(BF16))

    def shard(dx, dy):
        kx, ky = lax.rem(x + dx, 4), lax.rem(y + dy, 4)
        there = place.low_block(kx, ky)
        attend(1, kx, ky, 0, there * ROWS, False)
        sel = jnp.where(there < low, 0, 1)
        attend(sel, kx, ky, sel, jnp.where(there < low, there, 31 - there) * ROWS, False)

    def shards(count, offsets):
        def step(i, carry):
            shard(*offsets(i))
            return carry

        lax.fori_loop(0, count, step, 0)

    attend(0, x, y, 0, low * ROWS, True)
    attend(1, x, y, 1, (31 - low) * ROWS, True)
    attend(1, x, y, 0, low * ROWS, False)
    for s1, s2 in both:
        hand_on(s1)
        begin(s2[3])
        begin(s2[1])
    for s1, s2 in both:
        hand_on(s2[0])
    hidden_back(0)
    shards(4, lambda i: ((1 - i // 2) * (2 * i + 1), (i // 2) * (2 * i - 3)))
    for s1, s2 in both:
        complete(s1)
        begin(s2[2])
    hidden_back(1)
    for s1, s2 in both:
        hand_on(s2[3])
        hand_on(s2[1])
    shards(4, lambda i: (2 * (i // 2) + 1, 2 * lax.rem(i, 2) + 1))
    hidden_back(2)
    for s1, s2 in both:
        complete(s2[0])
        hand_on(s2[2])
    shards(2, lambda i: (2 * i, 2 - 2 * i))
    hidden_back(3)
    for s1, s2 in both:
        complete(s2[3])
        complete(s2[1])
    shards(4, lambda i: ((1 - i // 2) * (2 * i + 1) + 2 * (i // 2), (i // 2) * (2 * i - 3) + 2 * (1 - i // 2)))
    for s1, s2 in both:
        complete(s2[2])
    shard(2, 2)
    for s in range(2):
        out = acc[s] / total[s]
        lse[s] = peak[s] + jnp.log2(total[s])
        for h in range(2):
            part = out[:, h * ROWS : (h + 1) * ROWS]
            o[s, h * HEAD : (h + 1) * HEAD] = part
            mine[s, h * HEAD : (h + 1) * HEAD] = part.astype(BF16)

    for s1, s2 in both:
        for st in [s1, *s2]:
            for name in ("right", "left", "on_right", "on_left"):
                st[name].wait_send()
    k_cp.wait_send()
    q_cp.wait_send()

    group = me_t * 2 + zl
    att[group] = mine[zl]
    sends = [
        remote(mine.at[1 - zl], att.at[group], o_send.at[0], o_recv.at[0], partner),
        remote(mine.at[1 - zl], att.at[group], o_send.at[1], o_recv.at[1], far_partner),
        remote(mine.at[zl], att.at[group], o_send.at[2], o_recv.at[2], far),
    ]
    for cp in sends:
        cp.start()
    wo_far = wo_full.at[there_t]
    remote(wo_far, wo_far, w_send.at[0], w_recv.at[0], far).wait_recv()
    wo_relay = remote(wo_far, wo_far, w_send.at[2], w_recv.at[2], core)
    wo_relay.start()
    def load_wo(src, slot):
        pltpu.make_async_copy(src, wo_buf.at[slot], wo_sem.at[slot]).start()

    def wo_ready(slot):
        pltpu.make_async_copy(wo, wo_buf.at[slot], wo_sem.at[slot]).wait()

    def arrived(which, n):
        remote(att.at[which], att.at[which], o_send.at[n], o_recv.at[n], far).wait_recv()

    def relay(which, n):
        cp = remote(att.at[which], att.at[which], o_send.at[n], o_recv.at[n], core)
        cp.start()
        return cp

    def heads_of(t):
        return att[pl.ds(t * 2, 2)].reshape(HEADS_LOCAL, ROWS)

    w1, w2 = wo_full.at[mine_t], wo_full.at[other_t]
    load_wo(wo, 0)
    relays = [relay(group, 3)]
    left[...] = cot[...].T
    remote(w1, w1, w_send.at[1], w_recv.at[1], core).wait_recv()
    load_wo(w1, 1)
    arrived(me_t * 2 + 1 - zl, 0)
    relays.append(relay(me_t * 2 + 1 - zl, 4))
    wo_ready(0)
    mixed[...] = dot(heads_of(me_t), wo_buf[0], 0, 0)
    load_wo(wo_far, 0)
    arrived(mine_t * 2 + zl, 3)
    arrived(mine_t * 2 + 1 - zl, 4)
    arrived(there_t * 2 + zl, 2)
    relays.append(relay(there_t * 2 + zl, 5))
    arrived(there_t * 2 + 1 - zl, 1)
    relays.append(relay(there_t * 2 + 1 - zl, 6))
    wo_ready(1)
    mixed[...] = mixed[...] + dot(heads_of(mine_t), wo_buf[1], 0, 0)
    remote(w2, w2, w_send.at[2], w_recv.at[2], core).wait_recv()
    load_wo(w2, 1)
    wo_ready(0)
    back[...] = dot(heads_of(there_t), wo_buf[0], 0, 0)
    load_wo(wo, 0)
    arrived(other_t * 2 + zl, 5)
    arrived(other_t * 2 + 1 - zl, 6)
    wo_ready(1)
    back[...] = back[...] + dot(heads_of(other_t), wo_buf[1], 0, 0)
    mixed[...] = tokens[...].astype(F32) + (mixed[...] + back[...])
    normed_save.wait()
    gain = gain2[...].reshape(1, WIDTH)
    inverse_two = lax.rsqrt(jnp.mean(mixed[...] * mixed[...], -1, keepdims=True) + EPS)
    normed[...] = (mixed[...] * inverse_two * gain).astype(BF16)
    mixed_save = pltpu.make_async_copy(mixed, mixed_out, load_sem.at[1])
    mixed_save.start()

    for k in range(FF_CHUNKS):
        slot, cols = k % 2, slice(k * FF_CHUNK, (k + 1) * FF_CHUNK)
        for cp in ff_loads(k):
            cp.wait()
        both_ff = dot(normed[...], gu_buf[slot])
        gate, upper = both_ff[:, :FF_CHUNK], both_ff[:, FF_CHUNK:]
        hidden_grad = back_hidden[:, cols].astype(F32)
        sig = jax.nn.sigmoid(gate)
        silu = gate * sig
        hid = (silu * upper).astype(BF16)
        gg = (hidden_grad * upper * sig * (1.0 + gate * (1.0 - sig))).astype(BF16)
        ug = (hidden_grad * silu).astype(BF16)
        hidden[:, cols], gate_grad[:, cols], upper_grad[:, cols] = hid, gg, ug
        add_back = dot(jnp.concatenate([gg, ug], 1), gu_buf[slot], 1, 1)
        if k == 0:
            back[...] = add_back
        else:
            back[...] = back[...] + add_back
        if k + 2 < FF_CHUNKS:
            for cp in ff_loads(k + 2):
                cp.start()
    part3[...] = ar_view(back[...].astype(BF16))
    sum3 = TpSum(place, part3, buf3, (send3, recv3))
    sum3.start()
    def weight_grad(rhs, lo, cb=0):
        w = rhs.shape[1 - cb]

        def slab(i, carry):
            piece = dot(left[pl.ds(pl.multiple_of(i * 192, 192), 192)], rhs[...], 1, cb)
            grads[i // 4, i % 4, :, :, lo : lo + w] = piece.astype(BF16).reshape(4, 48, w)
            return carry

        lax.fori_loop(0, 8, slab, 0)

    groups, blo = {}, dict(plane=0, depth=0)
    for n, (name, kind, first, slo, w, glo) in enumerate(PLAN):
        if kind == "plane":
            piece = PlaneSum(place, first, grads, glo, blo[kind], slo, w, (b1, r1, b2, r2, zb), (gsend, grecv), n, sums)
        else:
            piece = DepthSum(place, first, grads, glo, blo[kind], slo, w, (z0, b1z, r1z, b2z), (gsend, grecv), n, sums)
        blo[kind] += w
        groups.setdefault(name, []).append(piece)
    pieces = [p for group_ in groups.values() for p in group_]

    def go(*names):
        for name in names:
            for piece in groups[name]:
                piece.next()

    weight_grad(hidden, 2 * FFL)
    go("down")
    sum3.mid()
    left[...] = normed[...].T
    weight_grad(gate_grad, 0)
    go("gate")
    weight_grad(upper_grad, FFL)
    go("up")
    mixed_save.wait()
    for k in range(FF_CHUNKS):
        down_load(k).wait()
        add_feed = dot(hidden[:, k * FF_CHUNK : (k + 1) * FF_CHUNK], d_buf[k % 2])
        mixed[...] = add_feed if k == 0 else mixed[...] + add_feed
        if k < 2:
            down_load(k + 2).start()
    feed_out[...] = ar_view(mixed[...].astype(BF16))
    mixed_load = pltpu.make_async_copy(mixed_out, mixed, load_sem.at[1])
    mixed_load.start()
    sum2 = TpSum(place, feed_out, buf2, (send2, recv2))
    sum2.start()
    for s in range(2):
        for h in range(2):
            dot_t[s, :, h * ROWS : (h + 1) * ROWS] = jnp.zeros((HEAD, ROWS), BF16)
    acc[...] = jnp.zeros(acc.shape, F32)
    dq = acc
    mixed_load.wait()
    go("down")
    sum3.fin()
    go("down_z", "gate_z", "up_z")
    sum3.landed()
    mixed_part, ffn_gain_grad = norm_back(mixed[...], inverse_two, gain, ar_load(part3).astype(F32))
    gain_sum[0, 1:2] = ffn_gain_grad
    back[...] = cot[...].astype(F32) + mixed_part
    normed[...] = back[...].astype(BF16)
    wo_ready(0)
    own_grad = dot(wo_buf[0], normed[...], 1, 1).astype(BF16)
    dgrp[0] = own_grad[: 2 * HEAD]
    dgrp[1] = own_grad[2 * HEAD :]
    grad_cp = remote(dgrp.at[1 - zl], dout.at[zl], pair_send.at[1], pair_recv.at[1], partner)
    grad_cp.start()
    dout[zl] = dgrp[zl]
    left[...] = normed[...].T
    weight_grad(heads_of(me_t), W_FFN, 1)
    go("out")
    normed_load = pltpu.make_async_copy(normed_out, normed, load_sem.at[0])
    normed_load.start()
    for cp in projections():
        cp.start()
    go("gate")
    grad_cp.wait_recv()
    for s in range(2):
        for h in range(2):
            lanes, feats = slice(h * ROWS, (h + 1) * ROWS), slice(h * HEAD, (h + 1) * HEAD)
            d = dout[s, feats]
            dot_t[s, :, lanes] = d
            delta[s, :, lanes] = jnp.sum(d.astype(F32) * o[s, feats], 0, keepdims=True)

    def attend_back(qs, kx, ky, ks, kbase, causal):
        pair = kv[kx, ky, ks]
        q = qaug[qs]
        do = dot_t[qs]
        ka = jnp.concatenate([pair[:HEAD], key_segments(ends, kbase)], 0)
        s = dot(ka, q, 0, 0)
        p = jnp.exp2(s - lse[qs])
        if causal:
            key = lax.broadcasted_iota(jnp.int32, (ROWS, 2 * ROWS), 0)
            query = lax.broadcasted_iota(jnp.int32, (ROWS, 2 * ROWS), 1)
            p = jnp.where(key <= jnp.where(query >= ROWS, query - ROWS, query), p, 0.0)
        dp = dot(pair[HEAD:], do, 0, 0)
        ds = (p * (dp - delta[qs])).astype(BF16)
        dq[qs] = dq[qs] + dot(pair[:HEAD], ds)
        dk = dot(q[:HEAD], ds, 1, 1)
        dv = dot(do, p.astype(BF16), 1, 1)
        return jnp.concatenate([dk, dv], 0)

    def shard_back(dx, dy):
        kx, ky = lax.rem(x + dx, 4), lax.rem(y + dy, 4)
        there = place.low_block(kx, ky)
        one = attend_back(1, kx, ky, 0, there * ROWS, False)
        before = there < low
        sel = jnp.where(before, 0, 1)
        two = attend_back(sel, kx, ky, sel, jnp.where(before, there, 31 - there) * ROWS, False)
        share = jnp.where(before, 1.0, 0.0)
        kv[kx, ky, 0] = (one + two * share).astype(BF16)
        kv[kx, ky, 1] = (two * (1.0 - share)).astype(BF16)

    def shards_back(count, offsets, events):
        def step(i, carry):
            shard_back(*offsets(i))
            for at, event in events:
                pl.when(i == at)(event)
            return carry

        lax.fori_loop(0, count, step, 0)

    def key_sum(slot, axis):
        other_axis = "y" if axis == "x" else "x"
        if axis == "x":
            half = lambda d, h: kv.at[d, :, slot, pl.ds(h * HEAD, HEAD)]
        else:
            half = lambda d, h: kv.at[:, d, slot, pl.ds(h * HEAD, HEAD)]
        one = RingSum(
            place, axis, half, lambda k: kb1.at[slot, k], lambda h: kr1.at[slot, h],
            lambda k: ksend.at[slot, k], lambda k: krecv.at[slot, k],
        )
        two = RingSum(
            place, other_axis, lambda d, h: kr1.at[slot, h, d], lambda k: kb2.at[slot, k],
            lambda h: kr2.at[slot, h], lambda k: ksend.at[slot, 6 + k], lambda k: krecv.at[slot, 6 + k],
        )
        return one, two

    ka, kb = key_sum(0, "x"), key_sum(1, "y")

    def two_away(i):
        k, j = i // 4, i - 4
        return (1 - k) * 2 + k * (j + j // 2), (1 - k) * i + k * 2

    def one_away(i):
        k, j = i // 4, i - 4
        along_x = (1 - j // 2) * (2 * j + 1)
        along_y = (j // 2) * (2 * j - 3)
        dx = (1 - k) * (2 * (i // 2) + 1) + k * along_x
        dy = (1 - k) * (2 * lax.rem(i, 2) + 1) + k * along_y
        return dx, dy

    shards_back(7, two_away, [(0, lambda: go("up", "out")), (3, lambda: go("down")), (6, lambda: go("gate"))])
    ka[0].start_far()
    kb[0].start_far()

    def near(part):
        part.start_near()
        part.mid()

    shards_back(
        8,
        one_away,
        [
            (1, lambda: go("up", "out")),
            (3, lambda: go("down", "down_z")),
            (5, lambda: near(ka[0])),
            (6, lambda: go("gate")),
        ],
    )
    near(kb[0])
    first = attend_back(0, x, y, 0, low * ROWS, True) + attend_back(1, x, y, 0, low * ROWS, False)
    kv[x, y, 0] = first.astype(BF16)
    kv[x, y, 1] = attend_back(1, x, y, 1, (31 - low) * ROWS, True).astype(BF16)

    for s in range(2):
        for h in range(2):
            grp[s, h * HEAD : (h + 1) * HEAD] = (dq[s, :, h * ROWS : (h + 1) * ROWS] * SCALE).astype(BF16)
    dq_cp = remote(grp.at[1 - zl, q_rows], dqkv.at[zl, q_rows], pair_send.at[2], pair_recv.at[2], partner)
    dq_cp.start()
    dqkv[zl, : 2 * HEAD] = grp[zl, : 2 * HEAD]
    go("up", "out", "down", "gate")

    ka[0].fin()
    kb[0].fin()
    ka[1].start()
    kb[1].start()
    go("gate_z", "down_z")
    sum2.mid()

    def unturned(g, h, at):
        a = dqkv[g, h * HEAD : h * HEAD + HALF].astype(F32)
        b = dqkv[g, h * HEAD + HALF : (h + 1) * HEAD].astype(F32)
        if h == 2:
            a, b = a * LN2, b * LN2
        rows[at : at + HALF] = (a * cosine + b * sine).astype(BF16)
        rows[at + HALF : at + HEAD] = (b * cosine - a * sine).astype(BF16)

    dq_there = dqkv.at[1 - zl, q_rows]
    remote(dq_there, dq_there, pair_send.at[2], pair_recv.at[2], partner).wait_recv()
    for g in range(2):
        for h in range(2):
            unturned(g, h, (2 * g + h) * HEAD)
    normed_load.wait()
    for piece in groups["down"]:
        piece.one.end()
    left[...] = normed[...].T
    weight_grad(rows.at[pl.ds(0, HEADS_LOCAL)], 2 * FFL, 1)
    ka[1].mid()
    kb[1].mid()
    go("query")
    for cp in projections():
        cp.wait()
    mixed[...] = dot(rows[:HEADS_LOCAL], gu_buf[0, :, :HEADS_LOCAL], 0, 1)
    go("down_z", "gate_z", "up", "out", "up_z")
    ka[1].fin()
    kb[1].fin()
    for s in range(2):
        for h in range(2):
            grp[s, (2 + h) * HEAD : (3 + h) * HEAD] = kr2[s, h]
    dk_cp = remote(grp.at[1 - zl, k_rows], dqkv.at[zl, k_rows], pair_send.at[3], pair_recv.at[3], partner)
    dk_cp.start()
    dqkv[zl, 2 * HEAD :] = grp[zl, 2 * HEAD :]
    go("down", "gate", "down_z", "gate_z", "query", "up_z", "up", "out")
    for piece in groups["gate"]:
        piece.one.end()
    sum2.fin()
    sum3.end()
    dk_there = dqkv.at[1 - zl, k_rows]
    remote(dk_there, dk_there, pair_send.at[3], pair_recv.at[3], partner).wait_recv()
    for g in range(2):
        unturned(g, 2, HEADS_LOCAL + g * HEAD)
        at = HEADS_LOCAL + PAIRS_LOCAL + g * HEAD
        rows[at : at + HEAD] = dqkv[g, 3 * HEAD :]
    weight_grad(rows.at[pl.ds(HEADS_LOCAL, 2 * PAIRS_LOCAL)], 0, 1)
    go("pair")
    grad_in = mixed[...] + dot(rows[HEADS_LOCAL : HEADS_LOCAL + PAIRS_LOCAL], d_buf[0, :PAIRS_LOCAL], 0, 0)
    grad_in = grad_in + dot(rows[HEADS_LOCAL + PAIRS_LOCAL :], d_buf[1, :PAIRS_LOCAL], 0, 0)
    part3[...] = ar_view(grad_in.astype(BF16))
    sum4 = TpSum(place, part3, buf4, (send4, recv4))
    sum4.start()
    source = tokens[...].astype(F32)
    gain_sum[0, 0:1] = jnp.sum(grad_in * source * inverse, 0, keepdims=True)
    gain_sum[0, 1:2] = 0.25 * gain_sum[0, 1:2]
    gain_sent = []

    def gain_step(stage):
        if stage:
            came = gain_sum[stage - 1]
            for k, cp in enumerate(gain_sent[-1]):
                cp.wait_recv()
                came = came + gain_buf[stage - 1, k]
            gain_sum[stage] = came
        if stage < 5:
            there = [
                [place.along("x", k) for k in (1, 2, 3)], [place.along("y", k) for k in (1, 2, 3)],
                [place.at(zl=1 - zl)], [far], [core],
            ][stage]
            gain_sent.append(
                [
                    remote(gain_sum.at[stage], gain_buf.at[stage, k], gn_send.at[stage, k], gn_recv.at[stage, k], peer)
                    for k, peer in enumerate(there)
                ]
            )
            for cp in gain_sent[-1]:
                cp.start()

    gain_step(0)
    go("down_z", "gate_z")
    sum4.mid()
    gain_step(1)
    go("query", "up_z", "pair")
    gain_step(2)
    go("gate_z", "query", "up_z")
    gain_step(3)
    go("pair")
    sum4.fin()
    gain_step(4)
    go("up_z", "query", "pair")
    sum4.landed()
    source_part, _ = norm_back(tokens[...].astype(F32), inverse, gain1[...].reshape(1, WIDTH), ar_load(part3).astype(F32))
    tokens_grad[...] = (back[...] + source_part).astype(BF16)
    gain_step(5)
    gains[...] = gain_sum[5]
    go("pair", "query", "pair")
    sum2.landed()
    for cp in [grad_cp, dq_cp, dk_cp, *wo_cps, wo_relay, *sends, *relays, *sum(gain_sent, [])]:
        cp.wait_send()
    sum2.end()
    sum4.end()
    for piece in pieces:
        assert piece.at == len(piece.steps)
        piece.end()
    for one, two in (ka, kb):
        one.end()
        two.end()


def layer(lengths, freq, tokens, cot, gain1, gain2, wq, wkt, wvt, wo, wg, wu, wd):
    vm = pl.BlockSpec(memory_space=pltpu.VMEM)
    hbm = pl.BlockSpec(memory_space=pl.ANY)
    dma = pltpu.SemaphoreType.DMA
    shape = (2, AR_PIECES, AR_ROWS, WIDTH)
    group = pltpu.VMEM((2, 4 * HEAD, ROWS), BF16)
    two_heads = pltpu.VMEM((2, 2 * HEAD, ROWS), BF16)
    line = pltpu.VMEM((2, 1, 2 * ROWS), F32)
    return pl.pallas_call(
        layer_kernel,
        out_shape=(
            jax.ShapeDtypeStruct((ROWS, WIDTH), F32),
            jax.ShapeDtypeStruct((ROWS, WIDTH), BF16),
            jax.ShapeDtypeStruct((4, HEADS_LOCAL, WIDTH), BF16),
            jax.ShapeDtypeStruct(shape, BF16),
            jax.ShapeDtypeStruct((ROWS, WIDTH), BF16),
            jax.ShapeDtypeStruct((48, W_ALL), F32),
            jax.ShapeDtypeStruct((2, WIDTH), F32),
        ),
        in_specs=[pl.BlockSpec(memory_space=pltpu.SMEM)] + [vm] * 5 + [hbm] * 7,
        out_specs=(hbm, hbm, hbm, vm, vm, vm, vm),
        scratch_shapes=[
            pltpu.VMEM((2, HEADS_LOCAL, WIDTH), BF16),
            pltpu.VMEM((2, WIDTH, 2 * FF_CHUNK), BF16),
            pltpu.VMEM((2, FF_CHUNK, WIDTH), BF16),
            pltpu.VMEM((ROWS, WIDTH), F32),
            pltpu.VMEM((ROWS, WIDTH), F32),
            pltpu.VMEM((ROWS, WIDTH), BF16),
            pltpu.VMEM((ROWS, FFL), BF16),
            pltpu.VMEM((ROWS, FFL), BF16),
            pltpu.VMEM((ROWS, FFL), BF16),
            pltpu.VMEM((ROWS, FFL), BF16),
            pltpu.VMEM((WIDTH, ROWS), BF16),
            pltpu.VMEM((2, 4, 4, 48, W_MID), BF16),
            pltpu.VMEM((6, 4, 48, W_PLANE), BF16),
            pltpu.VMEM((2, 4, 48, W_PLANE), BF16),
            pltpu.VMEM((6, 48, W_PLANE), BF16),
            pltpu.VMEM((2, 48, W_PLANE), BF16),
            pltpu.VMEM((48, W_PLANE), BF16),
            pltpu.VMEM((4, 4, 48, W_DEPTH), BF16),
            pltpu.VMEM((6, 4, 48, W_DEPTH // 2), BF16),
            pltpu.VMEM((4, 48, W_DEPTH), BF16),
            pltpu.VMEM((6, 48, W_DEPTH // 2), BF16),
            dma((len(PLAN), 13)),
            dma((len(PLAN), 13)),
            pltpu.VMEM(shape, BF16),
            *tp_scratch(),
            *tp_scratch(),
            *tp_scratch(),
            pltpu.VMEM((4, 4, 2, 2 * HEAD, ROWS), BF16),
            pltpu.VMEM((2, 6, 4, HEAD, ROWS), BF16),
            pltpu.VMEM((2, 2, 4, HEAD, ROWS), BF16),
            pltpu.VMEM((2, 6, HEAD, ROWS), BF16),
            pltpu.VMEM((2, 2, HEAD, ROWS), BF16),
            dma((2, 12)),
            dma((2, 12)),
            group,
            group,
            pltpu.VMEM((8, 2 * HEAD, ROWS), BF16),
            pltpu.VMEM((2, 2 * HEAD, ROWS), F32),
            line,
            pltpu.VMEM((2, HEAD + SEG, 2 * ROWS), BF16),
            pltpu.VMEM((2, HEAD, 2 * ROWS), F32),
            line,
            line,
            two_heads,
            two_heads,
            two_heads,
            pltpu.VMEM((2, HEAD, 2 * ROWS), BF16),
            line,
            group,
            pltpu.VMEM((W_TAIL, ROWS), BF16),
            pltpu.VMEM((6, 2, WIDTH), F32),
            pltpu.VMEM((5, 3, 2, WIDTH), F32),
            dma((5, 3)),
            dma((5, 3)),
            dma((5,)),
            dma((5,)),
            dma((2, 20)),
            dma((2, 20)),
            dma((7,)),
            dma((7,)),
            dma((3,)),
            dma((3,)),
            dma((2,)),
            dma((2, 3)),
            dma((2,)),
        ],
        compiler_params=pltpu.CompilerParams(
            collective_id=0, has_side_effects=True, vmem_limit_bytes=VMEM_LIMIT
        ),
        name="layer",
    )(lengths, freq, tokens, cot, gain1, gain2, wq, wkt, wvt, wo, wg, wu, wd)


def finish_kernel(
    mixed, feed, tokens_grad, sums, gains,
    result, tokens_grad_out, norm_gain, query, key, value, out, ffn_gain, gate, up, down,
):
    result[...] = (mixed[...] + ar_load(feed).astype(F32)).astype(BF16)
    tokens_grad_out[...] = tokens_grad[...]
    block = (lax.axis_index("zl") * 4 + lax.axis_index("x")) * 4 + lax.axis_index("y")
    own = jnp.zeros((2, 48), F32)
    for b in range(32):
        own = own + jnp.where(block == b, gains[:, 48 * b : 48 * b + 48], 0.0)
    norm_gain[...] = own[0:1]
    ffn_gain[...] = own[1:2]
    gate[...] = sums[:, :FFL]
    up[...] = sums[:, FFL : 2 * FFL]
    down[...] = sums[:, 2 * FFL : W_FFN]
    out[...] = sums[:, W_FFN:W_MID]
    query[...] = sums[:, W_MID : W_MID + HEADS_LOCAL]
    key[...] = sums[:, W_MID + HEADS_LOCAL : W_MID + HEADS_LOCAL + PAIRS_LOCAL]
    value[...] = sums[:, W_MID + HEADS_LOCAL + PAIRS_LOCAL :]


def finish(mixed, feed, tokens_grad, sums, gains):
    vm = pl.BlockSpec(memory_space=pltpu.VMEM)
    shapes = [(ROWS, WIDTH)] * 2 + [
        (1, 48), (48, HEADS_LOCAL), (48, PAIRS_LOCAL), (48, PAIRS_LOCAL), (48, HEADS_LOCAL), (1, 48),
        (48, FFL), (48, FFL), (48, FFL),
    ]
    return pl.pallas_call(
        finish_kernel,
        out_shape=[jax.ShapeDtypeStruct(s, BF16 if n < 2 else F32) for n, s in enumerate(shapes)],
        in_specs=[vm] * 5,
        out_specs=[vm] * len(shapes),
        compiler_params=pltpu.CompilerParams(vmem_limit_bytes=VMEM_LIMIT),
        name="finish",
    )(mixed, feed, tokens_grad, sums, gains)


def local(
    tokens, norm_gain, query_weight, key_matrix, value_matrix, out_weight,
    ffn_gain, gate_weight, up_weight, down_weight, cotangent, lengths,
):
    freq = jnp.asarray(
        (THETA ** (-2.0 * np.arange(HALF) / HEAD)).astype(np.float32).reshape(HALF, 1)
    )
    mixed, _, _, feed, tokens_grad, sums, gains = layer(
        lengths, freq, tokens, cotangent, norm_gain, ffn_gain, query_weight, key_matrix.T, value_matrix.T,
        out_weight, gate_weight, up_weight, down_weight,
    )
    result, tokens_grad, norm_gain_grad, query, key, value, out, ffn_gain_grad, gate, up, down = finish(
        mixed, feed, tokens_grad, sums, gains
    )
    return (
        result, tokens_grad, norm_gain_grad.reshape(48), query, key, value, out.T,
        ffn_gain_grad.reshape(48), gate, up, down.T,
    )


def solution(mesh):
    split = Mesh(mesh.devices.reshape(2, 4, 4, 2, 2), AXES)
    in_specs = (
        P(BLK, None),
        P(),
        P(None, TP),
        P(None, TP),
        P(None, TP),
        P(TP, None),
        P(),
        P(None, TP),
        P(None, TP),
        P(TP, None),
        P(BLK, None),
        P(),
    )
    out_specs = (
        P(BLK, None),
        P(BLK, None),
        P(BLK),
        P(BLK, TP),
        P(BLK, TP),
        P(BLK, TP),
        P(TP, BLK),
        P(BLK),
        P(BLK, TP),
        P(BLK, TP),
        P(TP, BLK),
    )
    return jax.shard_map(local, mesh=split, in_specs=in_specs, out_specs=out_specs, check_vma=False)
```
